128 devices in a mesh: mem: 4 (over y_lo, core), tile: 32 (over x, z, y_hi).
Axes of the slice: x: 4, y: 4 (y_hi: 2, y_lo: 2; y = y_hi * 2 + y_lo), z: 4, core: 2. Of those that a mesh axis runs over, the one named last changes fastest.
Arguments:
- member_collection: bfloat16 [256, 8, 256, 128], P('mem', None, 'tile'), may hold values from -6 to 6
- spreading_ratio: float32 [8, 256, 128], P(None, 'tile'), may hold values from 0.005 to 0.07
- transport_ratio_row: float32 [8], replicated, may hold values from 0.1 to 0.35
- transport_ratio_column: float32 [8], replicated, may hold values from 0.1 to 0.35
- obs_patch: int32 [32768], P(('mem', 'tile')), may hold values from 0 to 512, as said below
Outputs:
- forecast: bfloat16 [256, 8, 256, 128], P('mem', None, 'tile')
The draws below stay inside these ranges and needn't reach their ends.
Inputs may be any that keep to these rules, and one draw needn't show every extreme that they name: `obs_patch`: a value of 512 marks an empty slot that no patch counts.
All inputs are finite; a program needn't handle non-finite values.
Results may differ from the reference program's by a relative error of at most 0.001.
The reference program's roundings to bfloat16 on the way count: a program that leaves them out, or rounds other values in their place, can miss the bound.
Values may be sent and summed in bfloat16 or wider, within the bound.
A program may use at most 64 MiB of HBM per device.

```python
import math
import jax
import jax.numpy as jnp
from jax import lax

MEMBERS = 256
FL = 8
PX = 8
PY = 8
NY = 128
EARLIER_INCREMENTS = 2
LATER_INCREMENTS = 1
NS_ITERS = 14
OBS_DEV = 256
NX = 256
NPY = 16
PATCHES = 512
PATCH = 512
NOBS = 32768
OBS_HALF = 16


def draw_obs_patch(key, part):
    key_patch = jax.random.fold_in(key, 11)
    key_keep = jax.random.fold_in(key, 23)
    device_total = NOBS // OBS_DEV
    owner = jnp.arange(NOBS, dtype=jnp.int32) // OBS_DEV
    patch_ids = jax.random.randint(key_patch, (NOBS,), 0, PATCHES, dtype=jnp.int32)
    ticket = jax.random.randint(key_keep, (NOBS,), 0, 4 * device_total, dtype=jnp.int32)
    keep = ticket < device_total + 3 * owner
    return jnp.where(keep, patch_ids, PATCHES).astype(jnp.int32)


def block_levels(rng, shape, shards, least, largest):
    gain, own = 1.0, jax.random.fold_in(rng, 6)
    for axis_at, parts in shards:
        heights = jnp.exp(jax.random.uniform(jax.random.fold_in(own, axis_at), (parts,), jnp.float32, least / len(shards), largest / len(shards)))
        gain = gain * jnp.repeat(heights, shape[axis_at] // parts).reshape([-1 if axis == axis_at else 1 for axis in range(len(shape))])
    return gain


def normal_values(key, shape, deviation, most, shards=(), held_as=jnp.bfloat16):
    entries = deviation * jax.random.normal(key, shape, jnp.float32)
    if shards:
        entries = entries * block_levels(key, shape, shards, -0.22, 0.18)
    return jnp.clip(entries, -most, most).astype(held_as)


def setup_inputs(seed: int = 0) -> dict:
    keys = jax.random.split(jax.random.key(seed), 6)
    return {
        "member_collection": normal_values(keys[0], (MEMBERS, FL, NX, NY), 1.0, 6.0, ((0, 4), (2, 32))),
        "spreading_ratio": jnp.clip(jnp.exp(math.log(0.07) - 2.6390574 * jax.random.uniform(keys[1], (FL, NX, NY), jnp.float32) ** block_levels(keys[1], (FL, NX, NY), ((1, 32),), -0.2, 0.2)), 0.005, 0.07),
        "transport_ratio_row": jnp.clip(jax.random.uniform(keys[2], (FL,), jnp.float32, 0.1, 0.35), 0.1, 0.35),
        "transport_ratio_column": jnp.clip(jax.random.uniform(keys[3], (FL,), jnp.float32, 0.1, 0.35), 0.1, 0.35),
        "obs_patch": draw_obs_patch(jax.random.fold_in(keys[5], 71), 0),
    }


def advance_member(member, spreading_ratio, transport_ratio_row, transport_ratio_column):
    values = member.astype(jnp.float32)
    behind_x = jnp.roll(values, 1, 1)
    ahead_x = jnp.roll(values, -1, 1)
    behind_y = jnp.roll(values, 1, 2)
    ahead_y = jnp.roll(values, -1, 2)
    speed_x = transport_ratio_row[:, None, None]
    speed_y = transport_ratio_column[:, None, None]
    result = values - speed_x * (values - behind_x) - speed_y * (values - behind_y) + spreading_ratio * (ahead_x + behind_x + ahead_y + behind_y - 4.0 * values)
    return result.astype(jnp.bfloat16)

def march_prediction(member_collection, spreading_ratio, transport_ratio_row, transport_ratio_column, increment_total):

    def single(member):
        for repeat in range(increment_total):
            member = advance_member(member, spreading_ratio, transport_ratio_row, transport_ratio_column)
        return member
    return lax.map(single, member_collection)

def inverse_root(system):
    identity = jnp.eye(MEMBERS, dtype=jnp.float32)
    norm_scale = jnp.sqrt(jnp.sum(system * system))
    current = system / norm_scale
    inverse = identity
    for repeat in range(NS_ITERS):
        factor = 1.5 * identity - 0.5 * jnp.dot(inverse, current, precision=lax.Precision.HIGHEST)
        current = jnp.dot(current, factor, precision=lax.Precision.HIGHEST)
        inverse = jnp.dot(factor, inverse, precision=lax.Precision.HIGHEST)
    return (inverse / jnp.sqrt(norm_scale)).astype(jnp.bfloat16)

def reference(member_collection, spreading_ratio, transport_ratio_row, transport_ratio_column, obs_patch):
    prior_member_fields = march_prediction(member_collection, spreading_ratio, transport_ratio_row, transport_ratio_column, EARLIER_INCREMENTS)
    blocks = prior_member_fields.reshape(MEMBERS, FL, NX // PX, PX, NPY, PY).transpose(2, 4, 0, 1, 3, 5).reshape(PATCHES, MEMBERS, PATCH)

    def moments(block):
        values = block.astype(jnp.float32)
        centre = lax.optimization_barrier(jnp.mean(values, axis=0))
        anomaly = (values - centre[None, :]).astype(jnp.bfloat16)
        gram_matrix = jnp.dot(anomaly, anomaly.T, preferred_element_type=jnp.float32) / PATCH
        return (centre, anomaly, gram_matrix)
    centres, anomalies, grams = lax.map(moments, blocks)
    grid_grams = grams.reshape(NX // PX, NPY, MEMBERS, MEMBERS)
    averaged = (2.0 * grid_grams + jnp.roll(grid_grams, 1, 0) + jnp.roll(grid_grams, -1, 0) + jnp.roll(grid_grams, 1, 1) + jnp.roll(grid_grams, -1, 1)) / 6.0
    averaged = averaged.reshape(PATCHES, MEMBERS, MEMBERS)
    counts = lax.optimization_barrier(jnp.sum((obs_patch[:, None] == jnp.arange(PATCHES, dtype=jnp.int32)[None, :]).astype(jnp.float32), axis=0))
    obs_weight = counts / (counts + float(OBS_HALF))

    def analyse(inputs):
        centre, anomaly, average, weight = inputs
        system = jnp.eye(MEMBERS, dtype=jnp.float32) + weight * average
        weights = inverse_root(system)
        return (centre[None, :] + jnp.dot(weights.T, anomaly, preferred_element_type=jnp.float32)).astype(jnp.bfloat16)
    updated = lax.map(analyse, (centres, anomalies, averaged, obs_weight))
    corrected_member_fields = updated.reshape(NX // PX, NPY, MEMBERS, FL, PX, PY).transpose(2, 3, 0, 4, 1, 5).reshape(MEMBERS, FL, NX, NY)
    return march_prediction(corrected_member_fields, spreading_ratio, transport_ratio_row, transport_ratio_column, LATER_INCREMENTS)
```

```python
import jax
import jax.numpy as jnp
from jax import lax
from jax.experimental import pallas as pl
from jax.experimental.pallas import tpu as pltpu
from jax.sharding import PartitionSpec as P

F32 = jnp.float32
BF16 = jnp.bfloat16
MESH = pl.DeviceIdType.MESH
VMEM_LIMIT = 50 * 1024 * 1024
NS_ITERS = 14
PLAIN_NORM = 2500.0
CONVERGED = 1e-6
NT = (((1,), (1,)), ((), ()))
TN = (((0,), (0,)), ((), ()))


def place():
    tile = lax.axis_index("tile")
    mem = lax.axis_index("mem")
    ring = tile // 2
    half = lax.rem(tile, 2)
    return ring, half, mem, half * 4 + mem


def target(ring, slot):
    return {"mem": lax.rem(slot, 4), "tile": 2 * ring + slot // 4}


def remote(src, dst, send_sem, recv_sem, ring, slot):
    return pltpu.make_async_remote_copy(
        src_ref=src,
        dst_ref=dst,
        send_sem=send_sem,
        recv_sem=recv_sem,
        device_id=target(ring, slot),
        device_id_type=MESH,
    )


def signal(sem, ring, slot):
    pl.semaphore_signal(sem, inc=1, device_id=target(ring, slot), device_id_type=MESH)


def stencil(c, bx, ax, by, ay, s, sx, sy):
    return c - sx * (c - bx) - sy * (c - by) + s * (ax + bx + ay + by - 4.0 * c)


def rounded(x):
    return x.astype(BF16).astype(F32)


def loop(lower, upper, body):
    def step(i, carry):
        body(i)
        return carry

    lax.fori_loop(lower, upper, step, 0)


def forecast_kernel(
    rings,
    v_ref,
    spread_ref,
    sx_ref,
    sy_ref,
    obs_ref,
    anom_ref,
    cen_ref,
    avg_ref,
    wt_ref,
    coef_ref,
    snd,
    rcv,
    u0,
    u1,
    coef,
    spr,
    cst,
    cra,
    crb,
    gpk,
    gab,
    gbe,
    gle,
    gri,
    main_send,
    main_recv,
    halo_send,
    halo_recv,
    spr_send,
    spr_recv,
    cnt_send,
    cnt_recv,
    sum_send,
    sum_recv,
    gram_send,
    gram_recv,
):
    ring, half, mem, slot = place()
    above = lax.rem(ring + rings - 1, rings)
    below = lax.rem(ring + 1, rings)
    beside = lax.rem(ring + rings + 2 * half - 1, rings)

    barrier = pltpu.get_barrier_semaphore()
    loop(1, 8, lambda j: signal(barrier, ring, lax.rem(slot + j, 8)))
    loop(1, rings, lambda j: signal(barrier, lax.rem(ring + j, rings), slot))
    loop(0, 4, lambda j: signal(barrier, above, 4 + j))
    loop(0, 4, lambda j: signal(barrier, below, j))

    obs = obs_ref[...]
    in_ring = lax.broadcasted_iota(jnp.int32, (rings, 256), 0) == obs // 32
    in_patch = lax.broadcasted_iota(jnp.int32, (128, 256), 0) == lax.rem(obs, 32)
    tally = lax.dot_general(
        in_ring.astype(F32).astype(BF16), in_patch.astype(F32).astype(BF16), NT,
        preferred_element_type=F32,
    )
    for r in range(rings):
        cst[r] = jnp.broadcast_to(tally[r : r + 1, :], (8, 128))
    cra[ring] = cst[ring]
    spr[pl.ds(8 + 8 * half, 8)] = spread_ref[...]

    pl.semaphore_wait(barrier, 7 + rings - 1 + 8)

    spr_here = remote(
        spread_ref, spr.at[pl.ds(8 + 8 * half, 8)], spr_send.at[0], spr_recv.at[0],
        ring, (1 - half) * 4 + mem,
    )
    spr_here.start()
    spr_far = [
        remote(
            spread_ref, spr.at[pl.ds(24 - 24 * half, 8)], spr_send.at[1 + k],
            spr_recv.at[2 - half], beside, 4 * k + mem,
        )
        for k in range(2)
    ]
    for copy in spr_far:
        copy.start()

    def count_copy(j):
        to = lax.rem(ring + j, rings)
        return remote(cst.at[to], cra.at[ring], cnt_send.at[j], cnt_recv.at[ring], to, slot)

    loop(1, rings, lambda j: count_copy(j).start())

    edge_pair = 3 * half

    def permuted(to):
        row = lax.broadcasted_iota(jnp.int32, (160, 128), 0)
        lane = lax.broadcasted_iota(jnp.int32, (160, 128), 1)
        column = lax.rem(16 * to + row // 8 + 126, 128)
        level = lax.rem(row, 8)
        same = column == lane
        pick = jnp.concatenate(
            [jnp.where(same & (level == f), 1.0, 0.0).astype(BF16) for f in range(8)], axis=1
        )
        block = lax.dot_general(pick, v_ref[...], NT, preferred_element_type=F32).astype(BF16)
        for pair in range(4):
            snd[to, pair] = block[:, pair * 128 : (pair + 1) * 128]

    def main_copy(to):
        return remote(
            snd.at[to], rcv.at[pl.ds(1 + 4 * half, 4), mem], main_send.at[to],
            main_recv.at[slot], ring, to,
        )

    def halo_copy(to):
        return remote(
            snd.at[to, edge_pair], rcv.at[9 - 9 * half, mem], halo_send.at[to],
            halo_recv.at[1 - half, mem], beside, to,
        )

    def send_block(j):
        to = lax.rem(slot + j, 8)
        permuted(to)
        main_copy(to).start()
        halo_copy(to).start()

    loop(1, 8, send_block)
    permuted(slot)
    halo_copy(slot).start()
    own = pltpu.make_async_copy(
        snd.at[slot], rcv.at[pl.ds(1 + 4 * half, 4), mem], main_recv.at[slot]
    )
    own.start()

    def count_wait(j):
        frm = lax.rem(ring + j, rings)
        remote(cst.at[0], cra.at[frm], cnt_send.at[j], cnt_recv.at[frm], frm, slot).wait_recv()

    loop(1, rings, count_wait)
    total = cra[0]
    for r in range(1, rings):
        total = total + cra[r]
    crb[slot] = total

    def sum_copy(j):
        return remote(
            crb.at[slot], crb.at[slot], sum_send.at[j], sum_recv.at[slot], ring,
            lax.rem(slot + j, 8),
        )

    loop(1, 8, lambda j: sum_copy(j).start())

    spr_here.wait()
    for copy in spr_far:
        copy.wait_send()
    for k in range(2):
        remote(
            spread_ref, spr.at[pl.ds(24 * k, 8)], spr_send.at[0], spr_recv.at[1 + k],
            beside, mem,
        ).wait_recv()

    def spread_row(i):
        lane = lax.broadcasted_iota(jnp.int32, (20, 8, 128), 2)
        column = lax.rem(
            lax.broadcasted_iota(jnp.int32, (20, 8, 128), 0) + 16 * slot + 126, 128
        )
        values = jnp.where(lane == column, spr[i + 6][None], 0.0)
        coef[i] = jnp.broadcast_to(jnp.sum(values, axis=2, keepdims=True), (20, 8, 128))

    loop(0, 20, spread_row)

    def coef_row(i):
        coef_ref[i] = coef[i + 2, 2:18]

    loop(0, 16, coef_row)

    def sum_wait(j):
        frm = lax.rem(slot + j, 8)
        remote(crb.at[slot], crb.at[frm], sum_send.at[j], sum_recv.at[frm], ring, frm).wait_recv()

    loop(1, 8, sum_wait)
    counts = crb[0]
    for k in range(1, 8):
        counts = counts + crb[k]
    lane = lax.broadcasted_iota(jnp.int32, (8, 128), 1)
    for h in range(2):
        for c in range(2):
            mine = jnp.where(lane == h * 16 + 2 * slot + c, counts, 0.0)
            count = jnp.sum(mine, axis=1, keepdims=True)
            wt_ref[2 * h + c] = jnp.broadcast_to(count / (count + 16.0), (8, 128))

    own.wait()

    def main_wait(j):
        frm = lax.rem(slot + j, 8)
        remote(
            snd.at[0], rcv.at[pl.ds(1 + 4 * (frm // 4), 4), lax.rem(frm, 4)], main_send.at[0],
            main_recv.at[frm], ring, frm,
        ).wait_recv()

    loop(1, 8, main_wait)

    def halo_wait(k):
        remote(
            snd.at[0, 0], rcv.at[9 * (k // 4), lax.rem(k, 4)], halo_send.at[0],
            halo_recv.at[k // 4, lax.rem(k, 4)], beside, slot,
        ).wait_recv()

    loop(0, 8, halo_wait)

    def unshuffle(pair):
        low = lax.broadcasted_iota(jnp.int32, (160, 128), 1) < 64
        for mh in range(2):
            r0 = rcv[pair, 2 * mh].astype(F32)
            r1 = rcv[pair, 2 * mh + 1].astype(F32)
            even = jnp.where(low, r0, pltpu.roll(r1, 64, 1))
            odd = jnp.where(low, pltpu.roll(r0, 64, 1), r1)
            u0[mh, 2 * pair] = even.reshape(20, 8, 128)
            u0[mh, 2 * pair + 1] = odd.reshape(20, 8, 128)

    loop(0, 10, unshuffle)
    sx = sx_ref[...][None]
    sy = sy_ref[...][None]

    def first(x):
        s = coef[x, 1:19]
        for mh in range(2):
            u1[mh, x - 1] = rounded(
                stencil(
                    u0[mh, x, 1:19], u0[mh, x - 1, 1:19], u0[mh, x + 1, 1:19],
                    u0[mh, x, 0:18], u0[mh, x, 2:20], s, sx, sy,
                )
            )

    loop(1, 19, first)

    for h in range(2):

        def second(i):
            x = 8 * h + i + 1
            s = coef[x + 1, 2:18]
            prior = [
                rounded(
                    stencil(
                        u1[mh, x, 1:17], u1[mh, x - 1, 1:17], u1[mh, x + 1, 1:17],
                        u1[mh, x, 0:16], u1[mh, x, 2:18], s, sx, sy,
                    )
                )
                for mh in range(2)
            ]
            centre = jnp.sum(prior[0] + prior[1], axis=2, keepdims=True) * (1.0 / 256.0)
            centre = jnp.broadcast_to(centre, (16, 8, 128))
            for c in range(2):
                cols = slice(8 * c, 8 * c + 8)
                cen_ref[2 * h + c, i] = centre[cols].reshape(64, 128)
                for mh in range(2):
                    anom_ref[2 * h + c, i, :, mh * 128 : mh * 128 + 128] = (
                        (prior[mh][cols] - centre[cols]).reshape(64, 128).astype(BF16)
                    )

        loop(0, 8, second)

    row = lax.broadcasted_iota(jnp.int32, (128, 128), 0)
    col = lax.broadcasted_iota(jnp.int32, (128, 128), 1)

    def gram(p):
        a = anom_ref[p].reshape(512, 256)
        g = lax.dot_general(a, a, TN, preferred_element_type=F32) * (1.0 / 512.0)
        last = g[128:, 128:]
        gpk[p, 0:128] = g[:128, 128:]
        gpk[p, 128:256] = jnp.where(row >= col, g[:128, :128], last)
        diag = jnp.sum(jnp.where(row == col, last, 0.0), axis=0, keepdims=True)
        gpk[p, 256:264] = jnp.broadcast_to(diag, (8, 128))

    loop(0, 4, gram)
    copies = [
        remote(gpk.at[0:2], gbe, gram_send.at[0], gram_recv.at[0], above, slot),
        remote(gpk.at[2:4], gab, gram_send.at[1], gram_recv.at[1], below, slot),
    ]
    left = lax.rem(slot + 7, 8)
    right = lax.rem(slot + 1, 8)
    for h in range(2):
        copies.append(
            remote(gpk.at[2 * h], gri.at[h], gram_send.at[2 + h], gram_recv.at[2 + h], ring, left)
        )
        copies.append(
            remote(
                gpk.at[2 * h + 1], gle.at[h], gram_send.at[4 + h], gram_recv.at[4 + h], ring, right
            )
        )
    for copy in copies:
        copy.start()
    loop(1, rings, lambda j: count_copy(j).wait_send())
    loop(1, 8, lambda j: sum_copy(j).wait_send())
    loop(1, 8, lambda j: main_copy(lax.rem(slot + j, 8)).wait_send())
    loop(0, 8, lambda j: halo_copy(j).wait_send())
    for copy in copies:
        copy.wait()
    for h in range(2):
        for c in range(2):
            p = 2 * h + c
            up = gpk[c] if h else gab[c]
            down = gbe[c] if h else gpk[2 + c]
            lft = gpk[2 * h] if c else gle[h]
            rgt = gri[h] if c else gpk[2 * h + 1]
            avg_ref[p] = (2.0 * gpk[p] + up + down + lft + rgt) * (1.0 / 6.0)


def split(x):
    hi = x.astype(BF16)
    return hi, (x - hi.astype(F32)).astype(BF16)


def product(a, b):
    (ah, al), (bh, bl) = a, b
    return (
        jnp.dot(ah, bh, preferred_element_type=F32)
        + jnp.dot(ah, bl, preferred_element_type=F32)
        + jnp.dot(al, bh, preferred_element_type=F32)
    )


def analysis_kernel(anom_ref, cen_ref, avg_ref, wt_ref, out_ref, yh, yl, zh, zl):
    row = lax.broadcasted_iota(jnp.int32, (256, 256), 0)
    col = lax.broadcasted_iota(jnp.int32, (256, 256), 1)
    diagonal = row == col
    identity = jnp.where(diagonal, 1.0, 0.0)
    low = row[:128, :128] >= col[:128, :128]
    on = row[:128, :128] == col[:128, :128]

    def coefs(low_end, plain):
        alpha2 = jnp.where(plain, 1.0, 3.0 / (1.0 + low_end + low_end * low_end))
        alpha = jnp.sqrt(alpha2)
        reach = alpha * low_end
        after = 0.5 * reach * (3.0 - reach * reach)
        return 1.5 * alpha, 0.5 * alpha * alpha2, jnp.minimum(after, 1.0)

    ends, plains, scales = [], [], []
    for p in range(4):
        packed = avg_ref[p]
        upper_right = packed[0:128]
        both = packed[128:256]
        turned = both.T
        first = jnp.where(low, both, turned)
        last = jnp.where(on, jnp.broadcast_to(packed[256:257], (128, 128)), jnp.where(low, turned, both))
        averaged = jnp.concatenate(
            [
                jnp.concatenate([first, upper_right], axis=1),
                jnp.concatenate([upper_right.T, last], axis=1),
            ],
            axis=0,
        )
        system = identity + wt_ref[p, 0:1, 0:1] * averaged
        squares = jnp.sum(jnp.sum(system * system, axis=1, keepdims=True), axis=0, keepdims=True)
        norm = jnp.sqrt(squares)
        rows = jnp.max(
            jnp.sum(jnp.abs(system), axis=0, keepdims=True), axis=1, keepdims=True
        )
        plain = norm > PLAIN_NORM
        scale = jnp.where(plain, norm, jnp.minimum(norm, rows * 1.000001))
        start = system / scale
        low_end = jnp.where(plain, 0.0, jnp.sqrt(1.0 / scale) * 0.9999)
        a, b, after = coefs(low_end, plain)
        factor = a * identity - b * start
        y = product(split(start), split(factor))
        yh[p], yl[p] = split(y)
        zh[p], zl[p] = split(factor)
        ends.append(after)
        plains.append(plain)
        scales.append(scale)

    def some_left(ends, plains, k):
        left = jnp.zeros((1, 1), F32)
        for end, plain in zip(ends, plains):
            _, _, after = coefs(end, plain)
            todo = jnp.where(plain, jnp.where(k + 1 < NS_ITERS, 1.0, 0.0), jnp.where(1.0 - after > CONVERGED, 1.0, 0.0))
            left = jnp.maximum(left, todo)
        return jnp.max(left) > 0.5

    def body(carry):
        k, _, *ends = carry
        following = []
        for p in range(4):
            a, b, after = coefs(ends[p], plains[p])
            y = (yh[p], yl[p])
            z = (zh[p], zl[p])
            factor = split(a * identity - b * product(z, y))
            ny = product(y, factor)
            nz = product(factor, z)
            yh[p], yl[p] = split(ny)
            zh[p], zl[p] = split(nz)
            following.append(after)
        return (k + 1, some_left(following, plains, k + 1), *following)

    last_k, _, *ends = lax.while_loop(
        lambda carry: carry[1], body, (1, some_left(ends, plains, 1), *ends)
    )
    for p in range(4):
        a, b, _ = coefs(ends[p], plains[p])
        z = (zh[p], zl[p])
        factor = split(a * identity - b * product(z, (yh[p], yl[p])))
        inverse = product(factor, z)
        weights = (inverse / jnp.sqrt(scales[p])).astype(BF16)
        a = anom_ref[p].reshape(512, 256)
        update = jnp.dot(a, weights, preferred_element_type=F32)
        centre = cen_ref[p].reshape(512, 128)
        centre = jnp.concatenate([centre, centre], axis=1)
        h, c = p // 2, p % 2
        out_ref[8 * h : 8 * h + 8, 64 * c : 64 * c + 64, :] = (
            (centre + update).astype(BF16).reshape(8, 64, 256)
        )


def return_kernel(
    rings,
    f_ref,
    coef_ref,
    sx_ref,
    sy_ref,
    out_ref,
    g,
    west,
    east,
    from_above,
    from_below,
    from_left,
    from_right,
    snd,
    rcv,
    edge_send,
    edge_recv,
    main_send,
    main_recv,
    own_sem,
):
    ring, half, mem, slot = place()
    above = lax.rem(ring + rings - 1, rings)
    below = lax.rem(ring + 1, rings)
    left = lax.rem(slot + 7, 8)
    right = lax.rem(slot + 1, 8)
    barrier = pltpu.get_barrier_semaphore()
    loop(1, 8, lambda j: signal(barrier, ring, lax.rem(slot + j, 8)))
    signal(barrier, above, slot)
    signal(barrier, below, slot)

    def widen(x):
        plane = f_ref[x].astype(F32)
        for mh in range(2):
            g[mh, x + 1, 1:17] = plane[:, mh * 128 : mh * 128 + 128].reshape(16, 8, 128)

    loop(0, 16, widen)
    for mh in range(2):
        lanes = slice(mh * 128, mh * 128 + 128)
        west[:, lanes] = g[mh, 1:17, 1].reshape(128, 128).astype(BF16)
        east[:, lanes] = g[mh, 1:17, 16].reshape(128, 128).astype(BF16)
    pl.semaphore_wait(barrier, 9)
    edges = [
        remote(f_ref.at[0], from_below, edge_send.at[0], edge_recv.at[0], above, slot),
        remote(f_ref.at[15], from_above, edge_send.at[1], edge_recv.at[1], below, slot),
        remote(west, from_right, edge_send.at[2], edge_recv.at[2], ring, left),
        remote(east, from_left, edge_send.at[3], edge_recv.at[3], ring, right),
    ]
    for copy in edges:
        copy.start()
    for copy in edges:
        copy.wait()
    for mh in range(2):
        lanes = slice(mh * 128, mh * 128 + 128)
        g[mh, 0, 1:17] = from_above[:, lanes].astype(F32).reshape(16, 8, 128)
        g[mh, 17, 1:17] = from_below[:, lanes].astype(F32).reshape(16, 8, 128)
        g[mh, 1:17, 0] = from_left[:, lanes].astype(F32).reshape(16, 8, 128)
        g[mh, 1:17, 17] = from_right[:, lanes].astype(F32).reshape(16, 8, 128)
    sx = sx_ref[...][None]
    sy = sy_ref[...][None]
    low = lax.broadcasted_iota(jnp.int32, (128, 128), 1) < 64

    def main_copy(pair, to):
        return remote(
            snd.at[pair, to], rcv.at[pair, slot], main_send.at[pair, to],
            main_recv.at[pair, slot], ring, to,
        )

    def own_copy(pair):
        return pltpu.make_async_copy(snd.at[pair, slot], rcv.at[pair, slot], own_sem.at[pair])

    def send_pair(pair):
        for h in range(2):
            x = 8 * h + 2 * pair + 1
            for mh in range(2):
                even, odd = [
                    stencil(
                        g[mh, x + k, 1:17], g[mh, x + k - 1, 1:17], g[mh, x + k + 1, 1:17],
                        g[mh, x + k, 0:16], g[mh, x + k, 2:18], coef_ref[x + k - 1], sx, sy,
                    ).reshape(128, 128)
                    for k in range(2)
                ]
                snd[pair, 4 * h + 2 * mh] = jnp.where(low, even, pltpu.roll(odd, 64, 1)).astype(BF16)
                snd[pair, 4 * h + 2 * mh + 1] = jnp.where(low, pltpu.roll(even, 64, 1), odd).astype(BF16)
        loop(1, 8, lambda j: main_copy(pair, lax.rem(slot + j, 8)).start())
        own_copy(pair).start()

    loop(0, 4, send_pair)

    row = lax.broadcasted_iota(jnp.int32, (1024, 128), 0)
    lane = lax.broadcasted_iota(jnp.int32, (1024, 128), 1)
    same = row // 8 == lane
    level = lax.rem(row, 8)
    pick = jnp.concatenate(
        [jnp.where(same & (level == f), 1.0, 0.0).astype(BF16) for f in range(8)], axis=1
    )

    def receive_pair(pair):
        own_copy(pair).wait()

        def wait(j):
            frm = lax.rem(slot + j, 8)
            remote(
                snd.at[pair, frm], rcv.at[pair, frm], main_send.at[pair, frm],
                main_recv.at[pair, frm], ring, frm,
            ).wait_recv()

        loop(1, 8, wait)
        block = rcv[pair].reshape(1024, 128)
        result = lax.dot_general(block, pick, TN, preferred_element_type=F32).astype(BF16)
        out_ref[2 * pair] = result[:64]
        out_ref[2 * pair + 1] = result[64:]

    loop(0, 4, receive_pair)

    def finish(pair):
        loop(1, 8, lambda j: main_copy(pair, lax.rem(slot + j, 8)).wait_send())

    loop(0, 4, finish)


def vmem(count):
    return [pl.BlockSpec(memory_space=pltpu.VMEM)] * count


def local(member_collection, spreading_ratio, transport_ratio_row, transport_ratio_column, obs_patch):
    rings = lax.axis_size("tile") // 2
    DMA = pltpu.SemaphoreType.DMA
    state = jnp.transpose(member_collection, (2, 0, 1, 3)).reshape(512, 1024)
    spread = jnp.transpose(spreading_ratio, (1, 0, 2))
    sx = jnp.broadcast_to(transport_ratio_row[:, None], (8, 128))
    sy = jnp.broadcast_to(transport_ratio_column[:, None], (8, 128))
    obs = obs_patch.reshape(1, 256)

    def shape(dims, dtype=F32):
        return jax.ShapeDtypeStruct(dims, dtype)

    anom, cen, avg, wt, coef = pl.pallas_call(
        lambda *refs: forecast_kernel(rings, *refs),
        out_shape=[
            shape((4, 8, 64, 256), BF16),
            shape((4, 8, 64, 128)),
            shape((4, 264, 128)),
            shape((4, 8, 128)),
            shape((16, 16, 8, 128)),
        ],
        in_specs=vmem(5),
        out_specs=vmem(5),
        scratch_shapes=[
            pltpu.VMEM((8, 4, 160, 128), BF16),
            pltpu.VMEM((10, 4, 160, 128), BF16),
            pltpu.VMEM((2, 20, 20, 8, 128), F32),
            pltpu.VMEM((2, 18, 18, 8, 128), F32),
            pltpu.VMEM((20, 20, 8, 128), F32),
            pltpu.VMEM((32, 8, 128), F32),
            pltpu.VMEM((rings, 8, 128), F32),
            pltpu.VMEM((rings, 8, 128), F32),
            pltpu.VMEM((8, 8, 128), F32),
            pltpu.VMEM((4, 264, 128), F32),
            pltpu.VMEM((2, 264, 128), F32),
            pltpu.VMEM((2, 264, 128), F32),
            pltpu.VMEM((2, 264, 128), F32),
            pltpu.VMEM((2, 264, 128), F32),
            DMA((8,)),
            DMA((8,)),
            DMA((8,)),
            DMA((2, 4)),
            DMA((3,)),
            DMA((3,)),
            DMA((rings,)),
            DMA((rings,)),
            DMA((8,)),
            DMA((8,)),
            DMA((6,)),
            DMA((6,)),
        ],
        compiler_params=pltpu.CompilerParams(
            collective_id=0, has_side_effects=True, vmem_limit_bytes=VMEM_LIMIT
        ),
    )(state, spread, sx, sy, obs)

    field = pl.pallas_call(
        analysis_kernel,
        out_shape=shape((16, 128, 256), BF16),
        in_specs=vmem(4),
        out_specs=pl.BlockSpec(memory_space=pltpu.VMEM),
        scratch_shapes=[pltpu.VMEM((4, 256, 256), BF16)] * 4,
        compiler_params=pltpu.CompilerParams(vmem_limit_bytes=VMEM_LIMIT),
    )(anom, cen, avg, wt)

    out = pl.pallas_call(
        lambda *refs: return_kernel(rings, *refs),
        out_shape=shape((8, 64, 1024), BF16),
        in_specs=vmem(4),
        out_specs=pl.BlockSpec(memory_space=pltpu.VMEM),
        scratch_shapes=[
            pltpu.VMEM((2, 18, 18, 8, 128), F32),
            pltpu.VMEM((128, 256), BF16),
            pltpu.VMEM((128, 256), BF16),
            pltpu.VMEM((128, 256), BF16),
            pltpu.VMEM((128, 256), BF16),
            pltpu.VMEM((128, 256), BF16),
            pltpu.VMEM((128, 256), BF16),
            pltpu.VMEM((4, 8, 128, 128), BF16),
            pltpu.VMEM((4, 8, 128, 128), BF16),
            DMA((4,)),
            DMA((4,)),
            DMA((4, 8)),
            DMA((4, 8)),
            DMA((4,)),
        ],
        compiler_params=pltpu.CompilerParams(
            collective_id=1, has_side_effects=True, vmem_limit_bytes=VMEM_LIMIT
        ),
    )(field, coef, sx, sy)
    return jnp.transpose(out.reshape(8, 64, 8, 128), (1, 2, 0, 3))


def solution(mesh):
    placed = (P("mem", None, "tile", None), P(None, "tile", None), P(), P(), P(("mem", "tile")))
    return jax.shard_map(
        local, mesh=mesh, in_specs=placed, out_specs=P("mem", None, "tile", None), check_vma=False
    )
```

```python
import jax
import jax.numpy as jnp
from jax import lax
from jax.experimental import pallas as pl
from jax.experimental.pallas import tpu as pltpu
from jax.sharding import PartitionSpec as P

F32 = jnp.float32
BF16 = jnp.bfloat16
MESH = pl.DeviceIdType.MESH
VMEM_LIMIT = 50 * 1024 * 1024
NS_ITERS = 14
PLAIN_NORM = 2500.0
CONVERGED = 1e-6
NT = (((1,), (1,)), ((), ()))
TN = (((0,), (0,)), ((), ()))


def place():
    tile = lax.axis_index("tile")
    mem = lax.axis_index("mem")
    ring = tile // 2
    half = lax.rem(tile, 2)
    return ring, half, mem, half * 4 + mem


def target(ring, slot):
    return {"mem": lax.rem(slot, 4), "tile": 2 * ring + slot // 4}


def remote(src, dst, send_sem, recv_sem, ring, slot):
    return pltpu.make_async_remote_copy(
        src_ref=src,
        dst_ref=dst,
        send_sem=send_sem,
        recv_sem=recv_sem,
        device_id=target(ring, slot),
        device_id_type=MESH,
    )


def signal(sem, ring, slot):
    pl.semaphore_signal(sem, inc=1, device_id=target(ring, slot), device_id_type=MESH)


def stencil(c, bx, ax, by, ay, s, sx, sy):
    return c - sx * (c - bx) - sy * (c - by) + s * (ax + bx + ay + by - 4.0 * c)


def rounded(x):
    return x.astype(BF16).astype(F32)


def loop(lower, upper, body):
    def step(i, carry):
        body(i)
        return carry

    lax.fori_loop(lower, upper, step, 0)


def forecast_kernel(
    rings,
    u_hbm,
    spread_hbm,
    sx_hbm,
    sy_hbm,
    obs_hbm,
    anom_ref,
    cen_ref,
    avg_ref,
    wt_ref,
    coef_ref,
    raw,
    spread_in,
    sx_in,
    sy_in,
    obs_in,
    state,
    picks,
    snd,
    rcv,
    u0,
    u1,
    coef,
    spr,
    cst,
    cra,
    crb,
    gpk,
    gab,
    gbe,
    gle,
    gri,
    load_sem,
    edge_send,
    edge_recv,
    rest_send,
    rest_recv,
    halo_send,
    halo_recv,
    spr_send,
    spr_recv,
    cnt_send,
    cnt_recv,
    sum_send,
    sum_recv,
    gram_send,
    gram_recv,
):
    ring, half, mem, slot = place()
    above = lax.rem(ring + rings - 1, rings)
    below = lax.rem(ring + 1, rings)

    barrier = pltpu.get_barrier_semaphore()
    loop(1, 8, lambda j: signal(barrier, ring, lax.rem(slot + j, 8)))
    loop(1, rings, lambda j: signal(barrier, lax.rem(ring + j, rings), slot))
    loads = [
        pltpu.make_async_copy(src, dst, load_sem.at[k])
        for k, (src, dst) in enumerate(
            [
                (u_hbm, raw), (spread_hbm, spread_in), (sx_hbm, sx_in), (sy_hbm, sy_in),
                (obs_hbm, obs_in),
            ]
        )
    ]
    for copy in loads:
        copy.start()

    k = lax.broadcasted_iota(jnp.int32, (512, 512), 1)
    r = lax.broadcasted_iota(jnp.int32, (512, 512), 0)
    turn = jnp.where(k == lax.rem(r, 64) * 8 + r // 64, 1.0, 0.0).astype(BF16)
    loads[0].wait()
    for f in range(8):
        level = raw[:, f].astype(F32).reshape(512, 128).astype(BF16)
        state[:, f * 128 : f * 128 + 128] = jnp.dot(
            turn, level, preferred_element_type=F32
        ).astype(BF16)

    edge_pair = 3 * half
    rest_pair = 1 - half
    edge_rows = pl.ds(pl.multiple_of(128 * edge_pair, 128), 128)
    rest_rows = pl.ds(pl.multiple_of(128 * rest_pair, 128), 384)

    def edge_block(to):
        row = lax.broadcasted_iota(jnp.int32, (160, 128), 0)
        lane = lax.broadcasted_iota(jnp.int32, (160, 128), 1)
        column = lax.rem(16 * to + row // 8 + 126, 128)
        level = jnp.where(column == lane, lax.rem(row, 8), 8)
        for f in range(8):
            picks[to, :, f * 128 : f * 128 + 128] = jnp.where(level == f, 1.0, 0.0).astype(BF16)
        snd[to, edge_pair] = lax.dot_general(
            picks[to], state[edge_rows, :], NT, preferred_element_type=F32
        ).astype(BF16)

    def rest_block(to):
        block = lax.dot_general(
            picks[to], state[rest_rows, :], NT, preferred_element_type=F32
        ).astype(BF16)
        for pair in range(3):
            snd[to, rest_pair + pair] = block[:, pair * 128 : (pair + 1) * 128]

    def edge_copy(to):
        return remote(
            snd.at[to, edge_pair], rcv.at[1 + 7 * half, mem], edge_send.at[to],
            edge_recv.at[slot], ring, to,
        )

    def rest_copy(to):
        return remote(
            snd.at[to, pl.ds(rest_pair, 3)], rcv.at[pl.ds(2 + 3 * half, 3), mem],
            rest_send.at[to], rest_recv.at[slot], ring, to,
        )

    edge_block(lax.rem(slot + 1, 8))
    pl.semaphore_wait(barrier, 7 + rings - 1)
    edge_copy(lax.rem(slot + 1, 8)).start()

    def send_edge(j):
        to = lax.rem(slot + j, 8)
        edge_block(to)
        edge_copy(to).start()

    loop(2, 8, send_edge)

    def send_rest(j):
        to = lax.rem(slot + j, 8)
        rest_block(to)
        rest_copy(to).start()

    loop(1, 4, send_rest)
    edge_block(slot)
    own_edge = pltpu.make_async_copy(
        snd.at[slot, edge_pair], rcv.at[1 + 7 * half, mem], edge_recv.at[slot]
    )
    own_edge.start()
    loop(4, 8, send_rest)
    rest_block(slot)
    own_rest = pltpu.make_async_copy(
        snd.at[slot, pl.ds(rest_pair, 3)], rcv.at[pl.ds(2 + 3 * half, 3), mem],
        rest_recv.at[slot],
    )
    own_rest.start()

    loads[1].wait()
    mine = 8 + 8 * half
    for x in range(8):
        spr[mine + x] = spread_in[:, x, :]
    spr_here = remote(
        spr.at[pl.ds(mine, 8)], spr.at[pl.ds(mine, 8)], spr_send.at[0], spr_recv.at[0],
        ring, (1 - half) * 4 + mem,
    )
    spr_here.start()

    own_edge.wait()

    def edge_wait(j):
        frm = lax.rem(slot + j, 8)
        remote(
            snd.at[0, 0], rcv.at[1 + 7 * (frm // 4), lax.rem(frm, 4)], edge_send.at[frm],
            edge_recv.at[frm], ring, frm,
        ).wait_recv()

    loop(1, 8, edge_wait)
    halos = [
        remote(rcv.at[1], rcv.at[9], halo_send.at[0], halo_recv.at[0], above, slot),
        remote(rcv.at[8], rcv.at[0], halo_send.at[1], halo_recv.at[1], below, slot),
    ]
    for copy in halos:
        copy.start()

    loads[4].wait()
    obs = obs_in[...]
    in_ring = lax.broadcasted_iota(jnp.int32, (rings, 256), 0) == obs // 32
    in_patch = lax.broadcasted_iota(jnp.int32, (128, 256), 0) == lax.rem(obs, 32)
    tally = lax.dot_general(
        in_ring.astype(F32).astype(BF16), in_patch.astype(F32).astype(BF16), NT,
        preferred_element_type=F32,
    )
    for r in range(rings):
        cst[r] = jnp.broadcast_to(tally[r : r + 1, :], (8, 128))
    cra[ring] = cst[ring]

    def count_copy(j):
        to = lax.rem(ring + j, rings)
        return remote(cst.at[to], cra.at[ring], cnt_send.at[j], cnt_recv.at[ring], to, slot)

    loop(1, rings, lambda j: count_copy(j).start())

    spr_here.wait_send()
    other = 16 - 8 * half
    remote(
        spr.at[pl.ds(other, 8)], spr.at[pl.ds(other, 8)], spr_send.at[0], spr_recv.at[0],
        ring, (1 - half) * 4 + mem,
    ).wait_recv()
    spr_far = [
        remote(spr.at[8:10], spr.at[24:26], spr_send.at[1], spr_recv.at[1], above, slot),
        remote(spr.at[22:24], spr.at[6:8], spr_send.at[2], spr_recv.at[2], below, slot),
    ]
    for copy in spr_far:
        copy.start()

    def spread_row(i):
        lane = lax.broadcasted_iota(jnp.int32, (20, 8, 128), 2)
        column = lax.rem(
            lax.broadcasted_iota(jnp.int32, (20, 8, 128), 0) + 16 * slot + 126, 128
        )
        values = jnp.where(lane == column, spr[i + 6][None], 0.0)
        coef[i] = jnp.broadcast_to(jnp.sum(values, axis=2, keepdims=True), (20, 8, 128))

    loop(2, 18, spread_row)

    def coef_row(i):
        coef_ref[i] = coef[i + 2, 2:18]

    loop(0, 16, coef_row)
    for copy in spr_far:
        copy.wait()
    for i in (0, 1, 18, 19):
        spread_row(i)
    loads[2].wait()
    loads[3].wait()
    sublane = lax.broadcasted_iota(jnp.int32, (8, 128), 0)
    for k, ref in enumerate((sx_in, sy_in)):
        speed = jnp.zeros((8, 128), F32)
        for f in range(8):
            speed = jnp.where(sublane == f, ref[f], speed)
        wt_ref[4 + k] = speed

    def unshuffle(pair):
        low = lax.broadcasted_iota(jnp.int32, (160, 128), 1) < 64
        for mh in range(2):
            r0 = rcv[pair, 2 * mh].astype(F32)
            r1 = rcv[pair, 2 * mh + 1].astype(F32)
            even = jnp.where(low, r0, pltpu.roll(r1, 64, 1))
            odd = jnp.where(low, pltpu.roll(r0, 64, 1), r1)
            u0[mh, 2 * pair] = even.reshape(20, 8, 128)
            u0[mh, 2 * pair + 1] = odd.reshape(20, 8, 128)

    unshuffle(1)
    unshuffle(8)
    for copy in halos:
        copy.wait()
    unshuffle(0)
    unshuffle(9)

    own_rest.wait()

    def rest_wait(j):
        frm = lax.rem(slot + j, 8)
        remote(
            snd.at[0, 0:3], rcv.at[pl.ds(2 + 3 * (frm // 4), 3), lax.rem(frm, 4)],
            rest_send.at[frm], rest_recv.at[frm], ring, frm,
        ).wait_recv()

    loop(1, 8, rest_wait)
    loop(2, 8, unshuffle)
    sx = wt_ref[4][None]
    sy = wt_ref[5][None]

    def first(x):
        s = coef[x, 1:19]
        for mh in range(2):
            u1[mh, x - 1] = rounded(
                stencil(
                    u0[mh, x, 1:19], u0[mh, x - 1, 1:19], u0[mh, x + 1, 1:19],
                    u0[mh, x, 0:18], u0[mh, x, 2:20], s, sx, sy,
                )
            )

    loop(1, 19, first)

    def count_wait(j):
        frm = lax.rem(ring + j, rings)
        remote(cst.at[0], cra.at[frm], cnt_send.at[j], cnt_recv.at[frm], frm, slot).wait_recv()

    loop(1, rings, count_wait)
    total = cra[0]
    for r in range(1, rings):
        total = total + cra[r]
    crb[slot] = total

    def sum_copy(j):
        return remote(
            crb.at[slot], crb.at[slot], sum_send.at[j], sum_recv.at[slot], ring,
            lax.rem(slot + j, 8),
        )

    loop(1, 8, lambda j: sum_copy(j).start())

    row = lax.broadcasted_iota(jnp.int32, (128, 128), 0)
    col = lax.broadcasted_iota(jnp.int32, (128, 128), 1)
    left = lax.rem(slot + 7, 8)
    right = lax.rem(slot + 1, 8)
    copies = []
    for c in range(2):
        for h in range(2):
            p = 2 * h + c

            def second(i, h=h, c=c, p=p):
                x = 8 * h + i + 1
                y = 8 * c + 1
                s = coef[x + 1, y + 1 : y + 9]
                prior = [
                    rounded(
                        stencil(
                            u1[mh, x, y : y + 8], u1[mh, x - 1, y : y + 8],
                            u1[mh, x + 1, y : y + 8], u1[mh, x, y - 1 : y + 7],
                            u1[mh, x, y + 1 : y + 9], s, sx, sy,
                        )
                    )
                    for mh in range(2)
                ]
                centre = jnp.sum(prior[0] + prior[1], axis=2, keepdims=True) * (1.0 / 256.0)
                centre = jnp.broadcast_to(centre, (8, 8, 128))
                cen_ref[p, i] = centre.reshape(64, 128)
                for mh in range(2):
                    anom_ref[p, i, :, mh * 128 : mh * 128 + 128] = (
                        (prior[mh] - centre).reshape(64, 128).astype(BF16)
                    )

            loop(0, 8, second)
            a = anom_ref[p].reshape(512, 256)
            g = lax.dot_general(a, a, TN, preferred_element_type=F32) * (1.0 / 512.0)
            last = g[128:, 128:]
            gpk[p, 0:128] = g[:128, 128:]
            gpk[p, 128:256] = jnp.where(row >= col, g[:128, :128], last)
            diag = jnp.sum(jnp.where(row == col, last, 0.0), axis=0, keepdims=True)
            gpk[p, 256:264] = jnp.broadcast_to(diag, (8, 128))
            vertical = (gab, below) if h else (gbe, above)
            sideways = (gle, right) if c else (gri, left)
            pair = [
                remote(
                    gpk.at[p], vertical[0].at[c], gram_send.at[2 * p], gram_recv.at[2 * p],
                    vertical[1], slot,
                ),
                remote(
                    gpk.at[p], sideways[0].at[h], gram_send.at[2 * p + 1],
                    gram_recv.at[2 * p + 1], ring, sideways[1],
                ),
            ]
            for copy in pair:
                copy.start()
            copies += pair

    def sum_wait(j):
        frm = lax.rem(slot + j, 8)
        remote(crb.at[slot], crb.at[frm], sum_send.at[j], sum_recv.at[frm], ring, frm).wait_recv()

    loop(1, 8, sum_wait)
    counts = crb[0]
    for k in range(1, 8):
        counts = counts + crb[k]
    lane = lax.broadcasted_iota(jnp.int32, (8, 128), 1)
    for h in range(2):
        for c in range(2):
            chosen = jnp.where(lane == h * 16 + 2 * slot + c, counts, 0.0)
            count = jnp.sum(chosen, axis=1, keepdims=True)
            wt_ref[2 * h + c] = jnp.broadcast_to(count / (count + 16.0), (8, 128))
    loop(1, rings, lambda j: count_copy(j).wait_send())
    loop(1, 8, lambda j: sum_copy(j).wait_send())
    loop(1, 8, lambda j: edge_copy(lax.rem(slot + j, 8)).wait_send())
    loop(1, 8, lambda j: rest_copy(lax.rem(slot + j, 8)).wait_send())
    for copy in copies:
        copy.wait()
    for c in range(2):
        for h in range(2):
            p = 2 * h + c
            up = gpk[c] if h else gab[c]
            down = gbe[c] if h else gpk[2 + c]
            lft = gpk[2 * h] if c else gle[h]
            rgt = gri[h] if c else gpk[2 * h + 1]
            avg_ref[p] = (2.0 * gpk[p] + up + down + lft + rgt) * (1.0 / 6.0)


def split(x):
    hi = x.astype(BF16)
    return hi, (x - hi.astype(F32)).astype(BF16)


def product(a, b):
    (ah, al), (bh, bl) = a, b
    return (
        jnp.dot(ah, bh, preferred_element_type=F32)
        + jnp.dot(ah, bl, preferred_element_type=F32)
        + jnp.dot(al, bh, preferred_element_type=F32)
    )


def analysis_kernel(anom_ref, cen_ref, avg_ref, wt_ref, out_ref, yh, yl, zh, zl):
    row = lax.broadcasted_iota(jnp.int32, (256, 256), 0)
    col = lax.broadcasted_iota(jnp.int32, (256, 256), 1)
    diagonal = row == col
    identity = jnp.where(diagonal, 1.0, 0.0)
    low = row[:128, :128] >= col[:128, :128]
    on = row[:128, :128] == col[:128, :128]

    def coefs(low_end, plain):
        alpha2 = jnp.where(plain, 1.0, 3.0 / (1.0 + low_end + low_end * low_end))
        alpha = jnp.sqrt(alpha2)
        reach = alpha * low_end
        after = 0.5 * reach * (3.0 - reach * reach)
        return 1.5 * alpha, 0.5 * alpha * alpha2, jnp.minimum(after, 1.0)

    ends, plains, scales = [], [], []
    for p in range(4):
        packed = avg_ref[p]
        upper_right = packed[0:128]
        both = packed[128:256]
        turned = both.T
        first = jnp.where(low, both, turned)
        last = jnp.where(on, jnp.broadcast_to(packed[256:257], (128, 128)), jnp.where(low, turned, both))
        averaged = jnp.concatenate(
            [
                jnp.concatenate([first, upper_right], axis=1),
                jnp.concatenate([upper_right.T, last], axis=1),
            ],
            axis=0,
        )
        system = identity + wt_ref[p, 0:1, 0:1] * averaged
        squares = jnp.sum(jnp.sum(system * system, axis=1, keepdims=True), axis=0, keepdims=True)
        norm = jnp.sqrt(squares)
        rows = jnp.max(
            jnp.sum(jnp.abs(system), axis=0, keepdims=True), axis=1, keepdims=True
        )
        plain = norm > PLAIN_NORM
        scale = jnp.where(plain, norm, jnp.minimum(norm, rows * 1.000001))
        start = system / scale
        low_end = jnp.where(plain, 0.0, jnp.sqrt(1.0 / scale) * 0.9999)
        a, b, after = coefs(low_end, plain)
        factor = a * identity - b * start
        y = product(split(start), split(factor))
        yh[p], yl[p] = split(y)
        zh[p], zl[p] = split(factor)
        ends.append(after)
        plains.append(plain)
        scales.append(scale)

    def some_left(ends, plains, k):
        left = jnp.zeros((1, 1), F32)
        for end, plain in zip(ends, plains):
            _, _, after = coefs(end, plain)
            todo = jnp.where(plain, jnp.where(k + 1 < NS_ITERS, 1.0, 0.0), jnp.where(1.0 - after > CONVERGED, 1.0, 0.0))
            left = jnp.maximum(left, todo)
        return jnp.max(left) > 0.5

    def body(carry):
        k, _, *ends = carry
        following = []
        for p in range(4):
            a, b, after = coefs(ends[p], plains[p])
            y = (yh[p], yl[p])
            z = (zh[p], zl[p])
            factor = split(a * identity - b * product(z, y))
            ny = product(y, factor)
            nz = product(factor, z)
            yh[p], yl[p] = split(ny)
            zh[p], zl[p] = split(nz)
            following.append(after)
        return (k + 1, some_left(following, plains, k + 1), *following)

    last_k, _, *ends = lax.while_loop(
        lambda carry: carry[1], body, (1, some_left(ends, plains, 1), *ends)
    )
    for p in range(4):
        a, b, _ = coefs(ends[p], plains[p])
        z = (zh[p], zl[p])
        factor = split(a * identity - b * product(z, (yh[p], yl[p])))
        inverse = product(factor, z)
        weights = (inverse / jnp.sqrt(scales[p])).astype(BF16)
        a = anom_ref[p].reshape(512, 256)
        update = jnp.dot(a, weights, preferred_element_type=F32)
        centre = cen_ref[p].reshape(512, 128)
        centre = jnp.concatenate([centre, centre], axis=1)
        h, c = p // 2, p % 2
        out_ref[8 * h : 8 * h + 8, 64 * c : 64 * c + 64, :] = (
            (centre + update).astype(BF16).reshape(8, 64, 256)
        )


def return_kernel(
    rings,
    f_ref,
    coef_ref,
    wt_ref,
    out_ref,
    g,
    west,
    east,
    from_above,
    from_below,
    from_left,
    from_right,
    snd,
    rcv,
    edge_send,
    edge_recv,
    main_send,
    main_recv,
    own_sem,
):
    ring, half, mem, slot = place()
    above = lax.rem(ring + rings - 1, rings)
    below = lax.rem(ring + 1, rings)
    left = lax.rem(slot + 7, 8)
    right = lax.rem(slot + 1, 8)
    barrier = pltpu.get_barrier_semaphore()
    loop(1, 8, lambda j: signal(barrier, ring, lax.rem(slot + j, 8)))
    signal(barrier, above, slot)
    signal(barrier, below, slot)

    def widen(x):
        plane = f_ref[x].astype(F32)
        for mh in range(2):
            g[mh, x + 1, 1:17] = plane[:, mh * 128 : mh * 128 + 128].reshape(16, 8, 128)

    loop(0, 16, widen)
    for mh in range(2):
        lanes = slice(mh * 128, mh * 128 + 128)
        west[:, lanes] = g[mh, 1:17, 1].reshape(128, 128).astype(BF16)
        east[:, lanes] = g[mh, 1:17, 16].reshape(128, 128).astype(BF16)
    pl.semaphore_wait(barrier, 9)
    edges = [
        remote(f_ref.at[0], from_below, edge_send.at[0], edge_recv.at[0], above, slot),
        remote(f_ref.at[15], from_above, edge_send.at[1], edge_recv.at[1], below, slot),
        remote(west, from_right, edge_send.at[2], edge_recv.at[2], ring, left),
        remote(east, from_left, edge_send.at[3], edge_recv.at[3], ring, right),
    ]
    for copy in edges:
        copy.start()
    for copy in edges:
        copy.wait()
    for mh in range(2):
        lanes = slice(mh * 128, mh * 128 + 128)
        g[mh, 0, 1:17] = from_above[:, lanes].astype(F32).reshape(16, 8, 128)
        g[mh, 17, 1:17] = from_below[:, lanes].astype(F32).reshape(16, 8, 128)
        g[mh, 1:17, 0] = from_left[:, lanes].astype(F32).reshape(16, 8, 128)
        g[mh, 1:17, 17] = from_right[:, lanes].astype(F32).reshape(16, 8, 128)
    sx = wt_ref[4][None]
    sy = wt_ref[5][None]
    low = lax.broadcasted_iota(jnp.int32, (128, 128), 1) < 64

    def main_copy(pair, to):
        return remote(
            snd.at[pair, to], rcv.at[pair, slot], main_send.at[pair, to],
            main_recv.at[pair, slot], ring, to,
        )

    def own_copy(pair):
        return pltpu.make_async_copy(snd.at[pair, slot], rcv.at[pair, slot], own_sem.at[pair])

    def send_pair(pair):
        for h in range(2):
            x = 8 * h + 2 * pair + 1
            for mh in range(2):
                even, odd = [
                    stencil(
                        g[mh, x + k, 1:17], g[mh, x + k - 1, 1:17], g[mh, x + k + 1, 1:17],
                        g[mh, x + k, 0:16], g[mh, x + k, 2:18], coef_ref[x + k - 1], sx, sy,
                    ).reshape(128, 128)
                    for k in range(2)
                ]
                snd[pair, 4 * h + 2 * mh] = jnp.where(low, even, pltpu.roll(odd, 64, 1)).astype(BF16)
                snd[pair, 4 * h + 2 * mh + 1] = jnp.where(low, pltpu.roll(even, 64, 1), odd).astype(BF16)
        loop(1, 8, lambda j: main_copy(pair, lax.rem(slot + j, 8)).start())
        own_copy(pair).start()

    loop(0, 4, send_pair)

    row = lax.broadcasted_iota(jnp.int32, (1024, 128), 0)
    lane = lax.broadcasted_iota(jnp.int32, (1024, 128), 1)
    same = row // 8 == lane
    level = lax.rem(row, 8)
    pick = jnp.concatenate(
        [jnp.where(same & (level == f), 1.0, 0.0).astype(BF16) for f in range(8)], axis=1
    )

    def receive_pair(pair):
        own_copy(pair).wait()

        def wait(j):
            frm = lax.rem(slot + j, 8)
            remote(
                snd.at[pair, frm], rcv.at[pair, frm], main_send.at[pair, frm],
                main_recv.at[pair, frm], ring, frm,
            ).wait_recv()

        loop(1, 8, wait)
        block = rcv[pair].reshape(1024, 128)
        result = lax.dot_general(block, pick, TN, preferred_element_type=F32).astype(BF16)
        out_ref[2 * pair] = result[:64]
        out_ref[2 * pair + 1] = result[64:]

    loop(0, 4, receive_pair)

    def finish(pair):
        loop(1, 8, lambda j: main_copy(pair, lax.rem(slot + j, 8)).wait_send())

    loop(0, 4, finish)


def vmem(count):
    return [pl.BlockSpec(memory_space=pltpu.VMEM)] * count


def local(member_collection, spreading_ratio, transport_ratio_row, transport_ratio_column, obs_patch):
    rings = lax.axis_size("tile") // 2
    DMA = pltpu.SemaphoreType.DMA
    obs = obs_patch.reshape(1, 256)

    def shape(dims, dtype=F32):
        return jax.ShapeDtypeStruct(dims, dtype)

    anom, cen, avg, wt, coef = pl.pallas_call(
        lambda *refs: forecast_kernel(rings, *refs),
        out_shape=[
            shape((4, 8, 64, 256), BF16),
            shape((4, 8, 64, 128)),
            shape((4, 264, 128)),
            shape((6, 8, 128)),
            shape((16, 16, 8, 128)),
        ],
        in_specs=[pl.BlockSpec(memory_space=pltpu.HBM)] * 5,
        out_specs=vmem(5),
        scratch_shapes=[
            pltpu.VMEM((64, 8, 8, 128), BF16),
            pltpu.VMEM((8, 8, 128), F32),
            pltpu.SMEM((8,), F32),
            pltpu.SMEM((8,), F32),
            pltpu.VMEM((1, 256), jnp.int32),
            pltpu.VMEM((512, 1024), BF16),
            pltpu.VMEM((8, 160, 1024), BF16),
            pltpu.VMEM((8, 4, 160, 128), BF16),
            pltpu.VMEM((10, 4, 160, 128), BF16),
            pltpu.VMEM((2, 20, 20, 8, 128), F32),
            pltpu.VMEM((2, 18, 18, 8, 128), F32),
            pltpu.VMEM((20, 20, 8, 128), F32),
            pltpu.VMEM((32, 8, 128), F32),
            pltpu.VMEM((rings, 8, 128), F32),
            pltpu.VMEM((rings, 8, 128), F32),
            pltpu.VMEM((8, 8, 128), F32),
            pltpu.VMEM((4, 264, 128), F32),
            pltpu.VMEM((2, 264, 128), F32),
            pltpu.VMEM((2, 264, 128), F32),
            pltpu.VMEM((2, 264, 128), F32),
            pltpu.VMEM((2, 264, 128), F32),
            DMA((5,)),
            DMA((8,)),
            DMA((8,)),
            DMA((8,)),
            DMA((8,)),
            DMA((2,)),
            DMA((2,)),
            DMA((3,)),
            DMA((3,)),
            DMA((rings,)),
            DMA((rings,)),
            DMA((8,)),
            DMA((8,)),
            DMA((8,)),
            DMA((8,)),
        ],
        compiler_params=pltpu.CompilerParams(
            collective_id=0, has_side_effects=True, vmem_limit_bytes=VMEM_LIMIT
        ),
    )(member_collection, spreading_ratio, transport_ratio_row, transport_ratio_column, obs)

    field = pl.pallas_call(
        analysis_kernel,
        out_shape=shape((16, 128, 256), BF16),
        in_specs=vmem(4),
        out_specs=pl.BlockSpec(memory_space=pltpu.VMEM),
        scratch_shapes=[pltpu.VMEM((4, 256, 256), BF16)] * 4,
        compiler_params=pltpu.CompilerParams(vmem_limit_bytes=VMEM_LIMIT),
    )(anom, cen, avg, wt)

    out = pl.pallas_call(
        lambda *refs: return_kernel(rings, *refs),
        out_shape=shape((8, 64, 1024), BF16),
        in_specs=vmem(3),
        out_specs=pl.BlockSpec(memory_space=pltpu.VMEM),
        scratch_shapes=[
            pltpu.VMEM((2, 18, 18, 8, 128), F32),
            pltpu.VMEM((128, 256), BF16),
            pltpu.VMEM((128, 256), BF16),
            pltpu.VMEM((128, 256), BF16),
            pltpu.VMEM((128, 256), BF16),
            pltpu.VMEM((128, 256), BF16),
            pltpu.VMEM((128, 256), BF16),
            pltpu.VMEM((4, 8, 128, 128), BF16),
            pltpu.VMEM((4, 8, 128, 128), BF16),
            DMA((4,)),
            DMA((4,)),
            DMA((4, 8)),
            DMA((4, 8)),
            DMA((4,)),
        ],
        compiler_params=pltpu.CompilerParams(
            collective_id=1, has_side_effects=True, vmem_limit_bytes=VMEM_LIMIT
        ),
    )(field, coef, wt)
    return jnp.transpose(out.reshape(8, 64, 8, 128), (1, 2, 0, 3))


def solution(mesh):
    placed = (P("mem", None, "tile", None), P(None, "tile", None), P(), P(), P(("mem", "tile")))
    return jax.shard_map(
        local, mesh=mesh, in_specs=placed, out_specs=P("mem", None, "tile", None), check_vma=False
    )
```

```python
import jax
import jax.numpy as jnp
from jax import lax
from jax.experimental import pallas as pl
from jax.experimental.pallas import tpu as pltpu
from jax.sharding import PartitionSpec as P

F32 = jnp.float32
BF16 = jnp.bfloat16
MESH = pl.DeviceIdType.MESH
VMEM_LIMIT = 50 * 1024 * 1024
NS_ITERS = 14
PLAIN_NORM = 2500.0
CONVERGED = 1e-5
NT = (((1,), (1,)), ((), ()))
TN = (((0,), (0,)), ((), ()))


def place():
    tile = lax.axis_index("tile")
    mem = lax.axis_index("mem")
    ring = tile // 2
    half = lax.rem(tile, 2)
    return ring, half, mem, half * 4 + mem


def target(ring, slot):
    return {"mem": lax.rem(slot, 4), "tile": 2 * ring + slot // 4}


def remote(src, dst, send_sem, recv_sem, ring, slot):
    return pltpu.make_async_remote_copy(
        src_ref=src,
        dst_ref=dst,
        send_sem=send_sem,
        recv_sem=recv_sem,
        device_id=target(ring, slot),
        device_id_type=MESH,
    )


def signal(sem, ring, slot):
    pl.semaphore_signal(sem, inc=1, device_id=target(ring, slot), device_id_type=MESH)


def stencil(c, bx, ax, by, ay, s, sx, sy):
    return c - sx * (c - bx) - sy * (c - by) + s * (ax + bx + ay + by - 4.0 * c)


def rounded(x):
    return x.astype(BF16).astype(F32)


def loop(lower, upper, body):
    def step(i, carry):
        body(i)
        return carry

    lax.fori_loop(lower, upper, step, 0)


def forecast_kernel(
    rings,
    u_hbm,
    spread_hbm,
    sx_hbm,
    sy_hbm,
    obs_hbm,
    anom_ref,
    cen_ref,
    avg_ref,
    wt_ref,
    coef_ref,
    raw,
    spread_in,
    sx_in,
    sy_in,
    obs_in,
    flat,
    state,
    pick,
    wide,
    rcv,
    u0,
    u1,
    coef,
    spr,
    cst,
    cra,
    crb,
    gpk,
    gab,
    gbe,
    gle,
    gri,
    load_sem,
    edge_send,
    edge_recv,
    rest_send,
    rest_recv,
    halo_send,
    halo_recv,
    spr_send,
    spr_recv,
    cnt_send,
    cnt_recv,
    sum_send,
    sum_recv,
    gram_send,
    gram_recv,
):
    ring, half, mem, slot = place()
    above = lax.rem(ring + rings - 1, rings)
    below = lax.rem(ring + 1, rings)

    barrier = pltpu.get_barrier_semaphore()
    loop(1, 8, lambda j: signal(barrier, ring, lax.rem(slot + j, 8)))
    loop(1, rings, lambda j: signal(barrier, lax.rem(ring + j, rings), slot))
    loads = [
        pltpu.make_async_copy(src, dst, load_sem.at[k])
        for k, (src, dst) in enumerate(
            [
                (u_hbm, raw), (spread_hbm, spread_in), (sx_hbm, sx_in), (sy_hbm, sy_in),
                (obs_hbm, obs_in),
            ]
        )
    ]
    for copy in loads:
        copy.start()

    def pick_rows(i):
        row = lax.broadcasted_iota(jnp.int32, (128, 128), 0) + 128 * i
        lane = lax.broadcasted_iota(jnp.int32, (128, 128), 1)
        level = jnp.where(row // 8 == lane, lax.rem(row, 8), 8)
        rows = pl.ds(pl.multiple_of(128 * i, 128), 128)
        for f in range(8):
            pick[rows, f * 128 : f * 128 + 128] = jnp.where(level == f, 1.0, 0.0).astype(BF16)

    loop(0, 8, pick_rows)

    edge_pair = 3 * half
    rest_pair = 1 - half

    def turned(first, count):
        k = lax.broadcasted_iota(jnp.int32, (128 * count, 512), 1)
        r = lax.broadcasted_iota(jnp.int32, (128 * count, 512), 0) + 128 * first
        turn = jnp.where(k == lax.rem(r, 64) * 8 + r // 64, 1.0, 0.0).astype(BF16)
        return jnp.dot(turn, flat[...], preferred_element_type=F32).astype(BF16)

    def store_pair(pair, block):
        wide[pair, 16:1040] = block
        wide[pair, 0:16] = block[1008:1024]
        wide[pair, 1040:1056] = block[0:16]

    loads[0].wait()
    for f in range(8):
        flat[:, f * 128 : f * 128 + 128] = raw[:, f].astype(F32).reshape(512, 128).astype(BF16)
    state[0:128] = turned(edge_pair, 1)
    store_pair(
        edge_pair,
        lax.dot_general(pick[...], state[0:128], NT, preferred_element_type=F32).astype(BF16),
    )

    def edge_copy(to):
        return remote(
            wide.at[edge_pair, pl.ds(pl.multiple_of(128 * to, 128), 160)],
            rcv.at[1 + 7 * half, mem], edge_send.at[to], edge_recv.at[slot], ring, to,
        )

    def rest_copy(to):
        return remote(
            wide.at[pl.ds(rest_pair, 3), pl.ds(pl.multiple_of(128 * to, 128), 160)],
            rcv.at[pl.ds(2 + 3 * half, 3), mem], rest_send.at[to], rest_recv.at[slot], ring, to,
        )

    pl.semaphore_wait(barrier, 7 + rings - 1)
    loop(1, 8, lambda j: edge_copy(lax.rem(slot + j, 8)).start())
    own_rows = pl.ds(pl.multiple_of(128 * slot, 128), 160)
    own_edge = pltpu.make_async_copy(
        wide.at[edge_pair, own_rows], rcv.at[1 + 7 * half, mem], edge_recv.at[slot]
    )
    own_edge.start()
    state[128:512] = turned(rest_pair, 3)

    def rest_rows(i):
        rows = pl.ds(pl.multiple_of(128 * i, 128), 128)
        block = lax.dot_general(
            pick[rows, :], state[128:512], NT, preferred_element_type=F32
        ).astype(BF16)
        for pair in range(3):
            wide[rest_pair + pair, pl.ds(pl.multiple_of(128 * i + 16, 16), 128)] = block[
                :, pair * 128 : (pair + 1) * 128
            ]

    loop(0, 8, rest_rows)
    for pair in range(3):
        wide[rest_pair + pair, 0:16] = wide[rest_pair + pair, 1024:1040]
        wide[rest_pair + pair, 1040:1056] = wide[rest_pair + pair, 16:32]
    loop(1, 8, lambda j: rest_copy(lax.rem(slot + j, 8)).start())
    own_rest = pltpu.make_async_copy(
        wide.at[pl.ds(rest_pair, 3), own_rows], rcv.at[pl.ds(2 + 3 * half, 3), mem],
        rest_recv.at[slot],
    )
    own_rest.start()

    loads[1].wait()
    mine = 8 + 8 * half
    for x in range(8):
        spr[mine + x] = spread_in[:, x, :]
    spr_here = remote(
        spr.at[pl.ds(mine, 8)], spr.at[pl.ds(mine, 8)], spr_send.at[0], spr_recv.at[0],
        ring, (1 - half) * 4 + mem,
    )
    spr_here.start()

    own_edge.wait()

    def edge_wait(j):
        frm = lax.rem(slot + j, 8)
        remote(
            wide.at[0, 0:160], rcv.at[1 + 7 * (frm // 4), lax.rem(frm, 4)], edge_send.at[frm],
            edge_recv.at[frm], ring, frm,
        ).wait_recv()

    loop(1, 8, edge_wait)
    halos = [
        remote(rcv.at[1], rcv.at[9], halo_send.at[0], halo_recv.at[0], above, slot),
        remote(rcv.at[8], rcv.at[0], halo_send.at[1], halo_recv.at[1], below, slot),
    ]
    for copy in halos:
        copy.start()

    loads[4].wait()
    obs = obs_in[...]
    in_ring = lax.broadcasted_iota(jnp.int32, (rings, 256), 0) == obs // 32
    in_patch = lax.broadcasted_iota(jnp.int32, (128, 256), 0) == lax.rem(obs, 32)
    tally = lax.dot_general(
        in_ring.astype(F32).astype(BF16), in_patch.astype(F32).astype(BF16), NT,
        preferred_element_type=F32,
    )
    for r in range(rings):
        cst[r] = jnp.broadcast_to(tally[r : r + 1, :], (8, 128))
    cra[ring] = cst[ring]

    def count_copy(j):
        to = lax.rem(ring + j, rings)
        return remote(cst.at[to], cra.at[ring], cnt_send.at[j], cnt_recv.at[ring], to, slot)

    loop(1, rings, lambda j: count_copy(j).start())

    spr_here.wait_send()
    other = 16 - 8 * half
    remote(
        spr.at[pl.ds(other, 8)], spr.at[pl.ds(other, 8)], spr_send.at[0], spr_recv.at[0],
        ring, (1 - half) * 4 + mem,
    ).wait_recv()
    spr_far = [
        remote(spr.at[8:10], spr.at[24:26], spr_send.at[1], spr_recv.at[1], above, slot),
        remote(spr.at[22:24], spr.at[6:8], spr_send.at[2], spr_recv.at[2], below, slot),
    ]
    for copy in spr_far:
        copy.start()

    def spread_row(i):
        lane = lax.broadcasted_iota(jnp.int32, (20, 8, 128), 2)
        column = lax.rem(
            lax.broadcasted_iota(jnp.int32, (20, 8, 128), 0) + 16 * slot + 126, 128
        )
        values = jnp.where(lane == column, spr[i + 6][None], 0.0)
        coef[i] = jnp.broadcast_to(jnp.sum(values, axis=2, keepdims=True), (20, 8, 128))

    loop(2, 18, spread_row)

    def coef_row(i):
        coef_ref[i] = coef[i + 2, 2:18]

    loop(0, 16, coef_row)
    for copy in spr_far:
        copy.wait()
    for i in (0, 1, 18, 19):
        spread_row(i)
    loads[2].wait()
    loads[3].wait()
    sublane = lax.broadcasted_iota(jnp.int32, (8, 128), 0)
    for k, ref in enumerate((sx_in, sy_in)):
        speed = jnp.zeros((8, 128), F32)
        for f in range(8):
            speed = jnp.where(sublane == f, ref[f], speed)
        wt_ref[4 + k] = speed

    def unshuffle(pair):
        low = lax.broadcasted_iota(jnp.int32, (160, 128), 1) < 64
        for mh in range(2):
            r0 = rcv[pair, 2 * mh].astype(F32)
            r1 = rcv[pair, 2 * mh + 1].astype(F32)
            even = jnp.where(low, r0, pltpu.roll(r1, 64, 1))
            odd = jnp.where(low, pltpu.roll(r0, 64, 1), r1)
            u0[mh, 2 * pair] = even.reshape(20, 8, 128)
            u0[mh, 2 * pair + 1] = odd.reshape(20, 8, 128)

    unshuffle(1)
    unshuffle(8)
    for copy in halos:
        copy.wait()
    unshuffle(0)
    unshuffle(9)

    own_rest.wait()

    def rest_wait(j):
        frm = lax.rem(slot + j, 8)
        remote(
            wide.at[0:3, 0:160], rcv.at[pl.ds(2 + 3 * (frm // 4), 3), lax.rem(frm, 4)],
            rest_send.at[frm], rest_recv.at[frm], ring, frm,
        ).wait_recv()

    loop(1, 8, rest_wait)
    loop(2, 8, unshuffle)
    sx = wt_ref[4][None]
    sy = wt_ref[5][None]

    def first(x):
        s = coef[x, 1:19]
        for mh in range(2):
            u1[mh, x - 1] = rounded(
                stencil(
                    u0[mh, x, 1:19], u0[mh, x - 1, 1:19], u0[mh, x + 1, 1:19],
                    u0[mh, x, 0:18], u0[mh, x, 2:20], s, sx, sy,
                )
            )

    loop(1, 19, first)

    def count_wait(j):
        frm = lax.rem(ring + j, rings)
        remote(cst.at[0], cra.at[frm], cnt_send.at[j], cnt_recv.at[frm], frm, slot).wait_recv()

    loop(1, rings, count_wait)
    total = cra[0]
    for r in range(1, rings):
        total = total + cra[r]
    crb[slot] = total

    def sum_copy(j):
        return remote(
            crb.at[slot], crb.at[slot], sum_send.at[j], sum_recv.at[slot], ring,
            lax.rem(slot + j, 8),
        )

    loop(1, 8, lambda j: sum_copy(j).start())

    row = lax.broadcasted_iota(jnp.int32, (128, 128), 0)
    col = lax.broadcasted_iota(jnp.int32, (128, 128), 1)
    left = lax.rem(slot + 7, 8)
    right = lax.rem(slot + 1, 8)
    copies = []
    for c in range(2):
        for h in range(2):
            p = 2 * h + c

            def second(i, h=h, c=c, p=p):
                x = 8 * h + i + 1
                y = 8 * c + 1
                s = coef[x + 1, y + 1 : y + 9]
                prior = [
                    rounded(
                        stencil(
                            u1[mh, x, y : y + 8], u1[mh, x - 1, y : y + 8],
                            u1[mh, x + 1, y : y + 8], u1[mh, x, y - 1 : y + 7],
                            u1[mh, x, y + 1 : y + 9], s, sx, sy,
                        )
                    )
                    for mh in range(2)
                ]
                centre = jnp.sum(prior[0] + prior[1], axis=2, keepdims=True) * (1.0 / 256.0)
                centre = jnp.broadcast_to(centre, (8, 8, 128))
                cen_ref[p, i] = centre.reshape(64, 128)
                for mh in range(2):
                    anom_ref[p, i, :, mh * 128 : mh * 128 + 128] = (
                        (prior[mh] - centre).reshape(64, 128).astype(BF16)
                    )

            loop(0, 8, second)
            a = anom_ref[p].reshape(512, 256)
            g = lax.dot_general(a, a, TN, preferred_element_type=F32) * (1.0 / 512.0)
            last = g[128:, 128:]
            gpk[p, 0:128] = g[:128, 128:]
            gpk[p, 128:256] = jnp.where(row >= col, g[:128, :128], last)
            diag = jnp.sum(jnp.where(row == col, last, 0.0), axis=0, keepdims=True)
            gpk[p, 256:264] = jnp.broadcast_to(diag, (8, 128))
            vertical = (gab, below) if h else (gbe, above)
            sideways = (gle, right) if c else (gri, left)
            pair = [
                remote(
                    gpk.at[p], vertical[0].at[c], gram_send.at[2 * p], gram_recv.at[2 * p],
                    vertical[1], slot,
                ),
                remote(
                    gpk.at[p], sideways[0].at[h], gram_send.at[2 * p + 1],
                    gram_recv.at[2 * p + 1], ring, sideways[1],
                ),
            ]
            for copy in pair:
                copy.start()
            copies += pair

    def sum_wait(j):
        frm = lax.rem(slot + j, 8)
        remote(crb.at[slot], crb.at[frm], sum_send.at[j], sum_recv.at[frm], ring, frm).wait_recv()

    loop(1, 8, sum_wait)
    counts = crb[0]
    for k in range(1, 8):
        counts = counts + crb[k]
    lane = lax.broadcasted_iota(jnp.int32, (8, 128), 1)
    for h in range(2):
        for c in range(2):
            chosen = jnp.where(lane == h * 16 + 2 * slot + c, counts, 0.0)
            count = jnp.sum(chosen, axis=1, keepdims=True)
            wt_ref[2 * h + c] = jnp.broadcast_to(count / (count + 16.0), (8, 128))
    loop(1, rings, lambda j: count_copy(j).wait_send())
    loop(1, 8, lambda j: sum_copy(j).wait_send())
    loop(1, 8, lambda j: edge_copy(lax.rem(slot + j, 8)).wait_send())
    loop(1, 8, lambda j: rest_copy(lax.rem(slot + j, 8)).wait_send())
    for copy in copies:
        copy.wait()
    for c in range(2):
        for h in range(2):
            p = 2 * h + c
            up = gpk[c] if h else gab[c]
            down = gbe[c] if h else gpk[2 + c]
            lft = gpk[2 * h] if c else gle[h]
            rgt = gri[h] if c else gpk[2 * h + 1]
            avg_ref[p] = (2.0 * gpk[p] + up + down + lft + rgt) * (1.0 / 6.0)


def split(x):
    hi = x.astype(BF16)
    return hi, (x - hi.astype(F32)).astype(BF16)


def product(a, b):
    (ah, al), (bh, bl) = a, b
    return (
        jnp.dot(ah, bh, preferred_element_type=F32)
        + jnp.dot(ah, bl, preferred_element_type=F32)
        + jnp.dot(al, bh, preferred_element_type=F32)
    )


def analysis_kernel(anom_ref, cen_ref, avg_ref, wt_ref, out_ref, yh, yl, zh, zl, fh, fl):
    row = lax.broadcasted_iota(jnp.int32, (256, 256), 0)
    col = lax.broadcasted_iota(jnp.int32, (256, 256), 1)
    diagonal = row == col
    identity = jnp.where(diagonal, 1.0, 0.0)
    low = row[:128, :128] >= col[:128, :128]
    on = row[:128, :128] == col[:128, :128]

    def coefs(low_end, plain):
        alpha2 = jnp.where(plain, 1.0, 3.0 / (1.0 + low_end + low_end * low_end))
        alpha = jnp.sqrt(alpha2)
        reach = alpha * low_end
        after = 0.5 * reach * (3.0 - reach * reach)
        return 1.5 * alpha, 0.5 * alpha * alpha2, jnp.minimum(after, 1.0)

    ends, plains, scales = [], [], []
    for p in range(4):
        packed = avg_ref[p]
        upper_right = packed[0:128]
        both = packed[128:256]
        turned = both.T
        first = jnp.where(low, both, turned)
        last = jnp.where(on, jnp.broadcast_to(packed[256:257], (128, 128)), jnp.where(low, turned, both))
        averaged = jnp.concatenate(
            [
                jnp.concatenate([first, upper_right], axis=1),
                jnp.concatenate([upper_right.T, last], axis=1),
            ],
            axis=0,
        )
        system = identity + wt_ref[p, 0:1, 0:1] * averaged
        squares = jnp.sum(jnp.sum(system * system, axis=1, keepdims=True), axis=0, keepdims=True)
        norm = jnp.sqrt(squares)
        rows = jnp.max(
            jnp.sum(jnp.abs(system), axis=0, keepdims=True), axis=1, keepdims=True
        )
        plain = norm > PLAIN_NORM
        scale = jnp.where(plain, norm, jnp.minimum(norm, rows * 1.000001))
        start = system / scale
        low_end = jnp.where(plain, 0.0, jnp.sqrt(1.0 / scale) * 0.9999)
        a, b, after = coefs(low_end, plain)
        factor = a * identity - b * start
        y = product(split(start), split(factor))
        yh[p], yl[p] = split(y)
        zh[p], zl[p] = split(factor)
        ends.append(after)
        plains.append(plain)
        scales.append(scale)

    def some_left(ends, plains, k):
        left = jnp.zeros((1, 1), F32)
        for end, plain in zip(ends, plains):
            _, _, after = coefs(end, plain)
            todo = jnp.where(plain, jnp.where(k + 1 < NS_ITERS, 1.0, 0.0), jnp.where(1.0 - after > CONVERGED, 1.0, 0.0))
            left = jnp.maximum(left, todo)
        return jnp.max(left) > 0.5

    def body(carry):
        k, _, *ends = carry
        following = []
        for p in range(4):
            a, b, after = coefs(ends[p], plains[p])
            t = product((zh[p], zl[p]), (yh[p], yl[p]))
            fh[p], fl[p] = split(a * identity - b * t)
            following.append(after)
        for p in range(4):
            factor = (fh[p], fl[p])
            ny = product((yh[p], yl[p]), factor)
            nz = product(factor, (zh[p], zl[p]))
            yh[p], yl[p] = split(ny)
            zh[p], zl[p] = split(nz)
        return (k + 1, some_left(following, plains, k + 1), *following)

    last_k, _, *ends = lax.while_loop(
        lambda carry: carry[1], body, (1, some_left(ends, plains, 1), *ends)
    )
    for p in range(4):
        a, b, _ = coefs(ends[p], plains[p])
        fh[p], fl[p] = split(a * identity - b * product((zh[p], zl[p]), (yh[p], yl[p])))
    for p in range(4):
        _, _, after = coefs(ends[p], plains[p])
        inverse = product((fh[p], fl[p]), (zh[p], zl[p]))
        middle = jnp.where(plains[p], 1.0, 0.5 + 0.5 * after)
        weights = (inverse / (middle * jnp.sqrt(scales[p]))).astype(BF16)
        a = anom_ref[p].reshape(512, 256)
        update = jnp.dot(a, weights, preferred_element_type=F32)
        centre = cen_ref[p].reshape(512, 128)
        centre = jnp.concatenate([centre, centre], axis=1)
        h, c = p // 2, p % 2
        out_ref[8 * h : 8 * h + 8, 64 * c : 64 * c + 64, :] = (
            (centre + update).astype(BF16).reshape(8, 64, 256)
        )


def return_kernel(
    rings,
    f_ref,
    coef_ref,
    wt_ref,
    out_ref,
    g,
    west,
    east,
    from_above,
    from_below,
    from_left,
    from_right,
    snd,
    rcv,
    pick,
    edge_send,
    edge_recv,
    main_send,
    main_recv,
    own_sem,
):
    ring, half, mem, slot = place()
    above = lax.rem(ring + rings - 1, rings)
    below = lax.rem(ring + 1, rings)
    left = lax.rem(slot + 7, 8)
    right = lax.rem(slot + 1, 8)
    barrier = pltpu.get_barrier_semaphore()
    loop(1, 8, lambda j: signal(barrier, ring, lax.rem(slot + j, 8)))
    signal(barrier, above, slot)
    signal(barrier, below, slot)

    def widen(x):
        plane = f_ref[x].astype(F32)
        for mh in range(2):
            g[mh, x + 1, 1:17] = plane[:, mh * 128 : mh * 128 + 128].reshape(16, 8, 128)

    loop(0, 16, widen)
    for mh in range(2):
        lanes = slice(mh * 128, mh * 128 + 128)
        west[:, lanes] = g[mh, 1:17, 1].reshape(128, 128).astype(BF16)
        east[:, lanes] = g[mh, 1:17, 16].reshape(128, 128).astype(BF16)
    pl.semaphore_wait(barrier, 9)
    edges = [
        remote(f_ref.at[0], from_below, edge_send.at[0], edge_recv.at[0], above, slot),
        remote(f_ref.at[15], from_above, edge_send.at[1], edge_recv.at[1], below, slot),
        remote(west, from_right, edge_send.at[2], edge_recv.at[2], ring, left),
        remote(east, from_left, edge_send.at[3], edge_recv.at[3], ring, right),
    ]
    for copy in edges:
        copy.start()
    sx = wt_ref[4][None]
    sy = wt_ref[5][None]

    def step_pair(h, pair, y0, y1):
        x = 8 * h + 2 * pair + 1
        rows = slice(8 * y0, 8 * y1)
        low = lax.broadcasted_iota(jnp.int32, (8 * (y1 - y0), 128), 1) < 64
        here, behind, ahead = slice(y0 + 1, y1 + 1), slice(y0, y1), slice(y0 + 2, y1 + 2)
        for mh in range(2):
            even, odd = [
                stencil(
                    g[mh, x + k, here], g[mh, x + k - 1, here], g[mh, x + k + 1, here],
                    g[mh, x + k, behind], g[mh, x + k, ahead], coef_ref[x + k - 1, y0:y1], sx, sy,
                ).reshape(8 * (y1 - y0), 128)
                for k in range(2)
            ]
            to = 4 * h + 2 * mh
            snd[to, pair, rows] = jnp.where(low, even, pltpu.roll(odd, 64, 1)).astype(BF16)
            snd[to + 1, pair, rows] = jnp.where(low, pltpu.roll(even, 64, 1), odd).astype(BF16)

    def parts(half_of):
        inner = pl.ds(1 - half_of, 3)
        return [
            (inner, slice(16, 112)), (3 * half_of, slice(0, 128)), (inner, slice(0, 16)),
            (inner, slice(112, 128)),
        ]

    def main_copy(part, to):
        pairs, rows = parts(to // 4)[part]
        return remote(
            snd.at[to, pairs, rows], rcv.at[slot, pairs, rows], main_send.at[part, to],
            main_recv.at[part, slot], ring, to,
        )

    def send(part):
        loop(1, 8, lambda j: main_copy(part, lax.rem(slot + j, 8)).start())

    for h in range(2):
        loop(1 - h, 4 - h, lambda pair, h=h: step_pair(h, pair, 2, 14))
    send(0)
    for copy in edges:
        copy.wait()
    for mh in range(2):
        lanes = slice(mh * 128, mh * 128 + 128)
        g[mh, 0, 1:17] = from_above[:, lanes].astype(F32).reshape(16, 8, 128)
        g[mh, 17, 1:17] = from_below[:, lanes].astype(F32).reshape(16, 8, 128)
        g[mh, 1:17, 0] = from_left[:, lanes].astype(F32).reshape(16, 8, 128)
        g[mh, 1:17, 17] = from_right[:, lanes].astype(F32).reshape(16, 8, 128)
    for h in range(2):
        step_pair(h, 3 * h, 0, 16)
    send(1)
    for y0 in (0, 14):
        for h in range(2):
            loop(1 - h, 4 - h, lambda pair, h=h, y0=y0: step_pair(h, pair, y0, y0 + 2))
    send(2)
    send(3)
    own = pltpu.make_async_copy(snd.at[slot], rcv.at[slot], own_sem)
    own.start()

    def pick_rows(i):
        row = lax.broadcasted_iota(jnp.int32, (128, 128), 0) + 128 * i
        lane = lax.broadcasted_iota(jnp.int32, (128, 128), 1)
        level = jnp.where(row // 8 == lane, lax.rem(row, 8), 8)
        rows = pl.ds(pl.multiple_of(128 * i, 128), 128)
        for f in range(8):
            pick[rows, f * 128 : f * 128 + 128] = jnp.where(level == f, 1.0, 0.0).astype(BF16)

    loop(0, 8, pick_rows)
    own.wait()
    for part in range(4):

        def wait(j, part=part):
            frm = lax.rem(slot + j, 8)
            pairs, rows = parts(half)[part]
            remote(
                snd.at[frm, pairs, rows], rcv.at[frm, pairs, rows], main_send.at[part, frm],
                main_recv.at[part, frm], ring, frm,
            ).wait_recv()

        loop(1, 8, wait)

    def result_pair(pair):
        block = rcv[:, pair].reshape(1024, 128)
        result = lax.dot_general(block, pick[...], TN, preferred_element_type=F32).astype(BF16)
        out_ref[2 * pair] = result[:64]
        out_ref[2 * pair + 1] = result[64:]

    loop(0, 4, result_pair)
    for part in range(4):
        loop(1, 8, lambda j, part=part: main_copy(part, lax.rem(slot + j, 8)).wait_send())


def vmem(count):
    return [pl.BlockSpec(memory_space=pltpu.VMEM)] * count


def local(member_collection, spreading_ratio, transport_ratio_row, transport_ratio_column, obs_patch):
    rings = lax.axis_size("tile") // 2
    DMA = pltpu.SemaphoreType.DMA
    obs = obs_patch.reshape(1, 256)

    def shape(dims, dtype=F32):
        return jax.ShapeDtypeStruct(dims, dtype)

    anom, cen, avg, wt, coef = pl.pallas_call(
        lambda *refs: forecast_kernel(rings, *refs),
        out_shape=[
            shape((4, 8, 64, 256), BF16),
            shape((4, 8, 64, 128)),
            shape((4, 264, 128)),
            shape((6, 8, 128)),
            shape((16, 16, 8, 128)),
        ],
        in_specs=[pl.BlockSpec(memory_space=pltpu.HBM)] * 5,
        out_specs=vmem(5),
        scratch_shapes=[
            pltpu.VMEM((64, 8, 8, 128), BF16),
            pltpu.VMEM((8, 8, 128), F32),
            pltpu.SMEM((8,), F32),
            pltpu.SMEM((8,), F32),
            pltpu.VMEM((1, 256), jnp.int32),
            pltpu.VMEM((512, 1024), BF16),
            pltpu.VMEM((512, 1024), BF16),
            pltpu.VMEM((1024, 1024), BF16),
            pltpu.VMEM((4, 1056, 128), BF16),
            pltpu.VMEM((10, 4, 160, 128), BF16),
            pltpu.VMEM((2, 20, 20, 8, 128), F32),
            pltpu.VMEM((2, 18, 18, 8, 128), F32),
            pltpu.VMEM((20, 20, 8, 128), F32),
            pltpu.VMEM((32, 8, 128), F32),
            pltpu.VMEM((rings, 8, 128), F32),
            pltpu.VMEM((rings, 8, 128), F32),
            pltpu.VMEM((8, 8, 128), F32),
            pltpu.VMEM((4, 264, 128), F32),
            pltpu.VMEM((2, 264, 128), F32),
            pltpu.VMEM((2, 264, 128), F32),
            pltpu.VMEM((2, 264, 128), F32),
            pltpu.VMEM((2, 264, 128), F32),
            DMA((5,)),
            DMA((8,)),
            DMA((8,)),
            DMA((8,)),
            DMA((8,)),
            DMA((2,)),
            DMA((2,)),
            DMA((3,)),
            DMA((3,)),
            DMA((rings,)),
            DMA((rings,)),
            DMA((8,)),
            DMA((8,)),
            DMA((8,)),
            DMA((8,)),
        ],
        compiler_params=pltpu.CompilerParams(
            collective_id=0, has_side_effects=True, vmem_limit_bytes=VMEM_LIMIT
        ),
    )(member_collection, spreading_ratio, transport_ratio_row, transport_ratio_column, obs)

    field = pl.pallas_call(
        analysis_kernel,
        out_shape=shape((16, 128, 256), BF16),
        in_specs=vmem(4),
        out_specs=pl.BlockSpec(memory_space=pltpu.VMEM),
        scratch_shapes=[pltpu.VMEM((4, 256, 256), BF16)] * 6,
        compiler_params=pltpu.CompilerParams(vmem_limit_bytes=VMEM_LIMIT),
    )(anom, cen, avg, wt)

    out = pl.pallas_call(
        lambda *refs: return_kernel(rings, *refs),
        out_shape=shape((8, 64, 1024), BF16),
        in_specs=vmem(3),
        out_specs=pl.BlockSpec(memory_space=pltpu.VMEM),
        scratch_shapes=[
            pltpu.VMEM((2, 18, 18, 8, 128), F32),
            pltpu.VMEM((128, 256), BF16),
            pltpu.VMEM((128, 256), BF16),
            pltpu.VMEM((128, 256), BF16),
            pltpu.VMEM((128, 256), BF16),
            pltpu.VMEM((128, 256), BF16),
            pltpu.VMEM((128, 256), BF16),
            pltpu.VMEM((8, 4, 128, 128), BF16),
            pltpu.VMEM((8, 4, 128, 128), BF16),
            pltpu.VMEM((1024, 1024), BF16),
            DMA((4,)),
            DMA((4,)),
            DMA((4, 8)),
            DMA((4, 8)),
            DMA,
        ],
        compiler_params=pltpu.CompilerParams(
            collective_id=1, has_side_effects=True, vmem_limit_bytes=VMEM_LIMIT
        ),
    )(field, coef, wt)
    return jnp.transpose(out.reshape(8, 64, 8, 128), (1, 2, 0, 3))


def solution(mesh):
    placed = (P("mem", None, "tile", None), P(None, "tile", None), P(), P(), P(("mem", "tile")))
    return jax.shard_map(
        local, mesh=mesh, in_specs=placed, out_specs=P("mem", None, "tile", None), check_vma=False
    )
```

```python
import jax
import jax.numpy as jnp
from jax import lax
from jax.experimental import pallas as pl
from jax.experimental.pallas import tpu as pltpu
from jax.sharding import PartitionSpec as P

F32 = jnp.float32
BF16 = jnp.bfloat16
MESH = pl.DeviceIdType.MESH
VMEM_LIMIT = 50 * 1024 * 1024
NS_ITERS = 14
PLAIN_NORM = 2500.0
CONVERGED = 1e-5
NT = (((1,), (1,)), ((), ()))
TN = (((0,), (0,)), ((), ()))


def place():
    tile = lax.axis_index("tile")
    mem = lax.axis_index("mem")
    ring = tile // 2
    half = lax.rem(tile, 2)
    return ring, half, mem, half * 4 + mem


def target(ring, slot):
    return {"mem": lax.rem(slot, 4), "tile": 2 * ring + slot // 4}


def remote(src, dst, send_sem, recv_sem, ring, slot):
    return pltpu.make_async_remote_copy(
        src_ref=src,
        dst_ref=dst,
        send_sem=send_sem,
        recv_sem=recv_sem,
        device_id=target(ring, slot),
        device_id_type=MESH,
    )


def signal(sem, ring, slot):
    pl.semaphore_signal(sem, inc=1, device_id=target(ring, slot), device_id_type=MESH)


def stencil(c, bx, ax, by, ay, s, sx, sy):
    return c - sx * (c - bx) - sy * (c - by) + s * (ax + bx + ay + by - 4.0 * c)


def rounded(x):
    return x.astype(BF16).astype(F32)


def loop(lower, upper, body):
    def step(i, carry):
        body(i)
        return carry

    lax.fori_loop(lower, upper, step, 0)


def forecast_kernel(
    rings,
    u_hbm,
    spread_hbm,
    obs_hbm,
    sx_ref,
    sy_ref,
    anom_ref,
    cen_ref,
    avg_ref,
    wt_ref,
    coef_ref,
    raw,
    spread_in,
    obs_in,
    flat,
    state,
    pick,
    wide,
    rcv,
    u0,
    u1,
    coef,
    spr,
    cst,
    cra,
    crb,
    gpk,
    gab,
    gbe,
    gle,
    gri,
    load_sem,
    block_send,
    block_recv,
    halo_send,
    halo_recv,
    spr_send,
    spr_recv,
    cnt_send,
    cnt_recv,
    sum_send,
    sum_recv,
    gram_send,
    gram_recv,
):
    ring, half, mem, slot = place()
    above = lax.rem(ring + rings - 1, rings)
    below = lax.rem(ring + 1, rings)

    barrier = pltpu.get_barrier_semaphore()
    loop(1, 8, lambda j: signal(barrier, ring, lax.rem(slot + j, 8)))
    loop(1, rings, lambda j: signal(barrier, lax.rem(ring + j, rings), slot))
    load_raw = pltpu.make_async_copy(u_hbm, raw, load_sem.at[0])
    load_spread = pltpu.make_async_copy(spread_hbm, spread_in, load_sem.at[1])
    load_obs = pltpu.make_async_copy(obs_hbm, obs_in, load_sem.at[2])
    load_raw.start()
    load_spread.start()
    load_obs.start()

    def pick_rows(i):
        row = lax.broadcasted_iota(jnp.int32, (128, 128), 0) + 128 * i
        lane = lax.broadcasted_iota(jnp.int32, (128, 128), 1)
        level = jnp.where(row // 8 == lane, lax.rem(row, 8), 8)
        rows = pl.ds(pl.multiple_of(128 * i, 128), 128)
        for f in range(8):
            pick[rows, f * 128 : f * 128 + 128] = jnp.where(level == f, 1.0, 0.0).astype(BF16)

    loop(0, 8, pick_rows)

    load_raw.wait()
    for f in range(8):
        flat[:, f * 128 : f * 128 + 128] = raw[:, f].astype(F32).reshape(512, 128).astype(BF16)

    def pair_of(t, side):
        return t + side * (3 - 2 * t)

    def place_of(t, side):
        return 1 + 4 * side + pair_of(t, side)

    def turn_pair(t):
        pair = pair_of(t, half)
        k = lax.broadcasted_iota(jnp.int32, (128, 512), 1)
        r = lax.broadcasted_iota(jnp.int32, (128, 512), 0) + 128 * pair
        turn = jnp.where(k == lax.rem(r, 64) * 8 + r // 64, 1.0, 0.0).astype(BF16)
        state[...] = jnp.dot(turn, flat[...], preferred_element_type=F32).astype(BF16)
        block = lax.dot_general(
            pick[...], state[...], NT, preferred_element_type=F32
        ).astype(BF16)
        wide[pair, 16:1040] = block
        wide[pair, 0:16] = block[1008:1024]
        wide[pair, 1040:1056] = block[0:16]

    def block_copy(t, to):
        return remote(
            wide.at[pair_of(t, half), pl.ds(pl.multiple_of(128 * to, 128), 160)],
            rcv.at[place_of(t, half), mem], block_send.at[t, to], block_recv.at[t, slot], ring, to,
        )

    def own_copy(t):
        return pltpu.make_async_copy(
            wide.at[pair_of(t, half), pl.ds(pl.multiple_of(128 * slot, 128), 160)],
            rcv.at[place_of(t, half), mem], block_recv.at[t, slot],
        )

    def send_blocks(t):
        loop(1, 8, lambda j: block_copy(t, lax.rem(slot + j, 8)).start())
        own_copy(t).start()

    def wait_blocks(t):
        own_copy(t).wait()

        def wait(j):
            frm = lax.rem(slot + j, 8)
            remote(
                wide.at[0, 0:160], rcv.at[place_of(t, frm // 4), lax.rem(frm, 4)],
                block_send.at[t, frm], block_recv.at[t, frm], ring, frm,
            ).wait_recv()

        loop(1, 8, wait)

    turn_pair(0)
    pl.semaphore_wait(barrier, 7 + rings - 1)
    send_blocks(0)

    def next_pair(t):
        turn_pair(t)
        send_blocks(t)

    loop(1, 4, next_pair)

    load_spread.wait()
    mine = 8 + 8 * half
    for x in range(8):
        spr[mine + x] = spread_in[:, x, :]
    spr_here = remote(
        spr.at[pl.ds(mine, 8)], spr.at[pl.ds(mine, 8)], spr_send.at[0], spr_recv.at[0],
        ring, (1 - half) * 4 + mem,
    )
    spr_here.start()

    wait_blocks(0)
    halos = [
        remote(rcv.at[1], rcv.at[9], halo_send.at[0], halo_recv.at[0], above, slot),
        remote(rcv.at[8], rcv.at[0], halo_send.at[1], halo_recv.at[1], below, slot),
    ]
    for copy in halos:
        copy.start()

    load_obs.wait()
    obs = obs_in[...]
    in_ring = lax.broadcasted_iota(jnp.int32, (rings, 256), 0) == obs // 32
    in_patch = lax.broadcasted_iota(jnp.int32, (128, 256), 0) == lax.rem(obs, 32)
    tally = lax.dot_general(
        in_ring.astype(F32).astype(BF16), in_patch.astype(F32).astype(BF16), NT,
        preferred_element_type=F32,
    )
    for r in range(rings):
        cst[r] = jnp.broadcast_to(tally[r : r + 1, :], (8, 128))
    cra[ring] = cst[ring]

    def count_copy(j):
        to = lax.rem(ring + j, rings)
        return remote(cst.at[to], cra.at[ring], cnt_send.at[j], cnt_recv.at[ring], to, slot)

    loop(1, rings, lambda j: count_copy(j).start())

    spr_here.wait_send()
    other = 16 - 8 * half
    remote(
        spr.at[pl.ds(other, 8)], spr.at[pl.ds(other, 8)], spr_send.at[0], spr_recv.at[0],
        ring, (1 - half) * 4 + mem,
    ).wait_recv()
    spr_far = [
        remote(spr.at[8:10], spr.at[24:26], spr_send.at[1], spr_recv.at[1], above, slot),
        remote(spr.at[22:24], spr.at[6:8], spr_send.at[2], spr_recv.at[2], below, slot),
    ]
    for copy in spr_far:
        copy.start()

    def spread_row(i):
        lane = lax.broadcasted_iota(jnp.int32, (20, 8, 128), 2)
        column = lax.rem(
            lax.broadcasted_iota(jnp.int32, (20, 8, 128), 0) + 16 * slot + 126, 128
        )
        values = jnp.where(lane == column, spr[i + 6][None], 0.0)
        coef[i] = jnp.broadcast_to(jnp.sum(values, axis=2, keepdims=True), (20, 8, 128))

    loop(2, 18, spread_row)

    def coef_row(i):
        coef_ref[i] = coef[i + 2, 2:18]

    loop(0, 16, coef_row)
    for copy in spr_far:
        copy.wait()
    for i in (0, 1, 18, 19):
        spread_row(i)
    sublane = lax.broadcasted_iota(jnp.int32, (8, 128), 0)
    for k, ref in enumerate((sx_ref, sy_ref)):
        speed = jnp.zeros((8, 128), F32)
        for f in range(8):
            speed = jnp.where(sublane == f, ref[f], speed)
        wt_ref[4 + k] = speed

    def unshuffle(pair):
        low = lax.broadcasted_iota(jnp.int32, (160, 128), 1) < 64
        for mh in range(2):
            r0 = rcv[pair, 2 * mh].astype(F32)
            r1 = rcv[pair, 2 * mh + 1].astype(F32)
            even = jnp.where(low, r0, pltpu.roll(r1, 64, 1))
            odd = jnp.where(low, pltpu.roll(r0, 64, 1), r1)
            u0[mh, 2 * pair] = even.reshape(20, 8, 128)
            u0[mh, 2 * pair + 1] = odd.reshape(20, 8, 128)

    unshuffle(1)
    unshuffle(8)
    for copy in halos:
        copy.wait()
    unshuffle(0)
    unshuffle(9)

    sx = wt_ref[4][None]
    sy = wt_ref[5][None]

    def first(x):
        s = coef[x, 1:19]
        for mh in range(2):
            u1[mh, x - 1] = rounded(
                stencil(
                    u0[mh, x, 1:19], u0[mh, x - 1, 1:19], u0[mh, x + 1, 1:19],
                    u0[mh, x, 0:18], u0[mh, x, 2:20], s, sx, sy,
                )
            )

    def second(row, c):
        h, i = row // 8, lax.rem(row, 8)
        x, y = row + 1, 8 * c + 1
        s = coef[x + 1, y + 1 : y + 9]
        prior = [
            rounded(
                stencil(
                    u1[mh, x, y : y + 8], u1[mh, x - 1, y : y + 8], u1[mh, x + 1, y : y + 8],
                    u1[mh, x, y - 1 : y + 7], u1[mh, x, y + 1 : y + 9], s, sx, sy,
                )
            )
            for mh in range(2)
        ]
        centre = jnp.sum(prior[0] + prior[1], axis=2, keepdims=True) * (1.0 / 256.0)
        centre = jnp.broadcast_to(centre, (8, 8, 128))
        cen_ref[2 * h + c, i] = centre.reshape(64, 128)
        for mh in range(2):
            anom_ref[2 * h + c, i, :, mh * 128 : mh * 128 + 128] = (
                (prior[mh] - centre).reshape(64, 128).astype(BF16)
            )

    loop(1, 3, first)
    loop(17, 19, first)

    def inwards(t):
        wait_blocks(t)
        unshuffle(1 + t)
        unshuffle(8 - t)

        def firsts(k):
            first(2 * t + 1 + k)
            first(17 - 2 * t + k)

        loop(0, 2, firsts)

        def seconds(k):
            for c in range(2):
                second(2 * t - 2 + k, c)
                second(16 - 2 * t + k, c)

        loop(0, 2, seconds)

    loop(1, 3, inwards)

    def count_wait(j):
        frm = lax.rem(ring + j, rings)
        remote(cst.at[0], cra.at[frm], cnt_send.at[j], cnt_recv.at[frm], frm, slot).wait_recv()

    loop(1, rings, count_wait)
    total = cra[0]
    for r in range(1, rings):
        total = total + cra[r]
    crb[slot] = total

    def sum_copy(j):
        return remote(
            crb.at[slot], crb.at[slot], sum_send.at[j], sum_recv.at[slot], ring,
            lax.rem(slot + j, 8),
        )

    loop(1, 8, lambda j: sum_copy(j).start())

    wait_blocks(3)
    unshuffle(4)
    unshuffle(5)
    loop(7, 13, first)

    row = lax.broadcasted_iota(jnp.int32, (128, 128), 0)
    col = lax.broadcasted_iota(jnp.int32, (128, 128), 1)
    left = lax.rem(slot + 7, 8)
    right = lax.rem(slot + 1, 8)
    copies = []
    for c in range(2):
        for h in range(2):
            p = 2 * h + c

            loop(4 + 4 * h, 8 + 4 * h, lambda row, c=c: second(row, c))
            a = anom_ref[p].reshape(512, 256)
            g = lax.dot_general(a, a, TN, preferred_element_type=F32) * (1.0 / 512.0)
            last = g[128:, 128:]
            gpk[p, 0:128] = g[:128, 128:]
            gpk[p, 128:256] = jnp.where(row >= col, g[:128, :128], last)
            diag = jnp.sum(jnp.where(row == col, last, 0.0), axis=0, keepdims=True)
            gpk[p, 256:264] = jnp.broadcast_to(diag, (8, 128))
            vertical = (gab, below) if h else (gbe, above)
            sideways = (gle, right) if c else (gri, left)
            pair = [
                remote(
                    gpk.at[p], vertical[0].at[c], gram_send.at[2 * p], gram_recv.at[2 * p],
                    vertical[1], slot,
                ),
                remote(
                    gpk.at[p], sideways[0].at[h], gram_send.at[2 * p + 1],
                    gram_recv.at[2 * p + 1], ring, sideways[1],
                ),
            ]
            for copy in pair:
                copy.start()
            copies += pair

    def sum_wait(j):
        frm = lax.rem(slot + j, 8)
        remote(crb.at[slot], crb.at[frm], sum_send.at[j], sum_recv.at[frm], ring, frm).wait_recv()

    loop(1, 8, sum_wait)
    counts = crb[0]
    for k in range(1, 8):
        counts = counts + crb[k]
    lane = lax.broadcasted_iota(jnp.int32, (8, 128), 1)
    for h in range(2):
        for c in range(2):
            chosen = jnp.where(lane == h * 16 + 2 * slot + c, counts, 0.0)
            count = jnp.sum(chosen, axis=1, keepdims=True)
            wt_ref[2 * h + c] = jnp.broadcast_to(count / (count + 16.0), (8, 128))
    loop(1, rings, lambda j: count_copy(j).wait_send())
    loop(1, 8, lambda j: sum_copy(j).wait_send())
    loop(0, 4, lambda t: loop(1, 8, lambda j: block_copy(t, lax.rem(slot + j, 8)).wait_send()))
    for copy in copies:
        copy.wait()
    for c in range(2):
        for h in range(2):
            p = 2 * h + c
            up = gpk[c] if h else gab[c]
            down = gbe[c] if h else gpk[2 + c]
            lft = gpk[2 * h] if c else gle[h]
            rgt = gri[h] if c else gpk[2 * h + 1]
            avg_ref[p] = (2.0 * gpk[p] + up + down + lft + rgt) * (1.0 / 6.0)


def split(x):
    hi = x.astype(BF16)
    return hi, (x - hi.astype(F32)).astype(BF16)


def product(a, b):
    (ah, al), (bh, bl) = a, b
    return (
        jnp.dot(ah, bh, preferred_element_type=F32)
        + jnp.dot(ah, bl, preferred_element_type=F32)
        + jnp.dot(al, bh, preferred_element_type=F32)
    )


def analysis_kernel(avg_ref, wt_ref, yh, yl, zh, zl, last_ref, fh, fl):
    row = lax.broadcasted_iota(jnp.int32, (256, 256), 0)
    col = lax.broadcasted_iota(jnp.int32, (256, 256), 1)
    diagonal = row == col
    identity = jnp.where(diagonal, 1.0, 0.0)
    low = row[:128, :128] >= col[:128, :128]
    on = row[:128, :128] == col[:128, :128]

    def coefs(low_end, plain):
        alpha2 = jnp.where(plain, 1.0, 3.0 / (1.0 + low_end + low_end * low_end))
        alpha = jnp.sqrt(alpha2)
        reach = alpha * low_end
        after = 0.5 * reach * (3.0 - reach * reach)
        return 1.5 * alpha, 0.5 * alpha * alpha2, jnp.minimum(after, 1.0)

    ends, plains, scales = [], [], []
    for p in range(4):
        packed = avg_ref[p]
        upper_right = packed[0:128]
        both = packed[128:256]
        turned = both.T
        first = jnp.where(low, both, turned)
        last = jnp.where(on, jnp.broadcast_to(packed[256:257], (128, 128)), jnp.where(low, turned, both))
        averaged = jnp.concatenate(
            [
                jnp.concatenate([first, upper_right], axis=1),
                jnp.concatenate([upper_right.T, last], axis=1),
            ],
            axis=0,
        )
        system = identity + wt_ref[p, 0:1, 0:1] * averaged
        squares = jnp.sum(jnp.sum(system * system, axis=1, keepdims=True), axis=0, keepdims=True)
        norm = jnp.sqrt(squares)
        rows = jnp.max(
            jnp.sum(jnp.abs(system), axis=0, keepdims=True), axis=1, keepdims=True
        )
        plain = norm > PLAIN_NORM
        scale = jnp.where(plain, norm, jnp.minimum(norm, rows * 1.000001))
        start = system / scale
        low_end = jnp.where(plain, 0.0, jnp.sqrt(1.0 / scale) * 0.9999)
        a, b, after = coefs(low_end, plain)
        factor = a * identity - b * start
        y = product(split(start), split(factor))
        yh[p], yl[p] = split(y)
        zh[p], zl[p] = split(factor)
        ends.append(after)
        plains.append(plain)
        scales.append(scale)

    def some_left(ends, plains, k):
        left = jnp.zeros((1, 1), F32)
        for end, plain in zip(ends, plains):
            _, _, after = coefs(end, plain)
            todo = jnp.where(plain, jnp.where(k + 1 < NS_ITERS, 1.0, 0.0), jnp.where(1.0 - after > CONVERGED, 1.0, 0.0))
            left = jnp.maximum(left, todo)
        return jnp.max(left) > 0.5

    def body(carry):
        k, _, *ends = carry
        following = []
        for p in range(4):
            a, b, after = coefs(ends[p], plains[p])
            t = product((zh[p], zl[p]), (yh[p], yl[p]))
            fh[p], fl[p] = split(a * identity - b * t)
            following.append(after)
        for p in range(4):
            factor = (fh[p], fl[p])
            ny = product((yh[p], yl[p]), factor)
            nz = product(factor, (zh[p], zl[p]))
            yh[p], yl[p] = split(ny)
            zh[p], zl[p] = split(nz)
        return (k + 1, some_left(following, plains, k + 1), *following)

    last_k, _, *ends = lax.while_loop(
        lambda carry: carry[1], body, (1, some_left(ends, plains, 1), *ends)
    )
    for p in range(4):
        a, b, after = coefs(ends[p], plains[p])
        middle = jnp.where(plains[p], 1.0, 0.5 + 0.5 * after)
        for k, value in enumerate((a, b, 1.0 / (middle * jnp.sqrt(scales[p])))):
            last_ref[3 * p + k] = jnp.broadcast_to(value, (8, 128))


def return_kernel(
    rings,
    anom_ref,
    cen_ref,
    yh,
    yl,
    zh,
    zl,
    last_ref,
    coef_ref,
    wt_ref,
    out_ref,
    fh,
    fl,
    g,
    edge_out,
    edge_in,
    snd,
    rcv,
    pick,
    edge_send,
    edge_recv,
    main_send,
    main_recv,
    own_sem,
):
    ring, half, mem, slot = place()
    above = lax.rem(ring + rings - 1, rings)
    below = lax.rem(ring + 1, rings)
    left = lax.rem(slot + 7, 8)
    right = lax.rem(slot + 1, 8)
    barrier = pltpu.get_barrier_semaphore()
    loop(1, 8, lambda j: signal(barrier, ring, lax.rem(slot + j, 8)))
    signal(barrier, above, slot)
    signal(barrier, below, slot)

    diagonal = lax.broadcasted_iota(jnp.int32, (256, 256), 0) == lax.broadcasted_iota(
        jnp.int32, (256, 256), 1
    )
    for p in range(4):
        t = product((zh[p], zl[p]), (yh[p], yl[p]))
        a, b = last_ref[3 * p, 0:1, 0:1], last_ref[3 * p + 1, 0:1, 0:1]
        fh[p], fl[p] = split(jnp.where(diagonal, a, 0.0) - b * t)
    for p in range(4):
        inverse = product((fh[p], fl[p]), (zh[p], zl[p]))
        weights = (inverse * last_ref[3 * p + 2, 0:1, 0:1]).astype(BF16)
        update = jnp.dot(anom_ref[p].reshape(512, 256), weights, preferred_element_type=F32)
        centre = cen_ref[p].reshape(512, 128)
        h, c = p // 2, p % 2
        for mh in range(2):
            value = rounded(centre + update[:, mh * 128 : mh * 128 + 128])
            g[mh, 8 * h + 1 : 8 * h + 9, 8 * c + 1 : 8 * c + 9] = value.reshape(8, 8, 8, 128)
    for mh in range(2):
        lanes = slice(mh * 128, mh * 128 + 128)
        edge_out[0, :, lanes] = g[mh, 1, 1:17].reshape(128, 128).astype(BF16)
        edge_out[1, :, lanes] = g[mh, 16, 1:17].reshape(128, 128).astype(BF16)
        edge_out[2, :, lanes] = g[mh, 1:17, 1].reshape(128, 128).astype(BF16)
        edge_out[3, :, lanes] = g[mh, 1:17, 16].reshape(128, 128).astype(BF16)
    pl.semaphore_wait(barrier, 9)
    edges = [
        remote(edge_out.at[k], edge_in.at[k], edge_send.at[k], edge_recv.at[k], to_ring, to_slot)
        for k, (to_ring, to_slot) in enumerate(
            [(above, slot), (below, slot), (ring, left), (ring, right)]
        )
    ]
    for copy in edges:
        copy.start()
    sx = wt_ref[4][None]
    sy = wt_ref[5][None]

    def step_pair(h, pair, y0, y1):
        x = 8 * h + 2 * pair + 1
        rows = slice(8 * y0, 8 * y1)
        low = lax.broadcasted_iota(jnp.int32, (8 * (y1 - y0), 128), 1) < 64
        here, behind, ahead = slice(y0 + 1, y1 + 1), slice(y0, y1), slice(y0 + 2, y1 + 2)
        for mh in range(2):
            even, odd = [
                stencil(
                    g[mh, x + k, here], g[mh, x + k - 1, here], g[mh, x + k + 1, here],
                    g[mh, x + k, behind], g[mh, x + k, ahead], coef_ref[x + k - 1, y0:y1], sx, sy,
                ).reshape(8 * (y1 - y0), 128)
                for k in range(2)
            ]
            to = 4 * h + 2 * mh
            snd[to, pair, rows] = jnp.where(low, even, pltpu.roll(odd, 64, 1)).astype(BF16)
            snd[to + 1, pair, rows] = jnp.where(low, pltpu.roll(even, 64, 1), odd).astype(BF16)

    def parts(half_of):
        inner = pl.ds(1 - half_of, 3)
        return [
            (inner, slice(16, 112)), (inner, slice(0, 16)), (inner, slice(112, 128)),
            (3 * half_of, slice(0, 128)),
        ]

    def main_copy(part, to):
        pairs, rows = parts(to // 4)[part]
        return remote(
            snd.at[to, pairs, rows], rcv.at[slot, pairs, rows], main_send.at[part, to],
            main_recv.at[part, slot], ring, to,
        )

    def send(part):
        loop(1, 8, lambda j: main_copy(part, lax.rem(slot + j, 8)).start())

    for h in range(2):
        loop(1 - h, 4 - h, lambda pair, h=h: step_pair(h, pair, 2, 14))
    send(0)
    for copy in edges:
        copy.wait()
    for mh in range(2):
        lanes = slice(mh * 128, mh * 128 + 128)
        g[mh, 17, 1:17] = edge_in[0, :, lanes].astype(F32).reshape(16, 8, 128)
        g[mh, 0, 1:17] = edge_in[1, :, lanes].astype(F32).reshape(16, 8, 128)
        g[mh, 1:17, 17] = edge_in[2, :, lanes].astype(F32).reshape(16, 8, 128)
        g[mh, 1:17, 0] = edge_in[3, :, lanes].astype(F32).reshape(16, 8, 128)
    for part, y0 in ((1, 0), (2, 14)):
        for h in range(2):
            loop(1 - h, 4 - h, lambda pair, h=h, y0=y0: step_pair(h, pair, y0, y0 + 2))
        send(part)
    for h in range(2):
        step_pair(h, 3 * h, 0, 16)
    send(3)
    own = pltpu.make_async_copy(snd.at[slot], rcv.at[slot], own_sem)
    own.start()

    def pick_rows(i):
        row = lax.broadcasted_iota(jnp.int32, (128, 128), 0) + 128 * i
        lane = lax.broadcasted_iota(jnp.int32, (128, 128), 1)
        level = jnp.where(row // 8 == lane, lax.rem(row, 8), 8)
        rows = pl.ds(pl.multiple_of(128 * i, 128), 128)
        for f in range(8):
            pick[rows, f * 128 : f * 128 + 128] = jnp.where(level == f, 1.0, 0.0).astype(BF16)

    loop(0, 8, pick_rows)
    own.wait()

    def wait_part(part):
        def wait(j):
            frm = lax.rem(slot + j, 8)
            pairs, rows = parts(half)[part]
            remote(
                snd.at[frm, pairs, rows], rcv.at[frm, pairs, rows], main_send.at[part, frm],
                main_recv.at[part, frm], ring, frm,
            ).wait_recv()

        loop(1, 8, wait)

    def result_pair(pair):
        block = rcv[:, pair].reshape(1024, 128)
        result = lax.dot_general(block, pick[...], TN, preferred_element_type=F32).astype(BF16)
        out_ref[2 * pair] = result[:64]
        out_ref[2 * pair + 1] = result[64:]

    for part in range(3):
        wait_part(part)
    loop(1 - half, 4 - half, result_pair)
    wait_part(3)
    result_pair(3 * half)
    for part in range(4):
        loop(1, 8, lambda j, part=part: main_copy(part, lax.rem(slot + j, 8)).wait_send())


def vmem(count):
    return [pl.BlockSpec(memory_space=pltpu.VMEM)] * count


def local(member_collection, spreading_ratio, transport_ratio_row, transport_ratio_column, obs_patch):
    rings = lax.axis_size("tile") // 2
    DMA = pltpu.SemaphoreType.DMA
    obs = obs_patch.reshape(1, 256)

    def shape(dims, dtype=F32):
        return jax.ShapeDtypeStruct(dims, dtype)

    anom, cen, avg, wt, coef = pl.pallas_call(
        lambda *refs: forecast_kernel(rings, *refs),
        out_shape=[
            shape((4, 8, 64, 256), BF16),
            shape((4, 8, 64, 128)),
            shape((4, 264, 128)),
            shape((6, 8, 128)),
            shape((16, 16, 8, 128)),
        ],
        in_specs=[pl.BlockSpec(memory_space=pltpu.HBM)] * 3
        + [pl.BlockSpec(memory_space=pltpu.SMEM)] * 2,
        out_specs=vmem(5),
        scratch_shapes=[
            pltpu.VMEM((64, 8, 8, 128), BF16),
            pltpu.VMEM((8, 8, 128), F32),
            pltpu.VMEM((1, 256), jnp.int32),
            pltpu.VMEM((512, 1024), BF16),
            pltpu.VMEM((128, 1024), BF16),
            pltpu.VMEM((1024, 1024), BF16),
            pltpu.VMEM((4, 1056, 128), BF16),
            pltpu.VMEM((10, 4, 160, 128), BF16),
            pltpu.VMEM((2, 20, 20, 8, 128), F32),
            pltpu.VMEM((2, 18, 18, 8, 128), F32),
            pltpu.VMEM((20, 20, 8, 128), F32),
            pltpu.VMEM((32, 8, 128), F32),
            pltpu.VMEM((rings, 8, 128), F32),
            pltpu.VMEM((rings, 8, 128), F32),
            pltpu.VMEM((8, 8, 128), F32),
            pltpu.VMEM((4, 264, 128), F32),
            pltpu.VMEM((2, 264, 128), F32),
            pltpu.VMEM((2, 264, 128), F32),
            pltpu.VMEM((2, 264, 128), F32),
            pltpu.VMEM((2, 264, 128), F32),
            DMA((3,)),
            DMA((4, 8)),
            DMA((4, 8)),
            DMA((2,)),
            DMA((2,)),
            DMA((3,)),
            DMA((3,)),
            DMA((rings,)),
            DMA((rings,)),
            DMA((8,)),
            DMA((8,)),
            DMA((8,)),
            DMA((8,)),
        ],
        compiler_params=pltpu.CompilerParams(
            collective_id=0, has_side_effects=True, vmem_limit_bytes=VMEM_LIMIT
        ),
    )(member_collection, spreading_ratio, obs, transport_ratio_row, transport_ratio_column)

    square = shape((4, 256, 256), BF16)
    yh, yl, zh, zl, last = pl.pallas_call(
        analysis_kernel,
        out_shape=[square, square, square, square, shape((12, 8, 128))],
        in_specs=vmem(2),
        out_specs=vmem(5),
        scratch_shapes=[pltpu.VMEM((4, 256, 256), BF16)] * 2,
        compiler_params=pltpu.CompilerParams(vmem_limit_bytes=16 * 1024 * 1024),
    )(avg, wt)

    out = pl.pallas_call(
        lambda *refs: return_kernel(rings, *refs),
        out_shape=shape((8, 64, 1024), BF16),
        in_specs=vmem(9),
        out_specs=pl.BlockSpec(memory_space=pltpu.VMEM),
        scratch_shapes=[
            pltpu.VMEM((4, 256, 256), BF16),
            pltpu.VMEM((4, 256, 256), BF16),
            pltpu.VMEM((2, 18, 18, 8, 128), F32),
            pltpu.VMEM((4, 128, 256), BF16),
            pltpu.VMEM((4, 128, 256), BF16),
            pltpu.VMEM((8, 4, 128, 128), BF16),
            pltpu.VMEM((8, 4, 128, 128), BF16),
            pltpu.VMEM((1024, 1024), BF16),
            DMA((4,)),
            DMA((4,)),
            DMA((4, 8)),
            DMA((4, 8)),
            DMA,
        ],
        compiler_params=pltpu.CompilerParams(
            collective_id=1, has_side_effects=True, vmem_limit_bytes=24 * 1024 * 1024
        ),
    )(anom, cen, yh, yl, zh, zl, last, coef, wt)
    return jnp.transpose(out.reshape(8, 64, 8, 128), (1, 2, 0, 3))


def solution(mesh):
    placed = (P("mem", None, "tile", None), P(None, "tile", None), P(), P(), P(("mem", "tile")))
    return jax.shard_map(
        local, mesh=mesh, in_specs=placed, out_specs=P("mem", None, "tile", None), check_vma=False
    )
```

```python
import jax
import jax.numpy as jnp
from jax import lax
from jax.experimental import pallas as pl
from jax.experimental.pallas import tpu as pltpu
from jax.sharding import PartitionSpec as P

F32 = jnp.float32
BF16 = jnp.bfloat16
MESH = pl.DeviceIdType.MESH
VMEM_LIMIT = 50 * 1024 * 1024
NS_ITERS = 14
PLAIN_NORM = 2500.0
CONVERGED = 1e-5
NT = (((1,), (1,)), ((), ()))
TN = (((0,), (0,)), ((), ()))


def place():
    tile = lax.axis_index("tile")
    mem = lax.axis_index("mem")
    ring = tile // 2
    half = lax.rem(tile, 2)
    return ring, half, mem, half * 4 + mem


def target(ring, slot):
    return {"mem": lax.rem(slot, 4), "tile": 2 * ring + slot // 4}


def remote(src, dst, send_sem, recv_sem, ring, slot):
    return pltpu.make_async_remote_copy(
        src_ref=src,
        dst_ref=dst,
        send_sem=send_sem,
        recv_sem=recv_sem,
        device_id=target(ring, slot),
        device_id_type=MESH,
    )


def signal(sem, ring, slot):
    pl.semaphore_signal(sem, inc=1, device_id=target(ring, slot), device_id_type=MESH)


def stencil(c, bx, ax, by, ay, s, sx, sy):
    return c - sx * (c - bx) - sy * (c - by) + s * (ax + bx + ay + by - 4.0 * c)


def rounded(x):
    return x.astype(BF16).astype(F32)


def loop(lower, upper, body):
    def step(i, carry):
        body(i)
        return carry

    lax.fori_loop(lower, upper, step, 0)


def forecast_kernel(
    rings,
    u_hbm,
    spread_hbm,
    obs_hbm,
    sx_ref,
    sy_ref,
    anom_ref,
    cen_ref,
    avg_ref,
    wt_ref,
    coef_ref,
    raw,
    spread_in,
    obs_in,
    flat,
    state,
    pick,
    wide,
    rcv,
    u0,
    u1,
    coef,
    spr,
    cst,
    cra,
    crb,
    gpk,
    gab,
    gbe,
    gle,
    gri,
    load_sem,
    block_send,
    block_recv,
    halo_send,
    halo_recv,
    spr_send,
    spr_recv,
    cnt_send,
    cnt_recv,
    sum_send,
    sum_recv,
    gram_send,
    gram_recv,
):
    ring, half, mem, slot = place()
    above = lax.rem(ring + rings - 1, rings)
    below = lax.rem(ring + 1, rings)

    barrier = pltpu.get_barrier_semaphore()
    loop(1, 8, lambda j: signal(barrier, ring, lax.rem(slot + j, 8)))
    loop(1, rings, lambda j: signal(barrier, lax.rem(ring + j, rings), slot))
    load_raw = pltpu.make_async_copy(u_hbm, raw, load_sem.at[0])
    load_spread = pltpu.make_async_copy(spread_hbm, spread_in, load_sem.at[1])
    load_obs = pltpu.make_async_copy(obs_hbm, obs_in, load_sem.at[2])
    load_raw.start()
    load_spread.start()
    load_obs.start()

    def pick_rows(i):
        row = lax.broadcasted_iota(jnp.int32, (128, 128), 0) + 128 * i
        lane = lax.broadcasted_iota(jnp.int32, (128, 128), 1)
        level = jnp.where(row // 8 == lane, lax.rem(row, 8), 8)
        rows = pl.ds(pl.multiple_of(128 * i, 128), 128)
        for f in range(8):
            pick[rows, f * 128 : f * 128 + 128] = jnp.where(level == f, 1.0, 0.0).astype(BF16)

    loop(0, 8, pick_rows)

    load_raw.wait()
    for f in range(8):
        flat[:, f * 128 : f * 128 + 128] = raw[:, f].astype(F32).reshape(512, 128).astype(BF16)

    def pair_of(t, side):
        return t + side * (3 - 2 * t)

    def place_of(t, side):
        return 1 + 4 * side + pair_of(t, side)

    def turn_pair(t):
        pair = pair_of(t, half)
        k = lax.broadcasted_iota(jnp.int32, (128, 512), 1)
        r = lax.broadcasted_iota(jnp.int32, (128, 512), 0) + 128 * pair
        turn = jnp.where(k == lax.rem(r, 64) * 8 + r // 64, 1.0, 0.0).astype(BF16)
        state[...] = jnp.dot(turn, flat[...], preferred_element_type=F32).astype(BF16)
        block = lax.dot_general(
            pick[...], state[...], NT, preferred_element_type=F32
        ).astype(BF16)
        wide[pair, 16:1040] = block
        wide[pair, 0:16] = block[1008:1024]
        wide[pair, 1040:1056] = block[0:16]

    def block_copy(t, to):
        return remote(
            wide.at[pair_of(t, half), pl.ds(pl.multiple_of(128 * to, 128), 160)],
            rcv.at[place_of(t, half), mem], block_send.at[t, to], block_recv.at[t, slot], ring, to,
        )

    def own_copy(t):
        return pltpu.make_async_copy(
            wide.at[pair_of(t, half), pl.ds(pl.multiple_of(128 * slot, 128), 160)],
            rcv.at[place_of(t, half), mem], block_recv.at[t, slot],
        )

    def send_blocks(t):
        loop(1, 8, lambda j: block_copy(t, lax.rem(slot + j, 8)).start())
        own_copy(t).start()

    def wait_blocks(t):
        own_copy(t).wait()

        def wait(j):
            frm = lax.rem(slot + j, 8)
            remote(
                wide.at[0, 0:160], rcv.at[place_of(t, frm // 4), lax.rem(frm, 4)],
                block_send.at[t, frm], block_recv.at[t, frm], ring, frm,
            ).wait_recv()

        loop(1, 8, wait)

    turn_pair(0)
    pl.semaphore_wait(barrier, 7 + rings - 1)
    send_blocks(0)

    load_spread.wait()
    mine = 8 + 8 * half
    for x in range(8):
        spr[mine + x] = spread_in[:, x, :]
    spr_here = remote(
        spr.at[pl.ds(mine, 8)], spr.at[pl.ds(mine, 8)], spr_send.at[0], spr_recv.at[0],
        ring, (1 - half) * 4 + mem,
    )
    spr_here.start()

    turn_pair(1)
    send_blocks(1)
    turn_pair(2)

    load_obs.wait()
    obs = obs_in[...]
    in_ring = lax.broadcasted_iota(jnp.int32, (rings, 256), 0) == obs // 32
    in_patch = lax.broadcasted_iota(jnp.int32, (128, 256), 0) == lax.rem(obs, 32)
    tally = lax.dot_general(
        in_ring.astype(F32).astype(BF16), in_patch.astype(F32).astype(BF16), NT,
        preferred_element_type=F32,
    )
    for r in range(rings):
        cst[r] = jnp.broadcast_to(tally[r : r + 1, :], (8, 128))
    cra[ring] = cst[ring]

    def count_copy(j):
        to = lax.rem(ring + j, rings)
        return remote(cst.at[to], cra.at[ring], cnt_send.at[j], cnt_recv.at[ring], to, slot)

    wait_blocks(0)
    halos = [
        remote(rcv.at[1], rcv.at[9], halo_send.at[0], halo_recv.at[0], above, slot),
        remote(rcv.at[8], rcv.at[0], halo_send.at[1], halo_recv.at[1], below, slot),
    ]
    for copy in halos:
        copy.start()
    send_blocks(2)
    loop(1, rings, lambda j: count_copy(j).start())

    spr_here.wait_send()
    other = 16 - 8 * half
    remote(
        spr.at[pl.ds(other, 8)], spr.at[pl.ds(other, 8)], spr_send.at[0], spr_recv.at[0],
        ring, (1 - half) * 4 + mem,
    ).wait_recv()
    spr_far = [
        remote(spr.at[8:10], spr.at[24:26], spr_send.at[1], spr_recv.at[1], above, slot),
        remote(spr.at[22:24], spr.at[6:8], spr_send.at[2], spr_recv.at[2], below, slot),
    ]
    for copy in spr_far:
        copy.start()

    turn_pair(3)
    loop(1, 8, lambda j: block_copy(1, lax.rem(slot + j, 8)).wait_send())
    send_blocks(3)

    def spread_row(i):
        lane = lax.broadcasted_iota(jnp.int32, (20, 8, 128), 2)
        column = lax.rem(
            lax.broadcasted_iota(jnp.int32, (20, 8, 128), 0) + 16 * slot + 126, 128
        )
        values = jnp.where(lane == column, spr[i + 6][None], 0.0)
        coef[i] = jnp.broadcast_to(jnp.sum(values, axis=2, keepdims=True), (20, 8, 128))

    loop(2, 18, spread_row)

    def coef_row(i):
        coef_ref[i] = coef[i + 2, 2:18]

    loop(0, 16, coef_row)
    sublane = lax.broadcasted_iota(jnp.int32, (8, 128), 0)
    for k, ref in enumerate((sx_ref, sy_ref)):
        speed = jnp.zeros((8, 128), F32)
        for f in range(8):
            speed = jnp.where(sublane == f, ref[f], speed)
        wt_ref[4 + k] = speed

    def unshuffle(pair):
        low = lax.broadcasted_iota(jnp.int32, (160, 128), 1) < 64
        for mh in range(2):
            r0 = rcv[pair, 2 * mh].astype(F32)
            r1 = rcv[pair, 2 * mh + 1].astype(F32)
            even = jnp.where(low, r0, pltpu.roll(r1, 64, 1))
            odd = jnp.where(low, pltpu.roll(r0, 64, 1), r1)
            u0[mh, 2 * pair] = even.reshape(20, 8, 128)
            u0[mh, 2 * pair + 1] = odd.reshape(20, 8, 128)

    unshuffle(1)
    unshuffle(8)
    sx = wt_ref[4][None]
    sy = wt_ref[5][None]

    def first(x):
        s = coef[x, 1:19]
        for mh in range(2):
            u1[mh, x - 1] = rounded(
                stencil(
                    u0[mh, x, 1:19], u0[mh, x - 1, 1:19], u0[mh, x + 1, 1:19],
                    u0[mh, x, 0:18], u0[mh, x, 2:20], s, sx, sy,
                )
            )

    def second(row, c):
        h, i = row // 8, lax.rem(row, 8)
        x, y = row + 1, 8 * c + 1
        s = coef[x + 1, y + 1 : y + 9]
        prior = [
            rounded(
                stencil(
                    u1[mh, x, y : y + 8], u1[mh, x - 1, y : y + 8], u1[mh, x + 1, y : y + 8],
                    u1[mh, x, y - 1 : y + 7], u1[mh, x, y + 1 : y + 9], s, sx, sy,
                )
            )
            for mh in range(2)
        ]
        centre = jnp.sum(prior[0] + prior[1], axis=2, keepdims=True) * (1.0 / 256.0)
        centre = jnp.broadcast_to(centre, (8, 8, 128))
        cen_ref[2 * h + c, i] = centre.reshape(64, 128)
        for mh in range(2):
            anom_ref[2 * h + c, i, :, mh * 128 : mh * 128 + 128] = (
                (prior[mh] - centre).reshape(64, 128).astype(BF16)
            )

    def firsts(low, high):
        def both(k):
            first(low + k)
            first(high + k)

        loop(0, 2, both)

    def seconds(low, high):
        def both(k):
            for c in range(2):
                second(low + k, c)
                second(high + k, c)

        loop(0, 2, both)

    def inwards(t):
        wait_blocks(t)
        unshuffle(1 + t)
        unshuffle(8 - t)
        firsts(2 * t + 1, 17 - 2 * t)

    loop(1, 3, inwards)
    for copy in spr_far:
        copy.wait()
    for i in (0, 1, 18, 19):
        spread_row(i)
    for copy in halos:
        copy.wait()
    unshuffle(0)
    unshuffle(9)
    firsts(1, 17)

    def outer(t):
        seconds(2 * t, 14 - 2 * t)

    loop(0, 2, outer)

    def count_wait(j):
        frm = lax.rem(ring + j, rings)
        remote(cst.at[0], cra.at[frm], cnt_send.at[j], cnt_recv.at[frm], frm, slot).wait_recv()

    loop(1, rings, count_wait)
    total = cra[0]
    for r in range(1, rings):
        total = total + cra[r]
    crb[slot] = total

    def sum_copy(j):
        return remote(
            crb.at[slot], crb.at[slot], sum_send.at[j], sum_recv.at[slot], ring,
            lax.rem(slot + j, 8),
        )

    loop(1, 8, lambda j: sum_copy(j).start())

    wait_blocks(3)
    unshuffle(4)
    unshuffle(5)
    loop(7, 13, first)

    row = lax.broadcasted_iota(jnp.int32, (128, 128), 0)
    col = lax.broadcasted_iota(jnp.int32, (128, 128), 1)
    left = lax.rem(slot + 7, 8)
    right = lax.rem(slot + 1, 8)
    copies = []
    for c in range(2):
        for h in range(2):
            p = 2 * h + c

            loop(4 + 4 * h, 8 + 4 * h, lambda row, c=c: second(row, c))
            a = anom_ref[p].reshape(512, 256)
            g = lax.dot_general(a, a, TN, preferred_element_type=F32) * (1.0 / 512.0)
            last = g[128:, 128:]
            gpk[p, 0:128] = g[:128, 128:]
            gpk[p, 128:256] = jnp.where(row >= col, g[:128, :128], last)
            diag = jnp.sum(jnp.where(row == col, last, 0.0), axis=0, keepdims=True)
            gpk[p, 256:264] = jnp.broadcast_to(diag, (8, 128))
            vertical = (gab, below) if h else (gbe, above)
            sideways = (gle, right) if c else (gri, left)
            pair = [
                remote(
                    gpk.at[p], vertical[0].at[c], gram_send.at[2 * p], gram_recv.at[2 * p],
                    vertical[1], slot,
                ),
                remote(
                    gpk.at[p], sideways[0].at[h], gram_send.at[2 * p + 1],
                    gram_recv.at[2 * p + 1], ring, sideways[1],
                ),
            ]
            for copy in pair:
                copy.start()
            copies += pair

    def sum_wait(j):
        frm = lax.rem(slot + j, 8)
        remote(crb.at[slot], crb.at[frm], sum_send.at[j], sum_recv.at[frm], ring, frm).wait_recv()

    loop(1, 8, sum_wait)
    counts = crb[0]
    for k in range(1, 8):
        counts = counts + crb[k]
    lane = lax.broadcasted_iota(jnp.int32, (8, 128), 1)
    for h in range(2):
        for c in range(2):
            chosen = jnp.where(lane == h * 16 + 2 * slot + c, counts, 0.0)
            count = jnp.sum(chosen, axis=1, keepdims=True)
            wt_ref[2 * h + c] = jnp.broadcast_to(count / (count + 16.0), (8, 128))
    loop(1, rings, lambda j: count_copy(j).wait_send())
    loop(1, 8, lambda j: sum_copy(j).wait_send())
    for t in (0, 2, 3):
        loop(1, 8, lambda j, t=t: block_copy(t, lax.rem(slot + j, 8)).wait_send())
    for copy in copies:
        copy.wait()
    for c in range(2):
        for h in range(2):
            p = 2 * h + c
            up = gpk[c] if h else gab[c]
            down = gbe[c] if h else gpk[2 + c]
            lft = gpk[2 * h] if c else gle[h]
            rgt = gri[h] if c else gpk[2 * h + 1]
            avg_ref[p] = (2.0 * gpk[p] + up + down + lft + rgt) * (1.0 / 6.0)


def split(x):
    hi = x.astype(BF16)
    return hi, (x - hi.astype(F32)).astype(BF16)


def product(a, b):
    (ah, al), (bh, bl) = a, b
    return (
        jnp.dot(ah, bh, preferred_element_type=F32)
        + jnp.dot(ah, bl, preferred_element_type=F32)
        + jnp.dot(al, bh, preferred_element_type=F32)
    )


def analysis_kernel(avg_ref, wt_ref, yh, yl, zh, zl, last_ref, fh, fl):
    row = lax.broadcasted_iota(jnp.int32, (256, 256), 0)
    col = lax.broadcasted_iota(jnp.int32, (256, 256), 1)
    diagonal = row == col
    identity = jnp.where(diagonal, 1.0, 0.0)
    low = row[:128, :128] >= col[:128, :128]
    on = row[:128, :128] == col[:128, :128]

    def coefs(low_end, plain):
        alpha2 = jnp.where(plain, 1.0, 3.0 / (1.0 + low_end + low_end * low_end))
        alpha = jnp.sqrt(alpha2)
        reach = alpha * low_end
        after = 0.5 * reach * (3.0 - reach * reach)
        return 1.5 * alpha, 0.5 * alpha * alpha2, jnp.minimum(after, 1.0)

    ends, plains, scales = [], [], []
    for p in range(4):
        packed = avg_ref[p]
        upper_right = packed[0:128]
        both = packed[128:256]
        turned = both.T
        first = jnp.where(low, both, turned)
        last = jnp.where(on, jnp.broadcast_to(packed[256:257], (128, 128)), jnp.where(low, turned, both))
        averaged = jnp.concatenate(
            [
                jnp.concatenate([first, upper_right], axis=1),
                jnp.concatenate([upper_right.T, last], axis=1),
            ],
            axis=0,
        )
        system = identity + wt_ref[p, 0:1, 0:1] * averaged
        squares = jnp.sum(jnp.sum(system * system, axis=1, keepdims=True), axis=0, keepdims=True)
        norm = jnp.sqrt(squares)
        rows = jnp.max(
            jnp.sum(jnp.abs(system), axis=0, keepdims=True), axis=1, keepdims=True
        )
        plain = norm > PLAIN_NORM
        scale = jnp.where(plain, norm, jnp.minimum(norm, rows * 1.000001))
        start = system / scale
        low_end = jnp.where(plain, 0.0, jnp.sqrt(1.0 / scale) * 0.9999)
        a, b, after = coefs(low_end, plain)
        factor = a * identity - b * start
        y = product(split(start), split(factor))
        yh[p], yl[p] = split(y)
        zh[p], zl[p] = split(factor)
        ends.append(after)
        plains.append(plain)
        scales.append(scale)

    def some_left(ends, plains, k):
        left = jnp.zeros((1, 1), F32)
        for end, plain in zip(ends, plains):
            _, _, after = coefs(end, plain)
            todo = jnp.where(plain, jnp.where(k + 1 < NS_ITERS, 1.0, 0.0), jnp.where(1.0 - after > CONVERGED, 1.0, 0.0))
            left = jnp.maximum(left, todo)
        return jnp.max(left) > 0.5

    def body(carry):
        k, _, *ends = carry
        following = []
        for p in range(4):
            a, b, after = coefs(ends[p], plains[p])
            t = product((zh[p], zl[p]), (yh[p], yl[p]))
            fh[p], fl[p] = split(a * identity - b * t)
            following.append(after)
        for p in range(4):
            factor = (fh[p], fl[p])
            ny = product((yh[p], yl[p]), factor)
            nz = product(factor, (zh[p], zl[p]))
            yh[p], yl[p] = split(ny)
            zh[p], zl[p] = split(nz)
        return (k + 1, some_left(following, plains, k + 1), *following)

    last_k, _, *ends = lax.while_loop(
        lambda carry: carry[1], body, (1, some_left(ends, plains, 1), *ends)
    )
    for p in range(4):
        a, b, after = coefs(ends[p], plains[p])
        middle = jnp.where(plains[p], 1.0, 0.5 + 0.5 * after)
        for k, value in enumerate((a, b, 1.0 / (middle * jnp.sqrt(scales[p])))):
            last_ref[3 * p + k] = jnp.broadcast_to(value, (8, 128))


def return_kernel(
    rings,
    anom_ref,
    cen_ref,
    yh,
    yl,
    zh,
    zl,
    last_ref,
    coef_ref,
    wt_ref,
    out_ref,
    fh,
    fl,
    g,
    edge_out,
    edge_in,
    snd,
    rcv,
    pick,
    edge_send,
    edge_recv,
    main_send,
    main_recv,
    own_sem,
):
    ring, half, mem, slot = place()
    above = lax.rem(ring + rings - 1, rings)
    below = lax.rem(ring + 1, rings)
    left = lax.rem(slot + 7, 8)
    right = lax.rem(slot + 1, 8)
    barrier = pltpu.get_barrier_semaphore()
    loop(1, 8, lambda j: signal(barrier, ring, lax.rem(slot + j, 8)))
    signal(barrier, above, slot)
    signal(barrier, below, slot)

    diagonal = lax.broadcasted_iota(jnp.int32, (256, 256), 0) == lax.broadcasted_iota(
        jnp.int32, (256, 256), 1
    )
    for p in range(4):
        t = product((zh[p], zl[p]), (yh[p], yl[p]))
        a, b = last_ref[3 * p, 0:1, 0:1], last_ref[3 * p + 1, 0:1, 0:1]
        fh[p], fl[p] = split(jnp.where(diagonal, a, 0.0) - b * t)
    for p in range(4):
        inverse = product((fh[p], fl[p]), (zh[p], zl[p]))
        weights = (inverse * last_ref[3 * p + 2, 0:1, 0:1]).astype(BF16)
        update = jnp.dot(anom_ref[p].reshape(512, 256), weights, preferred_element_type=F32)
        centre = cen_ref[p].reshape(512, 128)
        h, c = p // 2, p % 2
        for mh in range(2):
            value = rounded(centre + update[:, mh * 128 : mh * 128 + 128])
            g[mh, 8 * h + 1 : 8 * h + 9, 8 * c + 1 : 8 * c + 9] = value.reshape(8, 8, 8, 128)
    for mh in range(2):
        lanes = slice(mh * 128, mh * 128 + 128)
        edge_out[0, :, lanes] = g[mh, 1, 1:17].reshape(128, 128).astype(BF16)
        edge_out[1, :, lanes] = g[mh, 16, 1:17].reshape(128, 128).astype(BF16)
        edge_out[2, :, lanes] = g[mh, 1:17, 1].reshape(128, 128).astype(BF16)
        edge_out[3, :, lanes] = g[mh, 1:17, 16].reshape(128, 128).astype(BF16)
    pl.semaphore_wait(barrier, 9)
    edges = [
        remote(edge_out.at[k], edge_in.at[k], edge_send.at[k], edge_recv.at[k], to_ring, to_slot)
        for k, (to_ring, to_slot) in enumerate(
            [(above, slot), (below, slot), (ring, left), (ring, right)]
        )
    ]
    for copy in edges:
        copy.start()
    sx = wt_ref[4][None]
    sy = wt_ref[5][None]

    def step_pair(h, pair, y0, y1):
        x = 8 * h + 2 * pair + 1
        rows = slice(8 * y0, 8 * y1)
        low = lax.broadcasted_iota(jnp.int32, (8 * (y1 - y0), 128), 1) < 64
        here, behind, ahead = slice(y0 + 1, y1 + 1), slice(y0, y1), slice(y0 + 2, y1 + 2)
        for mh in range(2):
            even, odd = [
                stencil(
                    g[mh, x + k, here], g[mh, x + k - 1, here], g[mh, x + k + 1, here],
                    g[mh, x + k, behind], g[mh, x + k, ahead], coef_ref[x + k - 1, y0:y1], sx, sy,
                ).reshape(8 * (y1 - y0), 128)
                for k in range(2)
            ]
            to = 4 * h + 2 * mh
            snd[to, pair, rows] = jnp.where(low, even, pltpu.roll(odd, 64, 1)).astype(BF16)
            snd[to + 1, pair, rows] = jnp.where(low, pltpu.roll(even, 64, 1), odd).astype(BF16)

    def parts(half_of):
        inner = pl.ds(1 - half_of, 3)
        return [
            (inner, slice(16, 112)), (inner, slice(0, 16)), (inner, slice(112, 128)),
            (3 * half_of, slice(0, 128)),
        ]

    def main_copy(part, to):
        pairs, rows = parts(to // 4)[part]
        return remote(
            snd.at[to, pairs, rows], rcv.at[slot, pairs, rows], main_send.at[part, to],
            main_recv.at[part, slot], ring, to,
        )

    def send(part):
        loop(1, 8, lambda j: main_copy(part, lax.rem(slot + j, 8)).start())

    for h in range(2):
        loop(1 - h, 4 - h, lambda pair, h=h: step_pair(h, pair, 2, 14))
    send(0)
    for copy in edges:
        copy.wait()
    for mh in range(2):
        lanes = slice(mh * 128, mh * 128 + 128)
        g[mh, 17, 1:17] = edge_in[0, :, lanes].astype(F32).reshape(16, 8, 128)
        g[mh, 0, 1:17] = edge_in[1, :, lanes].astype(F32).reshape(16, 8, 128)
        g[mh, 1:17, 17] = edge_in[2, :, lanes].astype(F32).reshape(16, 8, 128)
        g[mh, 1:17, 0] = edge_in[3, :, lanes].astype(F32).reshape(16, 8, 128)
    for part, y0 in ((1, 0), (2, 14)):
        for h in range(2):
            loop(1 - h, 4 - h, lambda pair, h=h, y0=y0: step_pair(h, pair, y0, y0 + 2))
        send(part)
    for h in range(2):
        step_pair(h, 3 * h, 0, 16)
    send(3)
    own = pltpu.make_async_copy(snd.at[slot], rcv.at[slot], own_sem)
    own.start()

    def pick_rows(i):
        row = lax.broadcasted_iota(jnp.int32, (128, 128), 0) + 128 * i
        lane = lax.broadcasted_iota(jnp.int32, (128, 128), 1)
        level = jnp.where(row // 8 == lane, lax.rem(row, 8), 8)
        rows = pl.ds(pl.multiple_of(128 * i, 128), 128)
        for f in range(8):
            pick[rows, f * 128 : f * 128 + 128] = jnp.where(level == f, 1.0, 0.0).astype(BF16)

    loop(0, 8, pick_rows)
    own.wait()

    def wait_part(part):
        def wait(j):
            frm = lax.rem(slot + j, 8)
            pairs, rows = parts(half)[part]
            remote(
                snd.at[frm, pairs, rows], rcv.at[frm, pairs, rows], main_send.at[part, frm],
                main_recv.at[part, frm], ring, frm,
            ).wait_recv()

        loop(1, 8, wait)

    def result_pair(pair):
        block = rcv[:, pair].reshape(1024, 128)
        result = lax.dot_general(block, pick[...], TN, preferred_element_type=F32).astype(BF16)
        out_ref[2 * pair] = result[:64]
        out_ref[2 * pair + 1] = result[64:]

    for part in range(3):
        wait_part(part)
    loop(1 - half, 4 - half, result_pair)
    wait_part(3)
    result_pair(3 * half)
    for part in range(4):
        loop(1, 8, lambda j, part=part: main_copy(part, lax.rem(slot + j, 8)).wait_send())


def vmem(count):
    return [pl.BlockSpec(memory_space=pltpu.VMEM)] * count


def local(member_collection, spreading_ratio, transport_ratio_row, transport_ratio_column, obs_patch):
    rings = lax.axis_size("tile") // 2
    DMA = pltpu.SemaphoreType.DMA
    obs = obs_patch.reshape(1, 256)

    def shape(dims, dtype=F32):
        return jax.ShapeDtypeStruct(dims, dtype)

    anom, cen, avg, wt, coef = pl.pallas_call(
        lambda *refs: forecast_kernel(rings, *refs),
        out_shape=[
            shape((4, 8, 64, 256), BF16),
            shape((4, 8, 64, 128)),
            shape((4, 264, 128)),
            shape((6, 8, 128)),
            shape((16, 16, 8, 128)),
        ],
        in_specs=[pl.BlockSpec(memory_space=pltpu.HBM)] * 3
        + [pl.BlockSpec(memory_space=pltpu.SMEM)] * 2,
        out_specs=vmem(5),
        scratch_shapes=[
            pltpu.VMEM((64, 8, 8, 128), BF16),
            pltpu.VMEM((8, 8, 128), F32),
            pltpu.VMEM((1, 256), jnp.int32),
            pltpu.VMEM((512, 1024), BF16),
            pltpu.VMEM((128, 1024), BF16),
            pltpu.VMEM((1024, 1024), BF16),
            pltpu.VMEM((4, 1056, 128), BF16),
            pltpu.VMEM((10, 4, 160, 128), BF16),
            pltpu.VMEM((2, 20, 20, 8, 128), F32),
            pltpu.VMEM((2, 18, 18, 8, 128), F32),
            pltpu.VMEM((20, 20, 8, 128), F32),
            pltpu.VMEM((32, 8, 128), F32),
            pltpu.VMEM((rings, 8, 128), F32),
            pltpu.VMEM((rings, 8, 128), F32),
            pltpu.VMEM((8, 8, 128), F32),
            pltpu.VMEM((4, 264, 128), F32),
            pltpu.VMEM((2, 264, 128), F32),
            pltpu.VMEM((2, 264, 128), F32),
            pltpu.VMEM((2, 264, 128), F32),
            pltpu.VMEM((2, 264, 128), F32),
            DMA((3,)),
            DMA((4, 8)),
            DMA((4, 8)),
            DMA((2,)),
            DMA((2,)),
            DMA((3,)),
            DMA((3,)),
            DMA((rings,)),
            DMA((rings,)),
            DMA((8,)),
            DMA((8,)),
            DMA((8,)),
            DMA((8,)),
        ],
        compiler_params=pltpu.CompilerParams(
            collective_id=0, has_side_effects=True, vmem_limit_bytes=VMEM_LIMIT
        ),
    )(member_collection, spreading_ratio, obs, transport_ratio_row, transport_ratio_column)

    square = shape((4, 256, 256), BF16)
    yh, yl, zh, zl, last = pl.pallas_call(
        analysis_kernel,
        out_shape=[square, square, square, square, shape((12, 8, 128))],
        in_specs=vmem(2),
        out_specs=vmem(5),
        scratch_shapes=[pltpu.VMEM((4, 256, 256), BF16)] * 2,
        compiler_params=pltpu.CompilerParams(vmem_limit_bytes=16 * 1024 * 1024),
    )(avg, wt)

    out = pl.pallas_call(
        lambda *refs: return_kernel(rings, *refs),
        out_shape=shape((8, 64, 1024), BF16),
        in_specs=vmem(9),
        out_specs=pl.BlockSpec(memory_space=pltpu.VMEM),
        scratch_shapes=[
            pltpu.VMEM((4, 256, 256), BF16),
            pltpu.VMEM((4, 256, 256), BF16),
            pltpu.VMEM((2, 18, 18, 8, 128), F32),
            pltpu.VMEM((4, 128, 256), BF16),
            pltpu.VMEM((4, 128, 256), BF16),
            pltpu.VMEM((8, 4, 128, 128), BF16),
            pltpu.VMEM((8, 4, 128, 128), BF16),
            pltpu.VMEM((1024, 1024), BF16),
            DMA((4,)),
            DMA((4,)),
            DMA((4, 8)),
            DMA((4, 8)),
            DMA,
        ],
        compiler_params=pltpu.CompilerParams(
            collective_id=1, has_side_effects=True, vmem_limit_bytes=24 * 1024 * 1024
        ),
    )(anom, cen, yh, yl, zh, zl, last, coef, wt)
    return jnp.transpose(out.reshape(8, 64, 8, 128), (1, 2, 0, 3))


def solution(mesh):
    placed = (P("mem", None, "tile", None), P(None, "tile", None), P(), P(), P(("mem", "tile")))
    return jax.shard_map(
        local, mesh=mesh, in_specs=placed, out_specs=P("mem", None, "tile", None), check_vma=False
    )
```

```python
import jax
import jax.numpy as jnp
from jax import lax
from jax.experimental import pallas as pl
from jax.experimental.pallas import tpu as pltpu
from jax.sharding import PartitionSpec as P

F32 = jnp.float32
BF16 = jnp.bfloat16
MESH = pl.DeviceIdType.MESH
VMEM_LIMIT = 50 * 1024 * 1024
NS_ITERS = 14
PLAIN_NORM = 2500.0
CONVERGED = 1e-5
NT = (((1,), (1,)), ((), ()))
TN = (((0,), (0,)), ((), ()))


def place():
    tile = lax.axis_index("tile")
    mem = lax.axis_index("mem")
    ring = tile // 2
    half = lax.rem(tile, 2)
    return ring, half, mem, half * 4 + mem


def target(ring, slot):
    return {"mem": lax.rem(slot, 4), "tile": 2 * ring + slot // 4}


def remote(src, dst, send_sem, recv_sem, ring, slot):
    return pltpu.make_async_remote_copy(
        src_ref=src,
        dst_ref=dst,
        send_sem=send_sem,
        recv_sem=recv_sem,
        device_id=target(ring, slot),
        device_id_type=MESH,
    )


def signal(sem, ring, slot):
    pl.semaphore_signal(sem, inc=1, device_id=target(ring, slot), device_id_type=MESH)


def stencil(c, bx, ax, by, ay, s, sx, sy):
    return c - sx * (c - bx) - sy * (c - by) + s * (ax + bx + ay + by - 4.0 * c)


def rounded(x):
    return x.astype(BF16).astype(F32)


def loop(lower, upper, body):
    def step(i, carry):
        body(i)
        return carry

    lax.fori_loop(lower, upper, step, 0)


def forecast_kernel(
    rings,
    u_hbm,
    spread_hbm,
    obs_hbm,
    sx_ref,
    sy_ref,
    anom_ref,
    cen_ref,
    avg_ref,
    wt_ref,
    coef_ref,
    raw,
    spread_in,
    obs_in,
    flat,
    state,
    pick,
    wide,
    rcv,
    u0,
    u1,
    coef,
    spr,
    cst,
    cra,
    crb,
    gpk,
    gab,
    gbe,
    gle,
    gri,
    load_sem,
    block_send,
    block_recv,
    halo_send,
    halo_recv,
    spr_send,
    spr_recv,
    cnt_send,
    cnt_recv,
    sum_send,
    sum_recv,
    gram_send,
    gram_recv,
):
    ring, half, mem, slot = place()
    above = lax.rem(ring + rings - 1, rings)
    below = lax.rem(ring + 1, rings)

    barrier = pltpu.get_barrier_semaphore()
    loop(1, 8, lambda j: signal(barrier, ring, lax.rem(slot + j, 8)))
    loop(1, rings, lambda j: signal(barrier, lax.rem(ring + j, rings), slot))
    load_raw = pltpu.make_async_copy(u_hbm, raw, load_sem.at[0])
    load_spread = pltpu.make_async_copy(spread_hbm, spread_in, load_sem.at[1])
    load_obs = pltpu.make_async_copy(obs_hbm, obs_in, load_sem.at[2])
    load_raw.start()
    load_spread.start()
    load_obs.start()

    def pick_rows(i):
        row = lax.broadcasted_iota(jnp.int32, (128, 128), 0) + 128 * i
        lane = lax.broadcasted_iota(jnp.int32, (128, 128), 1)
        level = jnp.where(row // 8 == lane, lax.rem(row, 8), 8)
        rows = pl.ds(pl.multiple_of(128 * i, 128), 128)
        for f in range(8):
            pick[rows, f * 128 : f * 128 + 128] = jnp.where(level == f, 1.0, 0.0).astype(BF16)

    loop(0, 8, pick_rows)

    load_raw.wait()
    for f in range(8):
        flat[:, f * 128 : f * 128 + 128] = raw[:, f].astype(F32).reshape(512, 128).astype(BF16)

    def pair_of(t, side):
        return t + side * (3 - 2 * t)

    def place_of(t, side):
        return 1 + 4 * side + pair_of(t, side)

    def turn_pair(t):
        pair = pair_of(t, half)
        k = lax.broadcasted_iota(jnp.int32, (128, 512), 1)
        r = lax.broadcasted_iota(jnp.int32, (128, 512), 0) + 128 * pair
        turn = jnp.where(k == lax.rem(r, 64) * 8 + r // 64, 1.0, 0.0).astype(BF16)
        state[...] = jnp.dot(turn, flat[...], preferred_element_type=F32).astype(BF16)
        block = lax.dot_general(
            pick[...], state[...], NT, preferred_element_type=F32
        ).astype(BF16)
        wide[pair, 16:1040] = block
        wide[pair, 0:16] = block[1008:1024]
        wide[pair, 1040:1056] = block[0:16]

    parts = [(0, 0, 160), (1, 0, 160), (2, 0, 96), (3, 0, 96), (2, 96, 160), (3, 96, 160)]

    def block_copy(q, to):
        t, low, high = parts[q]
        return remote(
            wide.at[
                pair_of(t, half), pl.ds(pl.multiple_of(128 * to + low, 16), high - low)
            ],
            rcv.at[place_of(t, half), mem, low:high], block_send.at[q, to],
            block_recv.at[q, slot], ring, to,
        )

    def own_copy(q):
        t, low, high = parts[q]
        return pltpu.make_async_copy(
            wide.at[
                pair_of(t, half), pl.ds(pl.multiple_of(128 * slot + low, 16), high - low)
            ],
            rcv.at[place_of(t, half), mem, low:high], block_recv.at[q, slot],
        )

    def send_blocks(q):
        loop(1, 8, lambda j: block_copy(q, lax.rem(slot + j, 8)).start())
        own_copy(q).start()

    def wait_blocks(q):
        own_copy(q).wait()
        t, low, high = parts[q]

        def wait(j):
            frm = lax.rem(slot + j, 8)
            remote(
                wide.at[0, low:high], rcv.at[place_of(t, frm // 4), lax.rem(frm, 4), low:high],
                block_send.at[q, frm], block_recv.at[q, frm], ring, frm,
            ).wait_recv()

        loop(1, 8, wait)

    turn_pair(0)
    pl.semaphore_wait(barrier, 7 + rings - 1)
    send_blocks(0)

    load_spread.wait()
    mine = 8 + 8 * half
    for x in range(8):
        spr[mine + x] = spread_in[:, x, :]
    spr_here = remote(
        spr.at[pl.ds(mine, 8)], spr.at[pl.ds(mine, 8)], spr_send.at[0], spr_recv.at[0],
        ring, (1 - half) * 4 + mem,
    )
    spr_here.start()

    turn_pair(1)
    send_blocks(1)
    turn_pair(2)

    load_obs.wait()
    obs = obs_in[...]
    in_ring = lax.broadcasted_iota(jnp.int32, (rings, 256), 0) == obs // 32
    in_patch = lax.broadcasted_iota(jnp.int32, (128, 256), 0) == lax.rem(obs, 32)
    tally = lax.dot_general(
        in_ring.astype(F32).astype(BF16), in_patch.astype(F32).astype(BF16), NT,
        preferred_element_type=F32,
    )
    for r in range(rings):
        cst[r] = jnp.broadcast_to(tally[r : r + 1, :], (8, 128))
    cra[ring] = cst[ring]

    def count_copy(j):
        to = lax.rem(ring + j, rings)
        return remote(cst.at[to], cra.at[ring], cnt_send.at[j], cnt_recv.at[ring], to, slot)

    wait_blocks(0)
    halos = [
        remote(rcv.at[1], rcv.at[9], halo_send.at[0], halo_recv.at[0], above, slot),
        remote(rcv.at[8], rcv.at[0], halo_send.at[1], halo_recv.at[1], below, slot),
    ]
    for copy in halos:
        copy.start()
    send_blocks(2)
    loop(1, rings, lambda j: count_copy(j).start())

    spr_here.wait_send()
    other = 16 - 8 * half
    remote(
        spr.at[pl.ds(other, 8)], spr.at[pl.ds(other, 8)], spr_send.at[0], spr_recv.at[0],
        ring, (1 - half) * 4 + mem,
    ).wait_recv()
    spr_far = [
        remote(spr.at[8:10], spr.at[24:26], spr_send.at[1], spr_recv.at[1], above, slot),
        remote(spr.at[22:24], spr.at[6:8], spr_send.at[2], spr_recv.at[2], below, slot),
    ]
    for copy in spr_far:
        copy.start()

    turn_pair(3)
    loop(1, 8, lambda j: block_copy(1, lax.rem(slot + j, 8)).wait_send())
    for q in (3, 4, 5):
        send_blocks(q)

    def spread_row(i):
        lane = lax.broadcasted_iota(jnp.int32, (20, 8, 128), 2)
        column = lax.rem(
            lax.broadcasted_iota(jnp.int32, (20, 8, 128), 0) + 16 * slot + 126, 128
        )
        values = jnp.where(lane == column, spr[i + 6][None], 0.0)
        coef[i] = jnp.broadcast_to(jnp.sum(values, axis=2, keepdims=True), (20, 8, 128))

    loop(2, 18, spread_row)

    def coef_row(i):
        coef_ref[i] = coef[i + 2, 2:18]

    loop(0, 16, coef_row)
    sublane = lax.broadcasted_iota(jnp.int32, (8, 128), 0)
    for k, ref in enumerate((sx_ref, sy_ref)):
        speed = jnp.zeros((8, 128), F32)
        for f in range(8):
            speed = jnp.where(sublane == f, ref[f], speed)
        wt_ref[4 + k] = speed

    def unshuffle(pair, y0=0, y1=20):
        low = lax.broadcasted_iota(jnp.int32, (8 * (y1 - y0), 128), 1) < 64
        rows = slice(8 * y0, 8 * y1)
        for mh in range(2):
            r0 = rcv[pair, 2 * mh, rows].astype(F32)
            r1 = rcv[pair, 2 * mh + 1, rows].astype(F32)
            even = jnp.where(low, r0, pltpu.roll(r1, 64, 1))
            odd = jnp.where(low, pltpu.roll(r0, 64, 1), r1)
            u0[mh, 2 * pair, y0:y1] = even.reshape(y1 - y0, 8, 128)
            u0[mh, 2 * pair + 1, y0:y1] = odd.reshape(y1 - y0, 8, 128)

    unshuffle(1)
    unshuffle(8)
    sx = wt_ref[4][None]
    sy = wt_ref[5][None]

    def first(x, y0=0, y1=18):
        s = coef[x, y0 + 1 : y1 + 1]
        here, behind, ahead = slice(y0 + 1, y1 + 1), slice(y0, y1), slice(y0 + 2, y1 + 2)
        for mh in range(2):
            u1[mh, x - 1, y0:y1] = rounded(
                stencil(
                    u0[mh, x, here], u0[mh, x - 1, here], u0[mh, x + 1, here],
                    u0[mh, x, behind], u0[mh, x, ahead], s, sx, sy,
                )
            )

    def second(row, c):
        h, i = row // 8, lax.rem(row, 8)
        x, y = row + 1, 8 * c + 1
        s = coef[x + 1, y + 1 : y + 9]
        prior = [
            rounded(
                stencil(
                    u1[mh, x, y : y + 8], u1[mh, x - 1, y : y + 8], u1[mh, x + 1, y : y + 8],
                    u1[mh, x, y - 1 : y + 7], u1[mh, x, y + 1 : y + 9], s, sx, sy,
                )
            )
            for mh in range(2)
        ]
        centre = jnp.sum(prior[0] + prior[1], axis=2, keepdims=True) * (1.0 / 256.0)
        centre = jnp.broadcast_to(centre, (8, 8, 128))
        cen_ref[2 * h + c, i] = centre.reshape(64, 128)
        for mh in range(2):
            anom_ref[2 * h + c, i, :, mh * 128 : mh * 128 + 128] = (
                (prior[mh] - centre).reshape(64, 128).astype(BF16)
            )

    def firsts(low, high, y0=0, y1=18):
        def both(k):
            first(low + k, y0, y1)
            first(high + k, y0, y1)

        loop(0, 2, both)

    def seconds(low, high, c):
        def both(k):
            second(low + k, c)
            second(high + k, c)

        loop(0, 2, both)

    wait_blocks(1)
    unshuffle(2)
    unshuffle(7)
    firsts(3, 15)
    for copy in spr_far:
        copy.wait()
    for i in (0, 1, 18, 19):
        spread_row(i)
    for copy in halos:
        copy.wait()
    unshuffle(0)
    unshuffle(9)
    firsts(1, 17)
    for c in range(2):
        seconds(0, 14, c)

    row = lax.broadcasted_iota(jnp.int32, (128, 128), 0)
    col = lax.broadcasted_iota(jnp.int32, (128, 128), 1)
    left = lax.rem(slot + 7, 8)
    right = lax.rem(slot + 1, 8)
    copies = []

    def sum_copy(j):
        return remote(
            crb.at[slot], crb.at[slot], sum_send.at[j], sum_recv.at[slot], ring,
            lax.rem(slot + j, 8),
        )

    for c in range(2):
        if c:
            def count_wait(j):
                frm = lax.rem(ring + j, rings)
                remote(cst.at[0], cra.at[frm], cnt_send.at[j], cnt_recv.at[frm], frm, slot).wait_recv()

            loop(1, rings, count_wait)
            total = cra[0]
            for r in range(1, rings):
                total = total + cra[r]
            crb[slot] = total

            loop(1, 8, lambda j: sum_copy(j).start())
        (y0, y1), (z0, z1) = (((0, 12), (0, 10)), ((12, 20), (10, 18)))[c]
        wait_blocks(2 + 2 * c)
        unshuffle(3, y0, y1)
        unshuffle(6, y0, y1)
        firsts(5, 13, z0, z1)
        seconds(2, 12, c)
        wait_blocks(3 + 2 * c)
        unshuffle(4, y0, y1)
        unshuffle(5, y0, y1)
        loop(7, 13, lambda x, z0=z0, z1=z1: first(x, z0, z1))
        for h in range(2):
            p = 2 * h + c
            loop(4 + 4 * h, 8 + 4 * h, lambda row, c=c: second(row, c))
            a = anom_ref[p].reshape(512, 256)
            g = lax.dot_general(a, a, TN, preferred_element_type=F32) * (1.0 / 512.0)
            last = g[128:, 128:]
            gpk[p, 0:128] = g[:128, 128:]
            gpk[p, 128:256] = jnp.where(row >= col, g[:128, :128], last)
            diag = jnp.sum(jnp.where(row == col, last, 0.0), axis=0, keepdims=True)
            gpk[p, 256:264] = jnp.broadcast_to(diag, (8, 128))
            vertical = (gab, below) if h else (gbe, above)
            sideways = (gle, right) if c else (gri, left)
            pair = [
                remote(
                    gpk.at[p], vertical[0].at[c], gram_send.at[2 * p], gram_recv.at[2 * p],
                    vertical[1], slot,
                ),
                remote(
                    gpk.at[p], sideways[0].at[h], gram_send.at[2 * p + 1],
                    gram_recv.at[2 * p + 1], ring, sideways[1],
                ),
            ]
            for copy in pair:
                copy.start()
            copies += pair

    def sum_wait(j):
        frm = lax.rem(slot + j, 8)
        remote(crb.at[slot], crb.at[frm], sum_send.at[j], sum_recv.at[frm], ring, frm).wait_recv()

    loop(1, 8, sum_wait)
    counts = crb[0]
    for k in range(1, 8):
        counts = counts + crb[k]
    lane = lax.broadcasted_iota(jnp.int32, (8, 128), 1)
    for h in range(2):
        for c in range(2):
            chosen = jnp.where(lane == h * 16 + 2 * slot + c, counts, 0.0)
            count = jnp.sum(chosen, axis=1, keepdims=True)
            wt_ref[2 * h + c] = jnp.broadcast_to(count / (count + 16.0), (8, 128))
    loop(1, rings, lambda j: count_copy(j).wait_send())
    loop(1, 8, lambda j: sum_copy(j).wait_send())
    for q in (0, 2, 3, 4, 5):
        loop(1, 8, lambda j, q=q: block_copy(q, lax.rem(slot + j, 8)).wait_send())
    for copy in copies:
        copy.wait()
    for c in range(2):
        for h in range(2):
            p = 2 * h + c
            up = gpk[c] if h else gab[c]
            down = gbe[c] if h else gpk[2 + c]
            lft = gpk[2 * h] if c else gle[h]
            rgt = gri[h] if c else gpk[2 * h + 1]
            avg_ref[p] = (2.0 * gpk[p] + up + down + lft + rgt) * (1.0 / 6.0)


def split(x):
    hi = x.astype(BF16)
    return hi, (x - hi.astype(F32)).astype(BF16)


def product(a, b):
    (ah, al), (bh, bl) = a, b
    return (
        jnp.dot(ah, bh, preferred_element_type=F32)
        + jnp.dot(ah, bl, preferred_element_type=F32)
        + jnp.dot(al, bh, preferred_element_type=F32)
    )


def analysis_kernel(avg_ref, wt_ref, yh, yl, zh, zl, last_ref, fh, fl):
    row = lax.broadcasted_iota(jnp.int32, (256, 256), 0)
    col = lax.broadcasted_iota(jnp.int32, (256, 256), 1)
    diagonal = row == col
    identity = jnp.where(diagonal, 1.0, 0.0)
    low = row[:128, :128] >= col[:128, :128]
    on = row[:128, :128] == col[:128, :128]

    def coefs(low_end, plain):
        alpha2 = jnp.where(plain, 1.0, 3.0 / (1.0 + low_end + low_end * low_end))
        alpha = jnp.sqrt(alpha2)
        reach = alpha * low_end
        after = 0.5 * reach * (3.0 - reach * reach)
        return 1.5 * alpha, 0.5 * alpha * alpha2, jnp.minimum(after, 1.0)

    ends, plains, scales = [], [], []
    for p in range(4):
        packed = avg_ref[p]
        upper_right = packed[0:128]
        both = packed[128:256]
        turned = both.T
        first = jnp.where(low, both, turned)
        last = jnp.where(on, jnp.broadcast_to(packed[256:257], (128, 128)), jnp.where(low, turned, both))
        averaged = jnp.concatenate(
            [
                jnp.concatenate([first, upper_right], axis=1),
                jnp.concatenate([upper_right.T, last], axis=1),
            ],
            axis=0,
        )
        system = identity + wt_ref[p, 0:1, 0:1] * averaged
        squares = jnp.sum(jnp.sum(system * system, axis=1, keepdims=True), axis=0, keepdims=True)
        norm = jnp.sqrt(squares)
        rows = jnp.max(
            jnp.sum(jnp.abs(system), axis=0, keepdims=True), axis=1, keepdims=True
        )
        plain = norm > PLAIN_NORM
        scale = jnp.where(plain, norm, jnp.minimum(norm, rows * 1.000001))
        start = system / scale
        low_end = jnp.where(plain, 0.0, jnp.sqrt(1.0 / scale) * 0.9999)
        a, b, after = coefs(low_end, plain)
        factor = a * identity - b * start
        y = product(split(start), split(factor))
        yh[p], yl[p] = split(y)
        zh[p], zl[p] = split(factor)
        ends.append(after)
        plains.append(plain)
        scales.append(scale)

    def some_left(ends, plains, k):
        left = jnp.zeros((1, 1), F32)
        for end, plain in zip(ends, plains):
            _, _, after = coefs(end, plain)
            todo = jnp.where(plain, jnp.where(k + 1 < NS_ITERS, 1.0, 0.0), jnp.where(1.0 - after > CONVERGED, 1.0, 0.0))
            left = jnp.maximum(left, todo)
        return jnp.max(left) > 0.5

    def body(carry):
        k, _, *ends = carry
        following = []
        for p in range(4):
            a, b, after = coefs(ends[p], plains[p])
            t = product((zh[p], zl[p]), (yh[p], yl[p]))
            fh[p], fl[p] = split(a * identity - b * t)
            following.append(after)
        for p in range(4):
            factor = (fh[p], fl[p])
            ny = product((yh[p], yl[p]), factor)
            nz = product(factor, (zh[p], zl[p]))
            yh[p], yl[p] = split(ny)
            zh[p], zl[p] = split(nz)
        return (k + 1, some_left(following, plains, k + 1), *following)

    last_k, _, *ends = lax.while_loop(
        lambda carry: carry[1], body, (1, some_left(ends, plains, 1), *ends)
    )
    for p in range(4):
        a, b, after = coefs(ends[p], plains[p])
        middle = jnp.where(plains[p], 1.0, 0.5 + 0.5 * after)
        for k, value in enumerate((a, b, 1.0 / (middle * jnp.sqrt(scales[p])))):
            last_ref[3 * p + k] = jnp.broadcast_to(value, (8, 128))


def return_kernel(
    rings,
    anom_ref,
    cen_ref,
    yh,
    yl,
    zh,
    zl,
    last_ref,
    coef_ref,
    wt_ref,
    out_ref,
    fh,
    fl,
    g,
    edge_out,
    edge_in,
    snd,
    rcv,
    pick,
    edge_send,
    edge_recv,
    main_send,
    main_recv,
    own_sem,
):
    ring, half, mem, slot = place()
    above = lax.rem(ring + rings - 1, rings)
    below = lax.rem(ring + 1, rings)
    left = lax.rem(slot + 7, 8)
    right = lax.rem(slot + 1, 8)
    barrier = pltpu.get_barrier_semaphore()
    loop(1, 8, lambda j: signal(barrier, ring, lax.rem(slot + j, 8)))
    signal(barrier, above, slot)
    signal(barrier, below, slot)

    diagonal = lax.broadcasted_iota(jnp.int32, (256, 256), 0) == lax.broadcasted_iota(
        jnp.int32, (256, 256), 1
    )
    for p in range(4):
        t = product((zh[p], zl[p]), (yh[p], yl[p]))
        a, b = last_ref[3 * p, 0:1, 0:1], last_ref[3 * p + 1, 0:1, 0:1]
        fh[p], fl[p] = split(jnp.where(diagonal, a, 0.0) - b * t)
    for p in range(4):
        inverse = product((fh[p], fl[p]), (zh[p], zl[p]))
        weights = (inverse * last_ref[3 * p + 2, 0:1, 0:1]).astype(BF16)
        update = jnp.dot(anom_ref[p].reshape(512, 256), weights, preferred_element_type=F32)
        centre = cen_ref[p].reshape(512, 128)
        h, c = p // 2, p % 2
        for mh in range(2):
            value = rounded(centre + update[:, mh * 128 : mh * 128 + 128])
            g[mh, 8 * h + 1 : 8 * h + 9, 8 * c + 1 : 8 * c + 9] = value.reshape(8, 8, 8, 128)
    for mh in range(2):
        lanes = slice(mh * 128, mh * 128 + 128)
        edge_out[0, :, lanes] = g[mh, 1, 1:17].reshape(128, 128).astype(BF16)
        edge_out[1, :, lanes] = g[mh, 16, 1:17].reshape(128, 128).astype(BF16)
        edge_out[2, :, lanes] = g[mh, 1:17, 1].reshape(128, 128).astype(BF16)
        edge_out[3, :, lanes] = g[mh, 1:17, 16].reshape(128, 128).astype(BF16)
    pl.semaphore_wait(barrier, 9)
    edges = [
        remote(edge_out.at[k], edge_in.at[k], edge_send.at[k], edge_recv.at[k], to_ring, to_slot)
        for k, (to_ring, to_slot) in enumerate(
            [(above, slot), (below, slot), (ring, left), (ring, right)]
        )
    ]
    for copy in edges:
        copy.start()
    sx = wt_ref[4][None]
    sy = wt_ref[5][None]

    def step_pair(h, pair, y0, y1):
        x = 8 * h + 2 * pair + 1
        rows = slice(8 * y0, 8 * y1)
        low = lax.broadcasted_iota(jnp.int32, (8 * (y1 - y0), 128), 1) < 64
        here, behind, ahead = slice(y0 + 1, y1 + 1), slice(y0, y1), slice(y0 + 2, y1 + 2)
        for mh in range(2):
            even, odd = [
                stencil(
                    g[mh, x + k, here], g[mh, x + k - 1, here], g[mh, x + k + 1, here],
                    g[mh, x + k, behind], g[mh, x + k, ahead], coef_ref[x + k - 1, y0:y1], sx, sy,
                ).reshape(8 * (y1 - y0), 128)
                for k in range(2)
            ]
            to = 4 * h + 2 * mh
            snd[to, pair, rows] = jnp.where(low, even, pltpu.roll(odd, 64, 1)).astype(BF16)
            snd[to + 1, pair, rows] = jnp.where(low, pltpu.roll(even, 64, 1), odd).astype(BF16)

    def parts(half_of):
        inner = pl.ds(1 - half_of, 3)
        return [
            (inner, slice(16, 112)), (inner, slice(0, 16)), (inner, slice(112, 128)),
            (3 * half_of, slice(0, 128)),
        ]

    def main_copy(part, to):
        pairs, rows = parts(to // 4)[part]
        return remote(
            snd.at[to, pairs, rows], rcv.at[slot, pairs, rows], main_send.at[part, to],
            main_recv.at[part, slot], ring, to,
        )

    def send(part):
        loop(1, 8, lambda j: main_copy(part, lax.rem(slot + j, 8)).start())

    for h in range(2):
        loop(1 - h, 4 - h, lambda pair, h=h: step_pair(h, pair, 2, 14))
    send(0)
    for copy in edges:
        copy.wait()
    for mh in range(2):
        lanes = slice(mh * 128, mh * 128 + 128)
        g[mh, 17, 1:17] = edge_in[0, :, lanes].astype(F32).reshape(16, 8, 128)
        g[mh, 0, 1:17] = edge_in[1, :, lanes].astype(F32).reshape(16, 8, 128)
        g[mh, 1:17, 17] = edge_in[2, :, lanes].astype(F32).reshape(16, 8, 128)
        g[mh, 1:17, 0] = edge_in[3, :, lanes].astype(F32).reshape(16, 8, 128)
    for part, y0 in ((1, 0), (2, 14)):
        for h in range(2):
            loop(1 - h, 4 - h, lambda pair, h=h, y0=y0: step_pair(h, pair, y0, y0 + 2))
        send(part)
    for h in range(2):
        step_pair(h, 3 * h, 0, 16)
    send(3)
    own = pltpu.make_async_copy(snd.at[slot], rcv.at[slot], own_sem)
    own.start()

    def pick_rows(i):
        row = lax.broadcasted_iota(jnp.int32, (128, 128), 0) + 128 * i
        lane = lax.broadcasted_iota(jnp.int32, (128, 128), 1)
        level = jnp.where(row // 8 == lane, lax.rem(row, 8), 8)
        rows = pl.ds(pl.multiple_of(128 * i, 128), 128)
        for f in range(8):
            pick[rows, f * 128 : f * 128 + 128] = jnp.where(level == f, 1.0, 0.0).astype(BF16)

    loop(0, 8, pick_rows)
    own.wait()

    def wait_part(part):
        def wait(j):
            frm = lax.rem(slot + j, 8)
            pairs, rows = parts(half)[part]
            remote(
                snd.at[frm, pairs, rows], rcv.at[frm, pairs, rows], main_send.at[part, frm],
                main_recv.at[part, frm], ring, frm,
            ).wait_recv()

        loop(1, 8, wait)

    def result_pair(pair):
        block = rcv[:, pair].reshape(1024, 128)
        result = lax.dot_general(block, pick[...], TN, preferred_element_type=F32).astype(BF16)
        out_ref[2 * pair] = result[:64]
        out_ref[2 * pair + 1] = result[64:]

    for part in range(3):
        wait_part(part)
    loop(1 - half, 4 - half, result_pair)
    wait_part(3)
    result_pair(3 * half)
    for part in range(4):
        loop(1, 8, lambda j, part=part: main_copy(part, lax.rem(slot + j, 8)).wait_send())


def vmem(count):
    return [pl.BlockSpec(memory_space=pltpu.VMEM)] * count


def local(member_collection, spreading_ratio, transport_ratio_row, transport_ratio_column, obs_patch):
    rings = lax.axis_size("tile") // 2
    DMA = pltpu.SemaphoreType.DMA
    obs = obs_patch.reshape(1, 256)

    def shape(dims, dtype=F32):
        return jax.ShapeDtypeStruct(dims, dtype)

    anom, cen, avg, wt, coef = pl.pallas_call(
        lambda *refs: forecast_kernel(rings, *refs),
        out_shape=[
            shape((4, 8, 64, 256), BF16),
            shape((4, 8, 64, 128)),
            shape((4, 264, 128)),
            shape((6, 8, 128)),
            shape((16, 16, 8, 128)),
        ],
        in_specs=[pl.BlockSpec(memory_space=pltpu.HBM)] * 3
        + [pl.BlockSpec(memory_space=pltpu.SMEM)] * 2,
        out_specs=vmem(5),
        scratch_shapes=[
            pltpu.VMEM((64, 8, 8, 128), BF16),
            pltpu.VMEM((8, 8, 128), F32),
            pltpu.VMEM((1, 256), jnp.int32),
            pltpu.VMEM((512, 1024), BF16),
            pltpu.VMEM((128, 1024), BF16),
            pltpu.VMEM((1024, 1024), BF16),
            pltpu.VMEM((4, 1056, 128), BF16),
            pltpu.VMEM((10, 4, 160, 128), BF16),
            pltpu.VMEM((2, 20, 20, 8, 128), F32),
            pltpu.VMEM((2, 18, 18, 8, 128), F32),
            pltpu.VMEM((20, 20, 8, 128), F32),
            pltpu.VMEM((32, 8, 128), F32),
            pltpu.VMEM((rings, 8, 128), F32),
            pltpu.VMEM((rings, 8, 128), F32),
            pltpu.VMEM((8, 8, 128), F32),
            pltpu.VMEM((4, 264, 128), F32),
            pltpu.VMEM((2, 264, 128), F32),
            pltpu.VMEM((2, 264, 128), F32),
            pltpu.VMEM((2, 264, 128), F32),
            pltpu.VMEM((2, 264, 128), F32),
            DMA((3,)),
            DMA((6, 8)),
            DMA((6, 8)),
            DMA((2,)),
            DMA((2,)),
            DMA((3,)),
            DMA((3,)),
            DMA((rings,)),
            DMA((rings,)),
            DMA((8,)),
            DMA((8,)),
            DMA((8,)),
            DMA((8,)),
        ],
        compiler_params=pltpu.CompilerParams(
            collective_id=0, has_side_effects=True, vmem_limit_bytes=VMEM_LIMIT
        ),
    )(member_collection, spreading_ratio, obs, transport_ratio_row, transport_ratio_column)

    square = shape((4, 256, 256), BF16)
    yh, yl, zh, zl, last = pl.pallas_call(
        analysis_kernel,
        out_shape=[square, square, square, square, shape((12, 8, 128))],
        in_specs=vmem(2),
        out_specs=vmem(5),
        scratch_shapes=[pltpu.VMEM((4, 256, 256), BF16)] * 2,
        compiler_params=pltpu.CompilerParams(vmem_limit_bytes=16 * 1024 * 1024),
    )(avg, wt)

    out = pl.pallas_call(
        lambda *refs: return_kernel(rings, *refs),
        out_shape=shape((8, 64, 1024), BF16),
        in_specs=vmem(9),
        out_specs=pl.BlockSpec(memory_space=pltpu.VMEM),
        scratch_shapes=[
            pltpu.VMEM((4, 256, 256), BF16),
            pltpu.VMEM((4, 256, 256), BF16),
            pltpu.VMEM((2, 18, 18, 8, 128), F32),
            pltpu.VMEM((4, 128, 256), BF16),
            pltpu.VMEM((4, 128, 256), BF16),
            pltpu.VMEM((8, 4, 128, 128), BF16),
            pltpu.VMEM((8, 4, 128, 128), BF16),
            pltpu.VMEM((1024, 1024), BF16),
            DMA((4,)),
            DMA((4,)),
            DMA((4, 8)),
            DMA((4, 8)),
            DMA,
        ],
        compiler_params=pltpu.CompilerParams(
            collective_id=1, has_side_effects=True, vmem_limit_bytes=24 * 1024 * 1024
        ),
    )(anom, cen, yh, yl, zh, zl, last, coef, wt)
    return jnp.transpose(out.reshape(8, 64, 8, 128), (1, 2, 0, 3))


def solution(mesh):
    placed = (P("mem", None, "tile", None), P(None, "tile", None), P(), P(), P(("mem", "tile")))
    return jax.shard_map(
        local, mesh=mesh, in_specs=placed, out_specs=P("mem", None, "tile", None), check_vma=False
    )
```

```python
import jax
import jax.numpy as jnp
from jax import lax
from jax.experimental import pallas as pl
from jax.experimental.pallas import tpu as pltpu
from jax.sharding import PartitionSpec as P

F32 = jnp.float32
BF16 = jnp.bfloat16
MESH = pl.DeviceIdType.MESH
VMEM_LIMIT = 50 * 1024 * 1024
NS_ITERS = 14
PLAIN_NORM = 2500.0
CONVERGED = 1e-5
NT = (((1,), (1,)), ((), ()))
TN = (((0,), (0,)), ((), ()))


def place():
    tile = lax.axis_index("tile")
    mem = lax.axis_index("mem")
    ring = tile // 2
    half = lax.rem(tile, 2)
    return ring, half, mem, half * 4 + mem


def target(ring, slot):
    return {"mem": lax.rem(slot, 4), "tile": 2 * ring + slot // 4}


def remote(src, dst, send_sem, recv_sem, ring, slot):
    return pltpu.make_async_remote_copy(
        src_ref=src,
        dst_ref=dst,
        send_sem=send_sem,
        recv_sem=recv_sem,
        device_id=target(ring, slot),
        device_id_type=MESH,
    )


def signal(sem, ring, slot):
    pl.semaphore_signal(sem, inc=1, device_id=target(ring, slot), device_id_type=MESH)


def stencil(c, bx, ax, by, ay, s, sx, sy):
    return c - sx * (c - bx) - sy * (c - by) + s * (ax + bx + ay + by - 4.0 * c)


def rounded(x):
    return x.astype(BF16).astype(F32)


def loop(lower, upper, body):
    def step(i, carry):
        body(i)
        return carry

    lax.fori_loop(lower, upper, step, 0)


def forecast_kernel(
    rings,
    u_hbm,
    spread_hbm,
    obs_hbm,
    sx_ref,
    sy_ref,
    anom_ref,
    cen_ref,
    avg_ref,
    wt_ref,
    coef_ref,
    raw,
    spread_in,
    obs_in,
    flat,
    state,
    pick,
    wide,
    rcv,
    u0,
    u1,
    coef,
    spr,
    cst,
    cra,
    crb,
    gpk,
    gab,
    gbe,
    gle,
    gri,
    load_sem,
    block_send,
    block_recv,
    halo_send,
    halo_recv,
    spr_send,
    spr_recv,
    cnt_send,
    cnt_recv,
    sum_send,
    sum_recv,
    gram_send,
    gram_recv,
):
    ring, half, mem, slot = place()
    above = lax.rem(ring + rings - 1, rings)
    below = lax.rem(ring + 1, rings)

    barrier = pltpu.get_barrier_semaphore()
    loop(1, 8, lambda j: signal(barrier, ring, lax.rem(slot + j, 8)))
    loop(1, rings, lambda j: signal(barrier, lax.rem(ring + j, rings), slot))
    load_raw = pltpu.make_async_copy(u_hbm, raw, load_sem.at[0])
    load_spread = pltpu.make_async_copy(spread_hbm, spread_in, load_sem.at[1])
    load_obs = pltpu.make_async_copy(obs_hbm, obs_in, load_sem.at[2])
    load_raw.start()
    load_spread.start()
    load_obs.start()

    def pick_rows(i):
        row = lax.broadcasted_iota(jnp.int32, (128, 128), 0) + 128 * i
        lane = lax.broadcasted_iota(jnp.int32, (128, 128), 1)
        level = jnp.where(row // 8 == lane, lax.rem(row, 8), 8)
        rows = pl.ds(pl.multiple_of(128 * i, 128), 128)
        for f in range(8):
            pick[rows, f * 128 : f * 128 + 128] = jnp.where(level == f, 1.0, 0.0).astype(BF16)

    loop(0, 8, pick_rows)

    load_raw.wait()
    for f in range(8):
        flat[:, f * 128 : f * 128 + 128] = raw[:, f].astype(F32).reshape(512, 128).astype(BF16)

    def pair_of(t, side):
        return t + side * (3 - 2 * t)

    def place_of(t, side):
        return 1 + 4 * side + pair_of(t, side)

    def turn_pair(t):
        pair = pair_of(t, half)
        k = lax.broadcasted_iota(jnp.int32, (128, 512), 1)
        r = lax.broadcasted_iota(jnp.int32, (128, 512), 0) + 128 * pair
        turn = jnp.where(k == lax.rem(r, 64) * 8 + r // 64, 1.0, 0.0).astype(BF16)
        state[...] = jnp.dot(turn, flat[...], preferred_element_type=F32).astype(BF16)
        block = lax.dot_general(
            pick[...], state[...], NT, preferred_element_type=F32
        ).astype(BF16)
        wide[pair, 16:1040] = block
        wide[pair, 0:16] = block[1008:1024]
        wide[pair, 1040:1056] = block[0:16]

    parts = [(0, 0, 160), (1, 0, 160), (2, 0, 96), (3, 0, 96), (2, 96, 160), (3, 96, 160)]

    def block_copy(q, to):
        t, low, high = parts[q]
        return remote(
            wide.at[
                pair_of(t, half), pl.ds(pl.multiple_of(128 * to + low, 16), high - low)
            ],
            rcv.at[place_of(t, half), mem, low:high], block_send.at[q, to],
            block_recv.at[q, slot], ring, to,
        )

    def own_copy(q):
        t, low, high = parts[q]
        return pltpu.make_async_copy(
            wide.at[
                pair_of(t, half), pl.ds(pl.multiple_of(128 * slot + low, 16), high - low)
            ],
            rcv.at[place_of(t, half), mem, low:high], block_recv.at[q, slot],
        )

    def send_blocks(q):
        loop(1, 8, lambda j: block_copy(q, lax.rem(slot + j, 8)).start())
        own_copy(q).start()

    def wait_blocks(q):
        own_copy(q).wait()
        t, low, high = parts[q]

        def wait(j):
            frm = lax.rem(slot + j, 8)
            remote(
                wide.at[0, low:high], rcv.at[place_of(t, frm // 4), lax.rem(frm, 4), low:high],
                block_send.at[q, frm], block_recv.at[q, frm], ring, frm,
            ).wait_recv()

        loop(1, 8, wait)

    turn_pair(0)
    pl.semaphore_wait(barrier, 7 + rings - 1)
    send_blocks(0)

    load_spread.wait()
    mine = 8 + 8 * half
    for x in range(8):
        spr[mine + x] = spread_in[:, x, :]
    spr_here = remote(
        spr.at[pl.ds(mine, 8)], spr.at[pl.ds(mine, 8)], spr_send.at[0], spr_recv.at[0],
        ring, (1 - half) * 4 + mem,
    )
    spr_here.start()

    turn_pair(1)
    send_blocks(1)
    turn_pair(2)

    load_obs.wait()
    obs = obs_in[...]
    in_ring = lax.broadcasted_iota(jnp.int32, (rings, 256), 0) == obs // 32
    in_patch = lax.broadcasted_iota(jnp.int32, (128, 256), 0) == lax.rem(obs, 32)
    tally = lax.dot_general(
        in_ring.astype(F32).astype(BF16), in_patch.astype(F32).astype(BF16), NT,
        preferred_element_type=F32,
    )
    for r in range(rings):
        cst[r] = jnp.broadcast_to(tally[r : r + 1, :], (8, 128))
    cra[ring] = cst[ring]

    def count_copy(j):
        to = lax.rem(ring + j, rings)
        return remote(cst.at[to], cra.at[ring], cnt_send.at[j], cnt_recv.at[ring], to, slot)

    wait_blocks(0)
    halos = [
        remote(rcv.at[1], rcv.at[9], halo_send.at[0], halo_recv.at[0], above, slot),
        remote(rcv.at[8], rcv.at[0], halo_send.at[1], halo_recv.at[1], below, slot),
    ]
    for copy in halos:
        copy.start()
    send_blocks(2)
    loop(1, rings, lambda j: count_copy(j).start())

    spr_here.wait_send()
    other = 16 - 8 * half
    remote(
        spr.at[pl.ds(other, 8)], spr.at[pl.ds(other, 8)], spr_send.at[0], spr_recv.at[0],
        ring, (1 - half) * 4 + mem,
    ).wait_recv()
    spr_far = [
        remote(spr.at[8:10], spr.at[24:26], spr_send.at[1], spr_recv.at[1], above, slot),
        remote(spr.at[22:24], spr.at[6:8], spr_send.at[2], spr_recv.at[2], below, slot),
    ]
    for copy in spr_far:
        copy.start()

    turn_pair(3)
    loop(1, 8, lambda j: block_copy(1, lax.rem(slot + j, 8)).wait_send())
    for q in (3, 4, 5):
        send_blocks(q)

    def spread_row(i):
        lane = lax.broadcasted_iota(jnp.int32, (20, 8, 128), 2)
        column = lax.rem(
            lax.broadcasted_iota(jnp.int32, (20, 8, 128), 0) + 16 * slot + 126, 128
        )
        values = jnp.where(lane == column, spr[i + 6][None], 0.0)
        coef[i] = jnp.broadcast_to(jnp.sum(values, axis=2, keepdims=True), (20, 8, 128))

    loop(2, 18, spread_row)

    def coef_row(i):
        coef_ref[i] = coef[i + 2, 2:18]

    loop(0, 16, coef_row)
    sublane = lax.broadcasted_iota(jnp.int32, (8, 128), 0)
    for k, ref in enumerate((sx_ref, sy_ref)):
        speed = jnp.zeros((8, 128), F32)
        for f in range(8):
            speed = jnp.where(sublane == f, ref[f], speed)
        wt_ref[4 + k] = speed

    def unshuffle(pair, y0=0, y1=20):
        low = lax.broadcasted_iota(jnp.int32, (8 * (y1 - y0), 128), 1) < 64
        rows = slice(8 * y0, 8 * y1)
        for mh in range(2):
            r0 = rcv[pair, 2 * mh, rows].astype(F32)
            r1 = rcv[pair, 2 * mh + 1, rows].astype(F32)
            even = jnp.where(low, r0, pltpu.roll(r1, 64, 1))
            odd = jnp.where(low, pltpu.roll(r0, 64, 1), r1)
            u0[mh, 2 * pair, y0:y1] = even.reshape(y1 - y0, 8, 128)
            u0[mh, 2 * pair + 1, y0:y1] = odd.reshape(y1 - y0, 8, 128)

    unshuffle(1)
    unshuffle(8)
    sx = wt_ref[4][None]
    sy = wt_ref[5][None]

    def first(x, y0=0, y1=18):
        s = coef[x, y0 + 1 : y1 + 1]
        here, behind, ahead = slice(y0 + 1, y1 + 1), slice(y0, y1), slice(y0 + 2, y1 + 2)
        for mh in range(2):
            u1[mh, x - 1, y0:y1] = rounded(
                stencil(
                    u0[mh, x, here], u0[mh, x - 1, here], u0[mh, x + 1, here],
                    u0[mh, x, behind], u0[mh, x, ahead], s, sx, sy,
                )
            )

    def second(row, c):
        h, i = row // 8, lax.rem(row, 8)
        x, y = row + 1, 8 * c + 1
        s = coef[x + 1, y + 1 : y + 9]
        prior = [
            rounded(
                stencil(
                    u1[mh, x, y : y + 8], u1[mh, x - 1, y : y + 8], u1[mh, x + 1, y : y + 8],
                    u1[mh, x, y - 1 : y + 7], u1[mh, x, y + 1 : y + 9], s, sx, sy,
                )
            )
            for mh in range(2)
        ]
        centre = jnp.sum(prior[0] + prior[1], axis=2, keepdims=True) * (1.0 / 256.0)
        centre = jnp.broadcast_to(centre, (8, 8, 128))
        cen_ref[2 * h + c, i] = centre.reshape(64, 128)
        for mh in range(2):
            anom_ref[2 * h + c, i, :, mh * 128 : mh * 128 + 128] = (
                (prior[mh] - centre).reshape(64, 128).astype(BF16)
            )

    def firsts(low, high, y0=0, y1=18):
        def both(k):
            first(low + k, y0, y1)
            first(high + k, y0, y1)

        loop(0, 2, both)

    def seconds(low, high, c):
        def both(k):
            second(low + k, c)
            second(high + k, c)

        loop(0, 2, both)

    wait_blocks(1)
    unshuffle(2)
    unshuffle(7)
    firsts(3, 15)
    for copy in spr_far:
        copy.wait()
    for i in (0, 1, 18, 19):
        spread_row(i)
    for copy in halos:
        copy.wait()
    unshuffle(0)
    unshuffle(9)
    firsts(1, 17)
    for c in range(2):
        seconds(0, 14, c)

    row = lax.broadcasted_iota(jnp.int32, (128, 128), 0)
    col = lax.broadcasted_iota(jnp.int32, (128, 128), 1)
    left = lax.rem(slot + 7, 8)
    right = lax.rem(slot + 1, 8)
    copies = []

    def sum_copy(j):
        return remote(
            crb.at[slot], crb.at[slot], sum_send.at[j], sum_recv.at[slot], ring,
            lax.rem(slot + j, 8),
        )

    for c in range(2):
        if c:
            def count_wait(j):
                frm = lax.rem(ring + j, rings)
                remote(cst.at[0], cra.at[frm], cnt_send.at[j], cnt_recv.at[frm], frm, slot).wait_recv()

            loop(1, rings, count_wait)
            total = cra[0]
            for r in range(1, rings):
                total = total + cra[r]
            crb[slot] = total

            loop(1, 8, lambda j: sum_copy(j).start())
        (y0, y1), (z0, z1) = (((0, 12), (0, 10)), ((12, 20), (10, 18)))[c]
        wait_blocks(2 + 2 * c)
        unshuffle(3, y0, y1)
        unshuffle(6, y0, y1)
        firsts(5, 13, z0, z1)
        seconds(2, 12, c)
        wait_blocks(3 + 2 * c)
        unshuffle(4, y0, y1)
        unshuffle(5, y0, y1)
        loop(7, 13, lambda x, z0=z0, z1=z1: first(x, z0, z1))
        for h in range(2):
            p = 2 * h + c
            loop(4 + 4 * h, 8 + 4 * h, lambda row, c=c: second(row, c))
            a = anom_ref[p].reshape(512, 256)
            g = lax.dot_general(a, a, TN, preferred_element_type=F32) * (1.0 / 512.0)
            last = g[128:, 128:]
            gpk[p, 0:128] = g[:128, 128:]
            gpk[p, 128:256] = jnp.where(row >= col, g[:128, :128], last)
            diag = jnp.sum(jnp.where(row == col, last, 0.0), axis=0, keepdims=True)
            gpk[p, 256:264] = jnp.broadcast_to(diag, (8, 128))
            vertical = (gab, below) if h else (gbe, above)
            sideways = (gle, right) if c else (gri, left)
            pair = [
                remote(
                    gpk.at[p], vertical[0].at[c], gram_send.at[2 * p], gram_recv.at[2 * p],
                    vertical[1], slot,
                ),
                remote(
                    gpk.at[p], sideways[0].at[h], gram_send.at[2 * p + 1],
                    gram_recv.at[2 * p + 1], ring, sideways[1],
                ),
            ]
            for copy in pair:
                copy.start()
            copies += pair

    def sum_wait(j):
        frm = lax.rem(slot + j, 8)
        remote(crb.at[slot], crb.at[frm], sum_send.at[j], sum_recv.at[frm], ring, frm).wait_recv()

    loop(1, 8, sum_wait)
    counts = crb[0]
    for k in range(1, 8):
        counts = counts + crb[k]
    lane = lax.broadcasted_iota(jnp.int32, (8, 128), 1)
    for h in range(2):
        for c in range(2):
            chosen = jnp.where(lane == h * 16 + 2 * slot + c, counts, 0.0)
            count = jnp.sum(chosen, axis=1, keepdims=True)
            wt_ref[2 * h + c] = jnp.broadcast_to(count / (count + 16.0), (8, 128))
    loop(1, rings, lambda j: count_copy(j).wait_send())
    loop(1, 8, lambda j: sum_copy(j).wait_send())
    for q in (0, 2, 3, 4, 5):
        loop(1, 8, lambda j, q=q: block_copy(q, lax.rem(slot + j, 8)).wait_send())
    for copy in copies:
        copy.wait()
    for c in range(2):
        for h in range(2):
            p = 2 * h + c
            up = gpk[c] if h else gab[c]
            down = gbe[c] if h else gpk[2 + c]
            lft = gpk[2 * h] if c else gle[h]
            rgt = gri[h] if c else gpk[2 * h + 1]
            avg_ref[p] = (2.0 * gpk[p] + up + down + lft + rgt) * (1.0 / 6.0)


def split(x):
    hi = x.astype(BF16)
    return hi, (x - hi.astype(F32)).astype(BF16)


def product(a, b):
    (ah, al), (bh, bl) = a, b
    return (
        jnp.dot(ah, bh, preferred_element_type=F32)
        + jnp.dot(ah, bl, preferred_element_type=F32)
        + jnp.dot(al, bh, preferred_element_type=F32)
    )


def analysis_kernel(avg_ref, wt_ref, yh, yl, zh, zl, last_ref, fh, fl):
    row = lax.broadcasted_iota(jnp.int32, (256, 256), 0)
    col = lax.broadcasted_iota(jnp.int32, (256, 256), 1)
    diagonal = row == col
    identity = jnp.where(diagonal, 1.0, 0.0)
    low = row[:128, :128] >= col[:128, :128]
    on = row[:128, :128] == col[:128, :128]

    def coefs(low_end, plain):
        alpha2 = jnp.where(plain, 1.0, 3.0 / (1.0 + low_end + low_end * low_end))
        alpha = jnp.sqrt(alpha2)
        reach = alpha * low_end
        after = 0.5 * reach * (3.0 - reach * reach)
        return 1.5 * alpha, 0.5 * alpha * alpha2, jnp.minimum(after, 1.0)

    ends, plains, scales = [], [], []
    for p in range(4):
        packed = avg_ref[p]
        upper_right = packed[0:128]
        both = packed[128:256]
        turned = both.T
        first = jnp.where(low, both, turned)
        last = jnp.where(on, jnp.broadcast_to(packed[256:257], (128, 128)), jnp.where(low, turned, both))
        averaged = jnp.concatenate(
            [
                jnp.concatenate([first, upper_right], axis=1),
                jnp.concatenate([upper_right.T, last], axis=1),
            ],
            axis=0,
        )
        system = identity + wt_ref[p, 0:1, 0:1] * averaged
        squares = jnp.sum(jnp.sum(system * system, axis=1, keepdims=True), axis=0, keepdims=True)
        norm = jnp.sqrt(squares)
        rows = jnp.max(
            jnp.sum(jnp.abs(system), axis=0, keepdims=True), axis=1, keepdims=True
        )
        plain = norm > PLAIN_NORM
        scale = jnp.where(plain, norm, jnp.minimum(norm, rows * 1.000001))
        start = system / scale
        low_end = jnp.where(plain, 0.0, jnp.sqrt(1.0 / scale) * 0.9999)
        a, b, after = coefs(low_end, plain)
        factor = a * identity - b * start
        y = product(split(start), split(factor))
        yh[p], yl[p] = split(y)
        zh[p], zl[p] = split(factor)
        ends.append(after)
        plains.append(plain)
        scales.append(scale)

    def some_left(ends, plains, k):
        left = jnp.zeros((1, 1), F32)
        for end, plain in zip(ends, plains):
            _, _, after = coefs(end, plain)
            todo = jnp.where(plain, jnp.where(k + 1 < NS_ITERS, 1.0, 0.0), jnp.where(1.0 - after > CONVERGED, 1.0, 0.0))
            left = jnp.maximum(left, todo)
        return jnp.max(left) > 0.5

    def body(carry):
        k, _, *ends = carry
        following = []
        for p in range(4):
            a, b, after = coefs(ends[p], plains[p])
            t = product((zh[p], zl[p]), (yh[p], yl[p]))
            fh[p], fl[p] = split(a * identity - b * t)
            following.append(after)
        for p in range(4):
            factor = (fh[p], fl[p])
            ny = product((yh[p], yl[p]), factor)
            nz = product(factor, (zh[p], zl[p]))
            yh[p], yl[p] = split(ny)
            zh[p], zl[p] = split(nz)
        return (k + 1, some_left(following, plains, k + 1), *following)

    last_k, _, *ends = lax.while_loop(
        lambda carry: carry[1], body, (1, some_left(ends, plains, 1), *ends)
    )
    for p in range(4):
        a, b, after = coefs(ends[p], plains[p])
        middle = jnp.where(plains[p], 1.0, 0.5 + 0.5 * after)
        for k, value in enumerate((a, b, 1.0 / (middle * jnp.sqrt(scales[p])))):
            last_ref[3 * p + k] = jnp.broadcast_to(value, (8, 128))


def return_kernel(
    rings,
    anom_ref,
    cen_ref,
    yh,
    yl,
    zh,
    zl,
    last_ref,
    coef_ref,
    wt_ref,
    out_ref,
    fh,
    fl,
    g,
    edge_out,
    edge_in,
    snd,
    rcv,
    pick,
    edge_send,
    edge_recv,
    main_send,
    main_recv,
    own_sem,
):
    ring, half, mem, slot = place()
    above = lax.rem(ring + rings - 1, rings)
    below = lax.rem(ring + 1, rings)
    left = lax.rem(slot + 7, 8)
    right = lax.rem(slot + 1, 8)
    barrier = pltpu.get_barrier_semaphore()
    loop(1, 8, lambda j: signal(barrier, ring, lax.rem(slot + j, 8)))
    signal(barrier, above, slot)
    signal(barrier, below, slot)

    diagonal = lax.broadcasted_iota(jnp.int32, (256, 256), 0) == lax.broadcasted_iota(
        jnp.int32, (256, 256), 1
    )
    for p in range(4):
        t = product((zh[p], zl[p]), (yh[p], yl[p]))
        a, b = last_ref[3 * p, 0:1, 0:1], last_ref[3 * p + 1, 0:1, 0:1]
        fh[p], fl[p] = split(jnp.where(diagonal, a, 0.0) - b * t)
    for p in range(4):
        inverse = product((fh[p], fl[p]), (zh[p], zl[p]))
        weights = (inverse * last_ref[3 * p + 2, 0:1, 0:1]).astype(BF16)
        update = jnp.dot(anom_ref[p].reshape(512, 256), weights, preferred_element_type=F32)
        centre = cen_ref[p].reshape(512, 128)
        h, c = p // 2, p % 2
        for mh in range(2):
            value = rounded(centre + update[:, mh * 128 : mh * 128 + 128])
            g[mh, 8 * h + 1 : 8 * h + 9, 8 * c + 1 : 8 * c + 9] = value.reshape(8, 8, 8, 128)
    for mh in range(2):
        lanes = slice(mh * 128, mh * 128 + 128)
        edge_out[0, :, lanes] = g[mh, 1, 1:17].reshape(128, 128).astype(BF16)
        edge_out[1, :, lanes] = g[mh, 16, 1:17].reshape(128, 128).astype(BF16)
        edge_out[2, :, lanes] = g[mh, 1:17, 1].reshape(128, 128).astype(BF16)
        edge_out[3, :, lanes] = g[mh, 1:17, 16].reshape(128, 128).astype(BF16)
    pl.semaphore_wait(barrier, 9)
    edges = [
        remote(edge_out.at[k], edge_in.at[k], edge_send.at[k], edge_recv.at[k], to_ring, to_slot)
        for k, (to_ring, to_slot) in enumerate(
            [(above, slot), (below, slot), (ring, left), (ring, right)]
        )
    ]
    for copy in edges:
        copy.start()
    sx = wt_ref[4][None]
    sy = wt_ref[5][None]

    def step_pair(h, pair, y0, y1):
        x = 8 * h + 2 * pair + 1
        rows = slice(8 * y0, 8 * y1)
        low = lax.broadcasted_iota(jnp.int32, (8 * (y1 - y0), 128), 1) < 64
        here, behind, ahead = slice(y0 + 1, y1 + 1), slice(y0, y1), slice(y0 + 2, y1 + 2)
        for mh in range(2):
            even, odd = [
                stencil(
                    g[mh, x + k, here], g[mh, x + k - 1, here], g[mh, x + k + 1, here],
                    g[mh, x + k, behind], g[mh, x + k, ahead], coef_ref[x + k - 1, y0:y1], sx, sy,
                ).reshape(8 * (y1 - y0), 128)
                for k in range(2)
            ]
            to = 4 * h + 2 * mh
            snd[to, pair, rows] = jnp.where(low, even, pltpu.roll(odd, 64, 1)).astype(BF16)
            snd[to + 1, pair, rows] = jnp.where(low, pltpu.roll(even, 64, 1), odd).astype(BF16)

    def parts(half_of):
        inner = pl.ds(1 - half_of, 3)
        return [
            (inner, slice(16, 112)), (inner, slice(0, 16)), (inner, slice(112, 128)),
            (3 * half_of, slice(0, 128)),
        ]

    def main_copy(part, to):
        pairs, rows = parts(to // 4)[part]
        return remote(
            snd.at[to, pairs, rows], rcv.at[slot, pairs, rows], main_send.at[part, to],
            main_recv.at[part, slot], ring, to,
        )

    def send(part):
        loop(1, 8, lambda j: main_copy(part, lax.rem(slot + j, 8)).start())

    for h in range(2):
        loop(1 - h, 4 - h, lambda pair, h=h: step_pair(h, pair, 2, 14))
        skip = half if h else 1 - half
        loop(skip, 4, lambda j, h=h: main_copy(0, 4 * h + lax.rem(mem + j, 4)).start())
    for copy in edges:
        copy.wait()
    for mh in range(2):
        lanes = slice(mh * 128, mh * 128 + 128)
        g[mh, 17, 1:17] = edge_in[0, :, lanes].astype(F32).reshape(16, 8, 128)
        g[mh, 0, 1:17] = edge_in[1, :, lanes].astype(F32).reshape(16, 8, 128)
        g[mh, 1:17, 17] = edge_in[2, :, lanes].astype(F32).reshape(16, 8, 128)
        g[mh, 1:17, 0] = edge_in[3, :, lanes].astype(F32).reshape(16, 8, 128)
    for part, y0 in ((1, 0), (2, 14)):
        for h in range(2):
            loop(1 - h, 4 - h, lambda pair, h=h, y0=y0: step_pair(h, pair, y0, y0 + 2))
        send(part)
    for h in range(2):
        step_pair(h, 3 * h, 0, 16)
    send(3)
    own = pltpu.make_async_copy(snd.at[slot], rcv.at[slot], own_sem)
    own.start()

    def pick_rows(i):
        row = lax.broadcasted_iota(jnp.int32, (128, 128), 0) + 128 * i
        lane = lax.broadcasted_iota(jnp.int32, (128, 128), 1)
        level = jnp.where(row // 8 == lane, lax.rem(row, 8), 8)
        rows = pl.ds(pl.multiple_of(128 * i, 128), 128)
        for f in range(8):
            pick[rows, f * 128 : f * 128 + 128] = jnp.where(level == f, 1.0, 0.0).astype(BF16)

    loop(0, 8, pick_rows)
    own.wait()

    def wait_part(part):
        def wait(j):
            frm = lax.rem(slot + j, 8)
            pairs, rows = parts(half)[part]
            remote(
                snd.at[frm, pairs, rows], rcv.at[frm, pairs, rows], main_send.at[part, frm],
                main_recv.at[part, frm], ring, frm,
            ).wait_recv()

        loop(1, 8, wait)

    def result_pair(pair):
        block = rcv[:, pair].reshape(1024, 128)
        result = lax.dot_general(block, pick[...], TN, preferred_element_type=F32).astype(BF16)
        out_ref[2 * pair] = result[:64]
        out_ref[2 * pair + 1] = result[64:]

    for part in range(3):
        wait_part(part)
    loop(1 - half, 4 - half, result_pair)
    wait_part(3)
    result_pair(3 * half)
    for part in range(4):
        loop(1, 8, lambda j, part=part: main_copy(part, lax.rem(slot + j, 8)).wait_send())


def vmem(count):
    return [pl.BlockSpec(memory_space=pltpu.VMEM)] * count


def local(member_collection, spreading_ratio, transport_ratio_row, transport_ratio_column, obs_patch):
    rings = lax.axis_size("tile") // 2
    DMA = pltpu.SemaphoreType.DMA
    obs = obs_patch.reshape(1, 256)

    def shape(dims, dtype=F32):
        return jax.ShapeDtypeStruct(dims, dtype)

    anom, cen, avg, wt, coef = pl.pallas_call(
        lambda *refs: forecast_kernel(rings, *refs),
        out_shape=[
            shape((4, 8, 64, 256), BF16),
            shape((4, 8, 64, 128)),
            shape((4, 264, 128)),
            shape((6, 8, 128)),
            shape((16, 16, 8, 128)),
        ],
        in_specs=[pl.BlockSpec(memory_space=pltpu.HBM)] * 3
        + [pl.BlockSpec(memory_space=pltpu.SMEM)] * 2,
        out_specs=vmem(5),
        scratch_shapes=[
            pltpu.VMEM((64, 8, 8, 128), BF16),
            pltpu.VMEM((8, 8, 128), F32),
            pltpu.VMEM((1, 256), jnp.int32),
            pltpu.VMEM((512, 1024), BF16),
            pltpu.VMEM((128, 1024), BF16),
            pltpu.VMEM((1024, 1024), BF16),
            pltpu.VMEM((4, 1056, 128), BF16),
            pltpu.VMEM((10, 4, 160, 128), BF16),
            pltpu.VMEM((2, 20, 20, 8, 128), F32),
            pltpu.VMEM((2, 18, 18, 8, 128), F32),
            pltpu.VMEM((20, 20, 8, 128), F32),
            pltpu.VMEM((32, 8, 128), F32),
            pltpu.VMEM((rings, 8, 128), F32),
            pltpu.VMEM((rings, 8, 128), F32),
            pltpu.VMEM((8, 8, 128), F32),
            pltpu.VMEM((4, 264, 128), F32),
            pltpu.VMEM((2, 264, 128), F32),
            pltpu.VMEM((2, 264, 128), F32),
            pltpu.VMEM((2, 264, 128), F32),
            pltpu.VMEM((2, 264, 128), F32),
            DMA((3,)),
            DMA((6, 8)),
            DMA((6, 8)),
            DMA((2,)),
            DMA((2,)),
            DMA((3,)),
            DMA((3,)),
            DMA((rings,)),
            DMA((rings,)),
            DMA((8,)),
            DMA((8,)),
            DMA((8,)),
            DMA((8,)),
        ],
        compiler_params=pltpu.CompilerParams(
            collective_id=0, has_side_effects=True, vmem_limit_bytes=VMEM_LIMIT
        ),
    )(member_collection, spreading_ratio, obs, transport_ratio_row, transport_ratio_column)

    square = shape((4, 256, 256), BF16)
    yh, yl, zh, zl, last = pl.pallas_call(
        analysis_kernel,
        out_shape=[square, square, square, square, shape((12, 8, 128))],
        in_specs=vmem(2),
        out_specs=vmem(5),
        scratch_shapes=[pltpu.VMEM((4, 256, 256), BF16)] * 2,
        compiler_params=pltpu.CompilerParams(vmem_limit_bytes=16 * 1024 * 1024),
    )(avg, wt)

    out = pl.pallas_call(
        lambda *refs: return_kernel(rings, *refs),
        out_shape=shape((8, 64, 1024), BF16),
        in_specs=vmem(9),
        out_specs=pl.BlockSpec(memory_space=pltpu.VMEM),
        scratch_shapes=[
            pltpu.VMEM((4, 256, 256), BF16),
            pltpu.VMEM((4, 256, 256), BF16),
            pltpu.VMEM((2, 18, 18, 8, 128), F32),
            pltpu.VMEM((4, 128, 256), BF16),
            pltpu.VMEM((4, 128, 256), BF16),
            pltpu.VMEM((8, 4, 128, 128), BF16),
            pltpu.VMEM((8, 4, 128, 128), BF16),
            pltpu.VMEM((1024, 1024), BF16),
            DMA((4,)),
            DMA((4,)),
            DMA((4, 8)),
            DMA((4, 8)),
            DMA,
        ],
        compiler_params=pltpu.CompilerParams(
            collective_id=1, has_side_effects=True, vmem_limit_bytes=24 * 1024 * 1024
        ),
    )(anom, cen, yh, yl, zh, zl, last, coef, wt)
    return jnp.transpose(out.reshape(8, 64, 8, 128), (1, 2, 0, 3))


def solution(mesh):
    placed = (P("mem", None, "tile", None), P(None, "tile", None), P(), P(), P(("mem", "tile")))
    return jax.shard_map(
        local, mesh=mesh, in_specs=placed, out_specs=P("mem", None, "tile", None), check_vma=False
    )
```

```python
import jax
import jax.numpy as jnp
from jax import lax
from jax.experimental import pallas as pl
from jax.experimental.pallas import tpu as pltpu
from jax.sharding import PartitionSpec as P

F32 = jnp.float32
BF16 = jnp.bfloat16
MESH = pl.DeviceIdType.MESH
VMEM_LIMIT = 50 * 1024 * 1024
NS_ITERS = 14
PLAIN_NORM = 2500.0
CONVERGED = 1e-5
NT = (((1,), (1,)), ((), ()))
TN = (((0,), (0,)), ((), ()))


def place():
    tile = lax.axis_index("tile")
    mem = lax.axis_index("mem")
    ring = tile // 2
    half = lax.rem(tile, 2)
    return ring, half, mem, half * 4 + mem


def target(ring, slot):
    return {"mem": lax.rem(slot, 4), "tile": 2 * ring + slot // 4}


def remote(src, dst, send_sem, recv_sem, ring, slot):
    return pltpu.make_async_remote_copy(
        src_ref=src,
        dst_ref=dst,
        send_sem=send_sem,
        recv_sem=recv_sem,
        device_id=target(ring, slot),
        device_id_type=MESH,
    )


def signal(sem, ring, slot):
    pl.semaphore_signal(sem, inc=1, device_id=target(ring, slot), device_id_type=MESH)


def stencil(c, bx, ax, by, ay, s, sx, sy):
    return c - sx * (c - bx) - sy * (c - by) + s * (ax + bx + ay + by - 4.0 * c)


def rounded(x):
    return x.astype(BF16).astype(F32)


def loop(lower, upper, body):
    def step(i, carry):
        body(i)
        return carry

    lax.fori_loop(lower, upper, step, 0)


def forecast_kernel(
    rings,
    u_hbm,
    spread_hbm,
    obs_hbm,
    sx_ref,
    sy_ref,
    anom_ref,
    cen_ref,
    avg_ref,
    wt_ref,
    coef_ref,
    raw,
    spread_in,
    obs_in,
    flat,
    state,
    pick,
    wide,
    rcv,
    u0,
    u1,
    coef,
    spr,
    cst,
    cra,
    crb,
    gpk,
    gab,
    gbe,
    gle,
    gri,
    load_sem,
    block_send,
    block_recv,
    halo_send,
    halo_recv,
    spr_send,
    spr_recv,
    cnt_send,
    cnt_recv,
    sum_send,
    sum_recv,
    gram_send,
    gram_recv,
):
    ring, half, mem, slot = place()
    above = lax.rem(ring + rings - 1, rings)
    below = lax.rem(ring + 1, rings)

    barrier = pltpu.get_barrier_semaphore()
    loop(1, 8, lambda j: signal(barrier, ring, lax.rem(slot + j, 8)))
    loop(1, rings, lambda j: signal(barrier, lax.rem(ring + j, rings), slot))
    load_raw = pltpu.make_async_copy(u_hbm, raw, load_sem.at[0])
    load_spread = pltpu.make_async_copy(spread_hbm, spread_in, load_sem.at[1])
    load_obs = pltpu.make_async_copy(obs_hbm, obs_in, load_sem.at[2])
    load_raw.start()
    load_spread.start()
    load_obs.start()

    def pick_rows(i):
        row = lax.broadcasted_iota(jnp.int32, (128, 128), 0) + 128 * i
        lane = lax.broadcasted_iota(jnp.int32, (128, 128), 1)
        level = jnp.where(row // 8 == lane, lax.rem(row, 8), 8)
        rows = pl.ds(pl.multiple_of(128 * i, 128), 128)
        for f in range(8):
            pick[rows, f * 128 : f * 128 + 128] = jnp.where(level == f, 1.0, 0.0).astype(BF16)

    loop(0, 8, pick_rows)

    load_raw.wait()
    for f in range(8):
        flat[:, f * 128 : f * 128 + 128] = raw[:, f].astype(F32).reshape(512, 128).astype(BF16)

    def pair_of(t, side):
        return t + side * (3 - 2 * t)

    def place_of(t, side):
        return 1 + 4 * side + pair_of(t, side)

    def turn_pair(t):
        pair = pair_of(t, half)
        k = lax.broadcasted_iota(jnp.int32, (128, 512), 1)
        r = lax.broadcasted_iota(jnp.int32, (128, 512), 0) + 128 * pair
        turn = jnp.where(k == lax.rem(r, 64) * 8 + r // 64, 1.0, 0.0).astype(BF16)
        state[...] = jnp.dot(turn, flat[...], preferred_element_type=F32).astype(BF16)
        block = lax.dot_general(
            pick[...], state[...], NT, preferred_element_type=F32
        ).astype(BF16)
        wide[pair, 16:1040] = block
        wide[pair, 0:16] = block[1008:1024]
        wide[pair, 1040:1056] = block[0:16]

    parts = [(0, 0, 160), (1, 0, 160), (2, 0, 96), (3, 0, 96), (2, 96, 160), (3, 96, 160)]

    def block_copy(q, to):
        t, low, high = parts[q]
        return remote(
            wide.at[
                pair_of(t, half), pl.ds(pl.multiple_of(128 * to + low, 16), high - low)
            ],
            rcv.at[place_of(t, half), mem, low:high], block_send.at[q, to],
            block_recv.at[q, slot], ring, to,
        )

    def own_copy(q):
        t, low, high = parts[q]
        return pltpu.make_async_copy(
            wide.at[
                pair_of(t, half), pl.ds(pl.multiple_of(128 * slot + low, 16), high - low)
            ],
            rcv.at[place_of(t, half), mem, low:high], block_recv.at[q, slot],
        )

    def send_blocks(q):
        loop(1, 8, lambda j: block_copy(q, lax.rem(slot + j, 8)).start())
        own_copy(q).start()

    def wait_blocks(q):
        own_copy(q).wait()
        t, low, high = parts[q]

        def wait(j):
            frm = lax.rem(slot + j, 8)
            remote(
                wide.at[0, low:high], rcv.at[place_of(t, frm // 4), lax.rem(frm, 4), low:high],
                block_send.at[q, frm], block_recv.at[q, frm], ring, frm,
            ).wait_recv()

        loop(1, 8, wait)

    turn_pair(0)
    pl.semaphore_wait(barrier, 7 + rings - 1)
    send_blocks(0)

    load_spread.wait()
    mine = 8 + 8 * half
    for x in range(8):
        spr[mine + x] = spread_in[:, x, :]
    spr_here = remote(
        spr.at[pl.ds(mine, 8)], spr.at[pl.ds(mine, 8)], spr_send.at[0], spr_recv.at[0],
        ring, (1 - half) * 4 + mem,
    )
    spr_here.start()

    turn_pair(1)
    send_blocks(1)
    turn_pair(2)

    load_obs.wait()
    obs = obs_in[...]
    in_ring = lax.broadcasted_iota(jnp.int32, (rings, 256), 0) == obs // 32
    in_patch = lax.broadcasted_iota(jnp.int32, (128, 256), 0) == lax.rem(obs, 32)
    tally = lax.dot_general(
        in_ring.astype(F32).astype(BF16), in_patch.astype(F32).astype(BF16), NT,
        preferred_element_type=F32,
    )
    for r in range(rings):
        cst[r] = jnp.broadcast_to(tally[r : r + 1, :], (8, 128))
    cra[ring] = cst[ring]

    def count_copy(j):
        to = lax.rem(ring + j, rings)
        return remote(cst.at[to], cra.at[ring], cnt_send.at[j], cnt_recv.at[ring], to, slot)

    wait_blocks(0)
    halos = [
        remote(rcv.at[1], rcv.at[9], halo_send.at[0], halo_recv.at[0], above, slot),
        remote(rcv.at[8], rcv.at[0], halo_send.at[1], halo_recv.at[1], below, slot),
    ]
    for copy in halos:
        copy.start()
    send_blocks(2)
    loop(1, rings, lambda j: count_copy(j).start())

    spr_here.wait_send()
    other = 16 - 8 * half
    remote(
        spr.at[pl.ds(other, 8)], spr.at[pl.ds(other, 8)], spr_send.at[0], spr_recv.at[0],
        ring, (1 - half) * 4 + mem,
    ).wait_recv()
    spr_far = [
        remote(spr.at[8:10], spr.at[24:26], spr_send.at[1], spr_recv.at[1], above, slot),
        remote(spr.at[22:24], spr.at[6:8], spr_send.at[2], spr_recv.at[2], below, slot),
    ]
    for copy in spr_far:
        copy.start()

    turn_pair(3)
    def spread_row(i):
        lane = lax.broadcasted_iota(jnp.int32, (20, 8, 128), 2)
        column = lax.rem(
            lax.broadcasted_iota(jnp.int32, (20, 8, 128), 0) + 16 * slot + 126, 128
        )
        values = jnp.where(lane == column, spr[i + 6][None], 0.0)
        coef[i] = jnp.broadcast_to(jnp.sum(values, axis=2, keepdims=True), (20, 8, 128))

    loop(2, 18, spread_row)

    def coef_row(i):
        coef_ref[i] = coef[i + 2, 2:18]

    loop(0, 16, coef_row)
    sublane = lax.broadcasted_iota(jnp.int32, (8, 128), 0)
    for k, ref in enumerate((sx_ref, sy_ref)):
        speed = jnp.zeros((8, 128), F32)
        for f in range(8):
            speed = jnp.where(sublane == f, ref[f], speed)
        wt_ref[4 + k] = speed

    loop(1, 8, lambda j: block_copy(1, lax.rem(slot + j, 8)).wait_send())
    for q in (3, 4, 5):
        send_blocks(q)

    def unshuffle(pair, y0=0, y1=20):
        low = lax.broadcasted_iota(jnp.int32, (8 * (y1 - y0), 128), 1) < 64
        rows = slice(8 * y0, 8 * y1)
        for mh in range(2):
            r0 = rcv[pair, 2 * mh, rows].astype(F32)
            r1 = rcv[pair, 2 * mh + 1, rows].astype(F32)
            even = jnp.where(low, r0, pltpu.roll(r1, 64, 1))
            odd = jnp.where(low, pltpu.roll(r0, 64, 1), r1)
            u0[mh, 2 * pair, y0:y1] = even.reshape(y1 - y0, 8, 128)
            u0[mh, 2 * pair + 1, y0:y1] = odd.reshape(y1 - y0, 8, 128)

    unshuffle(1)
    unshuffle(8)
    sx = wt_ref[4][None]
    sy = wt_ref[5][None]

    def first(x, y0=0, y1=18):
        s = coef[x, y0 + 1 : y1 + 1]
        here, behind, ahead = slice(y0 + 1, y1 + 1), slice(y0, y1), slice(y0 + 2, y1 + 2)
        for mh in range(2):
            u1[mh, x - 1, y0:y1] = rounded(
                stencil(
                    u0[mh, x, here], u0[mh, x - 1, here], u0[mh, x + 1, here],
                    u0[mh, x, behind], u0[mh, x, ahead], s, sx, sy,
                )
            )

    def second(row, c):
        h, i = row // 8, lax.rem(row, 8)
        x, y = row + 1, 8 * c + 1
        s = coef[x + 1, y + 1 : y + 9]
        prior = [
            rounded(
                stencil(
                    u1[mh, x, y : y + 8], u1[mh, x - 1, y : y + 8], u1[mh, x + 1, y : y + 8],
                    u1[mh, x, y - 1 : y + 7], u1[mh, x, y + 1 : y + 9], s, sx, sy,
                )
            )
            for mh in range(2)
        ]
        centre = jnp.sum(prior[0] + prior[1], axis=2, keepdims=True) * (1.0 / 256.0)
        centre = jnp.broadcast_to(centre, (8, 8, 128))
        cen_ref[2 * h + c, i] = centre.reshape(64, 128)
        for mh in range(2):
            anom_ref[2 * h + c, i, :, mh * 128 : mh * 128 + 128] = (
                (prior[mh] - centre).reshape(64, 128).astype(BF16)
            )

    def firsts(low, high, y0=0, y1=18):
        def both(k):
            first(low + k, y0, y1)
            first(high + k, y0, y1)

        loop(0, 2, both)

    def seconds(low, high, c):
        def both(k):
            second(low + k, c)
            second(high + k, c)

        loop(0, 2, both)

    wait_blocks(1)
    unshuffle(2)
    unshuffle(7)
    firsts(3, 15)
    for copy in spr_far:
        copy.wait()
    for i in (0, 1, 18, 19):
        spread_row(i)
    for copy in halos:
        copy.wait()
    unshuffle(0)
    unshuffle(9)
    firsts(1, 17)
    for c in range(2):
        seconds(0, 14, c)

    row = lax.broadcasted_iota(jnp.int32, (128, 128), 0)
    col = lax.broadcasted_iota(jnp.int32, (128, 128), 1)
    left = lax.rem(slot + 7, 8)
    right = lax.rem(slot + 1, 8)
    copies = []

    def sum_copy(j):
        return remote(
            crb.at[slot], crb.at[slot], sum_send.at[j], sum_recv.at[slot], ring,
            lax.rem(slot + j, 8),
        )

    for c in range(2):
        if c:
            def count_wait(j):
                frm = lax.rem(ring + j, rings)
                remote(cst.at[0], cra.at[frm], cnt_send.at[j], cnt_recv.at[frm], frm, slot).wait_recv()

            loop(1, rings, count_wait)
            total = cra[0]
            for r in range(1, rings):
                total = total + cra[r]
            crb[slot] = total

            loop(1, 8, lambda j: sum_copy(j).start())
        (y0, y1), (z0, z1) = (((0, 12), (0, 10)), ((12, 20), (10, 18)))[c]
        wait_blocks(2 + 2 * c)
        unshuffle(3, y0, y1)
        unshuffle(6, y0, y1)
        firsts(5, 13, z0, z1)
        seconds(2, 12, c)
        wait_blocks(3 + 2 * c)
        unshuffle(4, y0, y1)
        unshuffle(5, y0, y1)
        loop(7, 13, lambda x, z0=z0, z1=z1: first(x, z0, z1))
        for h in range(2):
            p = 2 * h + c
            loop(4 + 4 * h, 8 + 4 * h, lambda row, c=c: second(row, c))
            a = anom_ref[p].reshape(512, 256)
            g = lax.dot_general(a, a, TN, preferred_element_type=F32) * (1.0 / 512.0)
            last = g[128:, 128:]
            gpk[p, 0:128] = g[:128, 128:]
            gpk[p, 128:256] = jnp.where(row >= col, g[:128, :128], last)
            diag = jnp.sum(jnp.where(row == col, last, 0.0), axis=0, keepdims=True)
            gpk[p, 256:264] = jnp.broadcast_to(diag, (8, 128))
            vertical = (gab, below) if h else (gbe, above)
            sideways = (gle, right) if c else (gri, left)
            pair = [
                remote(
                    gpk.at[p], vertical[0].at[c], gram_send.at[2 * p], gram_recv.at[2 * p],
                    vertical[1], slot,
                ),
                remote(
                    gpk.at[p], sideways[0].at[h], gram_send.at[2 * p + 1],
                    gram_recv.at[2 * p + 1], ring, sideways[1],
                ),
            ]
            for copy in pair:
                copy.start()
            copies += pair

    def sum_wait(j):
        frm = lax.rem(slot + j, 8)
        remote(crb.at[slot], crb.at[frm], sum_send.at[j], sum_recv.at[frm], ring, frm).wait_recv()

    loop(1, 8, sum_wait)
    counts = crb[0]
    for k in range(1, 8):
        counts = counts + crb[k]
    lane = lax.broadcasted_iota(jnp.int32, (8, 128), 1)
    for h in range(2):
        for c in range(2):
            chosen = jnp.where(lane == h * 16 + 2 * slot + c, counts, 0.0)
            count = jnp.sum(chosen, axis=1, keepdims=True)
            wt_ref[2 * h + c] = jnp.broadcast_to(count / (count + 16.0), (8, 128))
    loop(1, rings, lambda j: count_copy(j).wait_send())
    loop(1, 8, lambda j: sum_copy(j).wait_send())
    for q in (0, 2, 3, 4, 5):
        loop(1, 8, lambda j, q=q: block_copy(q, lax.rem(slot + j, 8)).wait_send())
    for copy in copies:
        copy.wait()
    for c in range(2):
        for h in range(2):
            p = 2 * h + c
            up = gpk[c] if h else gab[c]
            down = gbe[c] if h else gpk[2 + c]
            lft = gpk[2 * h] if c else gle[h]
            rgt = gri[h] if c else gpk[2 * h + 1]
            avg_ref[p] = (2.0 * gpk[p] + up + down + lft + rgt) * (1.0 / 6.0)


def split(x):
    hi = x.astype(BF16)
    return hi, (x - hi.astype(F32)).astype(BF16)


def product(a, b):
    (ah, al), (bh, bl) = a, b
    return (
        jnp.dot(ah, bh, preferred_element_type=F32)
        + jnp.dot(ah, bl, preferred_element_type=F32)
        + jnp.dot(al, bh, preferred_element_type=F32)
    )


def analysis_kernel(avg_ref, wt_ref, yh, yl, zh, zl, last_ref, fh, fl):
    row = lax.broadcasted_iota(jnp.int32, (256, 256), 0)
    col = lax.broadcasted_iota(jnp.int32, (256, 256), 1)
    diagonal = row == col
    identity = jnp.where(diagonal, 1.0, 0.0)
    low = row[:128, :128] >= col[:128, :128]
    on = row[:128, :128] == col[:128, :128]

    def coefs(low_end, plain):
        alpha2 = jnp.where(plain, 1.0, 3.0 / (1.0 + low_end + low_end * low_end))
        alpha = jnp.sqrt(alpha2)
        reach = alpha * low_end
        after = 0.5 * reach * (3.0 - reach * reach)
        return 1.5 * alpha, 0.5 * alpha * alpha2, jnp.minimum(after, 1.0)

    ends, plains, scales = [], [], []
    for p in range(4):
        packed = avg_ref[p]
        upper_right = packed[0:128]
        both = packed[128:256]
        turned = both.T
        first = jnp.where(low, both, turned)
        last = jnp.where(on, jnp.broadcast_to(packed[256:257], (128, 128)), jnp.where(low, turned, both))
        averaged = jnp.concatenate(
            [
                jnp.concatenate([first, upper_right], axis=1),
                jnp.concatenate([upper_right.T, last], axis=1),
            ],
            axis=0,
        )
        system = identity + wt_ref[p, 0:1, 0:1] * averaged
        squares = jnp.sum(jnp.sum(system * system, axis=1, keepdims=True), axis=0, keepdims=True)
        norm = jnp.sqrt(squares)
        rows = jnp.max(
            jnp.sum(jnp.abs(system), axis=0, keepdims=True), axis=1, keepdims=True
        )
        plain = norm > PLAIN_NORM
        scale = jnp.where(plain, norm, jnp.minimum(norm, rows * 1.000001))
        start = system / scale
        low_end = jnp.where(plain, 0.0, jnp.sqrt(1.0 / scale) * 0.9999)
        a, b, after = coefs(low_end, plain)
        factor = a * identity - b * start
        y = product(split(start), split(factor))
        yh[p], yl[p] = split(y)
        zh[p], zl[p] = split(factor)
        ends.append(after)
        plains.append(plain)
        scales.append(scale)

    def some_left(ends, plains, k):
        left = jnp.zeros((1, 1), F32)
        for end, plain in zip(ends, plains):
            _, _, after = coefs(end, plain)
            todo = jnp.where(plain, jnp.where(k + 1 < NS_ITERS, 1.0, 0.0), jnp.where(1.0 - after > CONVERGED, 1.0, 0.0))
            left = jnp.maximum(left, todo)
        return jnp.max(left) > 0.5

    def body(carry):
        k, _, *ends = carry
        following = []
        for p in range(4):
            a, b, after = coefs(ends[p], plains[p])
            t = product((zh[p], zl[p]), (yh[p], yl[p]))
            fh[p], fl[p] = split(a * identity - b * t)
            following.append(after)
        for p in range(4):
            factor = (fh[p], fl[p])
            ny = product((yh[p], yl[p]), factor)
            nz = product(factor, (zh[p], zl[p]))
            yh[p], yl[p] = split(ny)
            zh[p], zl[p] = split(nz)
        return (k + 1, some_left(following, plains, k + 1), *following)

    last_k, _, *ends = lax.while_loop(
        lambda carry: carry[1], body, (1, some_left(ends, plains, 1), *ends)
    )
    for p in range(4):
        a, b, after = coefs(ends[p], plains[p])
        middle = jnp.where(plains[p], 1.0, 0.5 + 0.5 * after)
        for k, value in enumerate((a, b, 1.0 / (middle * jnp.sqrt(scales[p])))):
            last_ref[3 * p + k] = jnp.broadcast_to(value, (8, 128))


def return_kernel(
    rings,
    anom_ref,
    cen_ref,
    yh,
    yl,
    zh,
    zl,
    last_ref,
    coef_ref,
    wt_ref,
    out_ref,
    fh,
    fl,
    g,
    edge_out,
    edge_in,
    snd,
    rcv,
    pick,
    edge_send,
    edge_recv,
    main_send,
    main_recv,
    own_sem,
):
    ring, half, mem, slot = place()
    above = lax.rem(ring + rings - 1, rings)
    below = lax.rem(ring + 1, rings)
    left = lax.rem(slot + 7, 8)
    right = lax.rem(slot + 1, 8)
    barrier = pltpu.get_barrier_semaphore()
    loop(1, 8, lambda j: signal(barrier, ring, lax.rem(slot + j, 8)))
    signal(barrier, above, slot)
    signal(barrier, below, slot)

    diagonal = lax.broadcasted_iota(jnp.int32, (256, 256), 0) == lax.broadcasted_iota(
        jnp.int32, (256, 256), 1
    )
    for p in range(4):
        t = product((zh[p], zl[p]), (yh[p], yl[p]))
        a, b = last_ref[3 * p, 0:1, 0:1], last_ref[3 * p + 1, 0:1, 0:1]
        fh[p], fl[p] = split(jnp.where(diagonal, a, 0.0) - b * t)
    for p in range(4):
        inverse = product((fh[p], fl[p]), (zh[p], zl[p]))
        weights = (inverse * last_ref[3 * p + 2, 0:1, 0:1]).astype(BF16)
        update = jnp.dot(anom_ref[p].reshape(512, 256), weights, preferred_element_type=F32)
        centre = cen_ref[p].reshape(512, 128)
        h, c = p // 2, p % 2
        for mh in range(2):
            value = rounded(centre + update[:, mh * 128 : mh * 128 + 128])
            g[mh, 8 * h + 1 : 8 * h + 9, 8 * c + 1 : 8 * c + 9] = value.reshape(8, 8, 8, 128)
    for mh in range(2):
        lanes = slice(mh * 128, mh * 128 + 128)
        edge_out[0, :, lanes] = g[mh, 1, 1:17].reshape(128, 128).astype(BF16)
        edge_out[1, :, lanes] = g[mh, 16, 1:17].reshape(128, 128).astype(BF16)
        edge_out[2, :, lanes] = g[mh, 1:17, 1].reshape(128, 128).astype(BF16)
        edge_out[3, :, lanes] = g[mh, 1:17, 16].reshape(128, 128).astype(BF16)
    pl.semaphore_wait(barrier, 9)
    edges = [
        remote(edge_out.at[k], edge_in.at[k], edge_send.at[k], edge_recv.at[k], to_ring, to_slot)
        for k, (to_ring, to_slot) in enumerate(
            [(above, slot), (below, slot), (ring, left), (ring, right)]
        )
    ]
    for copy in edges:
        copy.start()
    sx = wt_ref[4][None]
    sy = wt_ref[5][None]

    def step_pair(h, pair, y0, y1):
        x = 8 * h + 2 * pair + 1
        rows = slice(8 * y0, 8 * y1)
        low = lax.broadcasted_iota(jnp.int32, (8 * (y1 - y0), 128), 1) < 64
        here, behind, ahead = slice(y0 + 1, y1 + 1), slice(y0, y1), slice(y0 + 2, y1 + 2)
        for mh in range(2):
            even, odd = [
                stencil(
                    g[mh, x + k, here], g[mh, x + k - 1, here], g[mh, x + k + 1, here],
                    g[mh, x + k, behind], g[mh, x + k, ahead], coef_ref[x + k - 1, y0:y1], sx, sy,
                ).reshape(8 * (y1 - y0), 128)
                for k in range(2)
            ]
            to = 4 * h + 2 * mh
            snd[to, pair, rows] = jnp.where(low, even, pltpu.roll(odd, 64, 1)).astype(BF16)
            snd[to + 1, pair, rows] = jnp.where(low, pltpu.roll(even, 64, 1), odd).astype(BF16)

    def parts(half_of):
        inner = pl.ds(1 - half_of, 3)
        return [
            (inner, slice(16, 112)), (inner, slice(0, 16)), (inner, slice(112, 128)),
            (3 * half_of, slice(0, 128)),
        ]

    def main_copy(part, to):
        pairs, rows = parts(to // 4)[part]
        return remote(
            snd.at[to, pairs, rows], rcv.at[slot, pairs, rows], main_send.at[part, to],
            main_recv.at[part, slot], ring, to,
        )

    def send(part):
        loop(1, 8, lambda j: main_copy(part, lax.rem(slot + j, 8)).start())

    for h in range(2):
        loop(1 - h, 4 - h, lambda pair, h=h: step_pair(h, pair, 2, 14))
        skip = half if h else 1 - half
        loop(skip, 4, lambda j, h=h: main_copy(0, 4 * h + lax.rem(mem + j, 4)).start())
    for copy in edges:
        copy.wait()
    for mh in range(2):
        lanes = slice(mh * 128, mh * 128 + 128)
        g[mh, 17, 1:17] = edge_in[0, :, lanes].astype(F32).reshape(16, 8, 128)
        g[mh, 0, 1:17] = edge_in[1, :, lanes].astype(F32).reshape(16, 8, 128)
        g[mh, 1:17, 17] = edge_in[2, :, lanes].astype(F32).reshape(16, 8, 128)
        g[mh, 1:17, 0] = edge_in[3, :, lanes].astype(F32).reshape(16, 8, 128)
    for part, y0 in ((1, 0), (2, 14)):
        for h in range(2):
            loop(1 - h, 4 - h, lambda pair, h=h, y0=y0: step_pair(h, pair, y0, y0 + 2))
        send(part)
    for h in range(2):
        step_pair(h, 3 * h, 0, 16)
    send(3)
    own = pltpu.make_async_copy(snd.at[slot], rcv.at[slot], own_sem)
    own.start()

    def pick_rows(i):
        row = lax.broadcasted_iota(jnp.int32, (128, 128), 0) + 128 * i
        lane = lax.broadcasted_iota(jnp.int32, (128, 128), 1)
        level = jnp.where(row // 8 == lane, lax.rem(row, 8), 8)
        rows = pl.ds(pl.multiple_of(128 * i, 128), 128)
        for f in range(8):
            pick[rows, f * 128 : f * 128 + 128] = jnp.where(level == f, 1.0, 0.0).astype(BF16)

    loop(0, 8, pick_rows)
    own.wait()

    def wait_part(part):
        def wait(j):
            frm = lax.rem(slot + j, 8)
            pairs, rows = parts(half)[part]
            remote(
                snd.at[frm, pairs, rows], rcv.at[frm, pairs, rows], main_send.at[part, frm],
                main_recv.at[part, frm], ring, frm,
            ).wait_recv()

        loop(1, 8, wait)

    def result_pair(pair):
        block = rcv[:, pair].reshape(1024, 128)
        result = lax.dot_general(block, pick[...], TN, preferred_element_type=F32).astype(BF16)
        out_ref[2 * pair] = result[:64]
        out_ref[2 * pair + 1] = result[64:]

    for part in range(3):
        wait_part(part)
    loop(1 - half, 4 - half, result_pair)
    wait_part(3)
    result_pair(3 * half)
    for part in range(4):
        loop(1, 8, lambda j, part=part: main_copy(part, lax.rem(slot + j, 8)).wait_send())


def vmem(count):
    return [pl.BlockSpec(memory_space=pltpu.VMEM)] * count


def local(member_collection, spreading_ratio, transport_ratio_row, transport_ratio_column, obs_patch):
    rings = lax.axis_size("tile") // 2
    DMA = pltpu.SemaphoreType.DMA
    obs = obs_patch.reshape(1, 256)

    def shape(dims, dtype=F32):
        return jax.ShapeDtypeStruct(dims, dtype)

    anom, cen, avg, wt, coef = pl.pallas_call(
        lambda *refs: forecast_kernel(rings, *refs),
        out_shape=[
            shape((4, 8, 64, 256), BF16),
            shape((4, 8, 64, 128)),
            shape((4, 264, 128)),
            shape((6, 8, 128)),
            shape((16, 16, 8, 128)),
        ],
        in_specs=[pl.BlockSpec(memory_space=pltpu.HBM)] * 3
        + [pl.BlockSpec(memory_space=pltpu.SMEM)] * 2,
        out_specs=vmem(5),
        scratch_shapes=[
            pltpu.VMEM((64, 8, 8, 128), BF16),
            pltpu.VMEM((8, 8, 128), F32),
            pltpu.VMEM((1, 256), jnp.int32),
            pltpu.VMEM((512, 1024), BF16),
            pltpu.VMEM((128, 1024), BF16),
            pltpu.VMEM((1024, 1024), BF16),
            pltpu.VMEM((4, 1056, 128), BF16),
            pltpu.VMEM((10, 4, 160, 128), BF16),
            pltpu.VMEM((2, 20, 20, 8, 128), F32),
            pltpu.VMEM((2, 18, 18, 8, 128), F32),
            pltpu.VMEM((20, 20, 8, 128), F32),
            pltpu.VMEM((32, 8, 128), F32),
            pltpu.VMEM((rings, 8, 128), F32),
            pltpu.VMEM((rings, 8, 128), F32),
            pltpu.VMEM((8, 8, 128), F32),
            pltpu.VMEM((4, 264, 128), F32),
            pltpu.VMEM((2, 264, 128), F32),
            pltpu.VMEM((2, 264, 128), F32),
            pltpu.VMEM((2, 264, 128), F32),
            pltpu.VMEM((2, 264, 128), F32),
            DMA((3,)),
            DMA((6, 8)),
            DMA((6, 8)),
            DMA((2,)),
            DMA((2,)),
            DMA((3,)),
            DMA((3,)),
            DMA((rings,)),
            DMA((rings,)),
            DMA((8,)),
            DMA((8,)),
            DMA((8,)),
            DMA((8,)),
        ],
        compiler_params=pltpu.CompilerParams(
            collective_id=0, has_side_effects=True, vmem_limit_bytes=VMEM_LIMIT
        ),
    )(member_collection, spreading_ratio, obs, transport_ratio_row, transport_ratio_column)

    square = shape((4, 256, 256), BF16)
    yh, yl, zh, zl, last = pl.pallas_call(
        analysis_kernel,
        out_shape=[square, square, square, square, shape((12, 8, 128))],
        in_specs=vmem(2),
        out_specs=vmem(5),
        scratch_shapes=[pltpu.VMEM((4, 256, 256), BF16)] * 2,
        compiler_params=pltpu.CompilerParams(vmem_limit_bytes=16 * 1024 * 1024),
    )(avg, wt)

    out = pl.pallas_call(
        lambda *refs: return_kernel(rings, *refs),
        out_shape=shape((8, 64, 1024), BF16),
        in_specs=vmem(9),
        out_specs=pl.BlockSpec(memory_space=pltpu.VMEM),
        scratch_shapes=[
            pltpu.VMEM((4, 256, 256), BF16),
            pltpu.VMEM((4, 256, 256), BF16),
            pltpu.VMEM((2, 18, 18, 8, 128), F32),
            pltpu.VMEM((4, 128, 256), BF16),
            pltpu.VMEM((4, 128, 256), BF16),
            pltpu.VMEM((8, 4, 128, 128), BF16),
            pltpu.VMEM((8, 4, 128, 128), BF16),
            pltpu.VMEM((1024, 1024), BF16),
            DMA((4,)),
            DMA((4,)),
            DMA((4, 8)),
            DMA((4, 8)),
            DMA,
        ],
        compiler_params=pltpu.CompilerParams(
            collective_id=1, has_side_effects=True, vmem_limit_bytes=24 * 1024 * 1024
        ),
    )(anom, cen, yh, yl, zh, zl, last, coef, wt)
    return jnp.transpose(out.reshape(8, 64, 8, 128), (1, 2, 0, 3))


def solution(mesh):
    placed = (P("mem", None, "tile", None), P(None, "tile", None), P(), P(), P(("mem", "tile")))
    return jax.shard_map(
        local, mesh=mesh, in_specs=placed, out_specs=P("mem", None, "tile", None), check_vma=False
    )
```

```python
import jax
import jax.numpy as jnp
from jax import lax
from jax.experimental import pallas as pl
from jax.experimental.pallas import tpu as pltpu
from jax.sharding import PartitionSpec as P

F32 = jnp.float32
BF16 = jnp.bfloat16
MESH = pl.DeviceIdType.MESH
VMEM_LIMIT = 50 * 1024 * 1024
NS_ITERS = 14
PLAIN_NORM = 2500.0
CONVERGED = 1e-5
NT = (((1,), (1,)), ((), ()))
TN = (((0,), (0,)), ((), ()))


def place():
    tile = lax.axis_index("tile")
    mem = lax.axis_index("mem")
    ring = tile // 2
    half = lax.rem(tile, 2)
    return ring, half, mem, half * 4 + mem


def target(ring, slot):
    return {"mem": lax.rem(slot, 4), "tile": 2 * ring + slot // 4}


def remote(src, dst, send_sem, recv_sem, ring, slot):
    return pltpu.make_async_remote_copy(
        src_ref=src,
        dst_ref=dst,
        send_sem=send_sem,
        recv_sem=recv_sem,
        device_id=target(ring, slot),
        device_id_type=MESH,
    )


def signal(sem, ring, slot):
    pl.semaphore_signal(sem, inc=1, device_id=target(ring, slot), device_id_type=MESH)


def stencil(c, bx, ax, by, ay, s, sx, sy):
    return c - sx * (c - bx) - sy * (c - by) + s * (ax + bx + ay + by - 4.0 * c)


def rounded(x):
    return x.astype(BF16).astype(F32)


def loop(lower, upper, body):
    def step(i, carry):
        body(i)
        return carry

    lax.fori_loop(lower, upper, step, 0)


def forecast_kernel(
    rings,
    u_hbm,
    spread_hbm,
    obs_hbm,
    sx_ref,
    sy_ref,
    anom_ref,
    cen_ref,
    avg_ref,
    wt_ref,
    coef_ref,
    raw,
    spread_in,
    obs_in,
    flat,
    state,
    pick,
    wide,
    rcv,
    u0,
    u1,
    coef,
    spr,
    cst,
    cra,
    crb,
    gpk,
    gab,
    gbe,
    gle,
    gri,
    load_sem,
    block_send,
    block_recv,
    halo_send,
    halo_recv,
    spr_send,
    spr_recv,
    cnt_send,
    cnt_recv,
    sum_send,
    sum_recv,
    gram_send,
    gram_recv,
):
    ring, half, mem, slot = place()
    above = lax.rem(ring + rings - 1, rings)
    below = lax.rem(ring + 1, rings)

    barrier = pltpu.get_barrier_semaphore()
    loop(1, 8, lambda j: signal(barrier, ring, lax.rem(slot + j, 8)))
    loop(1, rings, lambda j: signal(barrier, lax.rem(ring + j, rings), slot))
    load_raw = pltpu.make_async_copy(u_hbm, raw, load_sem.at[0])
    load_spread = pltpu.make_async_copy(spread_hbm, spread_in, load_sem.at[1])
    load_obs = pltpu.make_async_copy(obs_hbm, obs_in, load_sem.at[2])
    load_raw.start()
    load_spread.start()
    load_obs.start()

    def pick_rows(i):
        row = lax.broadcasted_iota(jnp.int32, (128, 128), 0) + 128 * i
        lane = lax.broadcasted_iota(jnp.int32, (128, 128), 1)
        level = jnp.where(row // 8 == lane, lax.rem(row, 8), 8)
        rows = pl.ds(pl.multiple_of(128 * i, 128), 128)
        for f in range(8):
            pick[rows, f * 128 : f * 128 + 128] = jnp.where(level == f, 1.0, 0.0).astype(BF16)

    loop(0, 8, pick_rows)

    load_raw.wait()
    for f in range(8):
        flat[:, f * 128 : f * 128 + 128] = raw[:, f].astype(F32).reshape(512, 128).astype(BF16)

    def pair_of(t, side):
        return t + side * (3 - 2 * t)

    def place_of(t, side):
        return 1 + 4 * side + pair_of(t, side)

    def turn_pair(t):
        pair = pair_of(t, half)
        k = lax.broadcasted_iota(jnp.int32, (128, 512), 1)
        r = lax.broadcasted_iota(jnp.int32, (128, 512), 0) + 128 * pair
        turn = jnp.where(k == lax.rem(r, 64) * 8 + r // 64, 1.0, 0.0).astype(BF16)
        state[...] = jnp.dot(turn, flat[...], preferred_element_type=F32).astype(BF16)
        block = lax.dot_general(
            pick[...], state[...], NT, preferred_element_type=F32
        ).astype(BF16)
        wide[pair, 16:1040] = block
        wide[pair, 0:16] = block[1008:1024]
        wide[pair, 1040:1056] = block[0:16]

    parts = [(0, 0, 160), (1, 0, 160), (2, 0, 96), (3, 0, 96), (2, 96, 160), (3, 96, 160)]

    def block_copy(q, to):
        t, low, high = parts[q]
        return remote(
            wide.at[
                pair_of(t, half), pl.ds(pl.multiple_of(128 * to + low, 16), high - low)
            ],
            rcv.at[place_of(t, half), mem, low:high], block_send.at[q, to],
            block_recv.at[q, slot], ring, to,
        )

    def own_copy(q):
        t, low, high = parts[q]
        return pltpu.make_async_copy(
            wide.at[
                pair_of(t, half), pl.ds(pl.multiple_of(128 * slot + low, 16), high - low)
            ],
            rcv.at[place_of(t, half), mem, low:high], block_recv.at[q, slot],
        )

    def send_blocks(q):
        loop(1, 8, lambda j: block_copy(q, lax.rem(slot + j, 8)).start())
        own_copy(q).start()

    def wait_blocks(q):
        own_copy(q).wait()
        t, low, high = parts[q]

        def wait(j):
            frm = lax.rem(slot + j, 8)
            remote(
                wide.at[0, low:high], rcv.at[place_of(t, frm // 4), lax.rem(frm, 4), low:high],
                block_send.at[q, frm], block_recv.at[q, frm], ring, frm,
            ).wait_recv()

        loop(1, 8, wait)

    turn_pair(0)
    pl.semaphore_wait(barrier, 7 + rings - 1)
    send_blocks(0)

    load_spread.wait()
    mine = 8 + 8 * half
    for x in range(8):
        spr[mine + x] = spread_in[:, x, :]
    spr_here = remote(
        spr.at[pl.ds(mine, 8)], spr.at[pl.ds(mine, 8)], spr_send.at[0], spr_recv.at[0],
        ring, (1 - half) * 4 + mem,
    )
    spr_here.start()

    turn_pair(1)
    send_blocks(1)
    turn_pair(2)
    turn_pair(3)

    load_obs.wait()
    obs = obs_in[...]
    in_ring = lax.broadcasted_iota(jnp.int32, (rings, 256), 0) == obs // 32
    in_patch = lax.broadcasted_iota(jnp.int32, (128, 256), 0) == lax.rem(obs, 32)
    tally = lax.dot_general(
        in_ring.astype(F32).astype(BF16), in_patch.astype(F32).astype(BF16), NT,
        preferred_element_type=F32,
    )
    for r in range(rings):
        cst[r] = jnp.broadcast_to(tally[r : r + 1, :], (8, 128))
    cra[ring] = cst[ring]

    def count_copy(j):
        to = lax.rem(ring + j, rings)
        return remote(cst.at[to], cra.at[ring], cnt_send.at[j], cnt_recv.at[ring], to, slot)

    wait_blocks(0)
    halos = [
        remote(rcv.at[1], rcv.at[9], halo_send.at[0], halo_recv.at[0], above, slot),
        remote(rcv.at[8], rcv.at[0], halo_send.at[1], halo_recv.at[1], below, slot),
    ]
    for copy in halos:
        copy.start()
    send_blocks(2)
    loop(1, rings, lambda j: count_copy(j).start())

    spr_here.wait_send()
    other = 16 - 8 * half
    remote(
        spr.at[pl.ds(other, 8)], spr.at[pl.ds(other, 8)], spr_send.at[0], spr_recv.at[0],
        ring, (1 - half) * 4 + mem,
    ).wait_recv()
    spr_far = [
        remote(spr.at[8:10], spr.at[24:26], spr_send.at[1], spr_recv.at[1], above, slot),
        remote(spr.at[22:24], spr.at[6:8], spr_send.at[2], spr_recv.at[2], below, slot),
    ]
    for copy in spr_far:
        copy.start()

    def spread_row(i):
        lane = lax.broadcasted_iota(jnp.int32, (20, 8, 128), 2)
        column = lax.rem(
            lax.broadcasted_iota(jnp.int32, (20, 8, 128), 0) + 16 * slot + 126, 128
        )
        values = jnp.where(lane == column, spr[i + 6][None], 0.0)
        coef[i] = jnp.broadcast_to(jnp.sum(values, axis=2, keepdims=True), (20, 8, 128))

    loop(2, 18, spread_row)

    def coef_row(i):
        coef_ref[i] = coef[i + 2, 2:18]

    loop(0, 16, coef_row)
    sublane = lax.broadcasted_iota(jnp.int32, (8, 128), 0)
    for k, ref in enumerate((sx_ref, sy_ref)):
        speed = jnp.zeros((8, 128), F32)
        for f in range(8):
            speed = jnp.where(sublane == f, ref[f], speed)
        wt_ref[4 + k] = speed

    loop(1, 8, lambda j: block_copy(1, lax.rem(slot + j, 8)).wait_send())
    for q in (3, 4, 5):
        send_blocks(q)

    def unshuffle(pair, y0=0, y1=20):
        low = lax.broadcasted_iota(jnp.int32, (8 * (y1 - y0), 128), 1) < 64
        rows = slice(8 * y0, 8 * y1)
        for mh in range(2):
            r0 = rcv[pair, 2 * mh, rows].astype(F32)
            r1 = rcv[pair, 2 * mh + 1, rows].astype(F32)
            even = jnp.where(low, r0, pltpu.roll(r1, 64, 1))
            odd = jnp.where(low, pltpu.roll(r0, 64, 1), r1)
            u0[mh, 2 * pair, y0:y1] = even.reshape(y1 - y0, 8, 128)
            u0[mh, 2 * pair + 1, y0:y1] = odd.reshape(y1 - y0, 8, 128)

    unshuffle(1)
    unshuffle(8)
    sx = wt_ref[4][None]
    sy = wt_ref[5][None]

    def first(x, y0=0, y1=18):
        s = coef[x, y0 + 1 : y1 + 1]
        here, behind, ahead = slice(y0 + 1, y1 + 1), slice(y0, y1), slice(y0 + 2, y1 + 2)
        for mh in range(2):
            u1[mh, x - 1, y0:y1] = rounded(
                stencil(
                    u0[mh, x, here], u0[mh, x - 1, here], u0[mh, x + 1, here],
                    u0[mh, x, behind], u0[mh, x, ahead], s, sx, sy,
                )
            )

    def second(row, c):
        h, i = row // 8, lax.rem(row, 8)
        x, y = row + 1, 8 * c + 1
        s = coef[x + 1, y + 1 : y + 9]
        prior = [
            rounded(
                stencil(
                    u1[mh, x, y : y + 8], u1[mh, x - 1, y : y + 8], u1[mh, x + 1, y : y + 8],
                    u1[mh, x, y - 1 : y + 7], u1[mh, x, y + 1 : y + 9], s, sx, sy,
                )
            )
            for mh in range(2)
        ]
        centre = jnp.sum(prior[0] + prior[1], axis=2, keepdims=True) * (1.0 / 256.0)
        centre = jnp.broadcast_to(centre, (8, 8, 128))
        cen_ref[2 * h + c, i] = centre.reshape(64, 128)
        for mh in range(2):
            anom_ref[2 * h + c, i, :, mh * 128 : mh * 128 + 128] = (
                (prior[mh] - centre).reshape(64, 128).astype(BF16)
            )

    def firsts(low, high, y0=0, y1=18):
        def both(k):
            first(low + k, y0, y1)
            first(high + k, y0, y1)

        loop(0, 2, both)

    def seconds(low, high, c):
        def both(k):
            second(low + k, c)
            second(high + k, c)

        loop(0, 2, both)

    wait_blocks(1)
    unshuffle(2)
    unshuffle(7)
    firsts(3, 15)
    for copy in spr_far:
        copy.wait()
    for i in (0, 1, 18, 19):
        spread_row(i)
    for copy in halos:
        copy.wait()
    unshuffle(0)
    unshuffle(9)
    firsts(1, 17)
    for c in range(2):
        seconds(0, 14, c)

    row = lax.broadcasted_iota(jnp.int32, (128, 128), 0)
    col = lax.broadcasted_iota(jnp.int32, (128, 128), 1)
    left = lax.rem(slot + 7, 8)
    right = lax.rem(slot + 1, 8)
    copies = []

    def sum_copy(j):
        return remote(
            crb.at[slot], crb.at[slot], sum_send.at[j], sum_recv.at[slot], ring,
            lax.rem(slot + j, 8),
        )

    for c in range(2):
        if c:
            def count_wait(j):
                frm = lax.rem(ring + j, rings)
                remote(cst.at[0], cra.at[frm], cnt_send.at[j], cnt_recv.at[frm], frm, slot).wait_recv()

            loop(1, rings, count_wait)
            total = cra[0]
            for r in range(1, rings):
                total = total + cra[r]
            crb[slot] = total

            loop(1, 8, lambda j: sum_copy(j).start())
        (y0, y1), (z0, z1) = (((0, 12), (0, 10)), ((12, 20), (10, 18)))[c]
        wait_blocks(2 + 2 * c)
        unshuffle(3, y0, y1)
        unshuffle(6, y0, y1)
        firsts(5, 13, z0, z1)
        seconds(2, 12, c)
        wait_blocks(3 + 2 * c)
        unshuffle(4, y0, y1)
        unshuffle(5, y0, y1)
        loop(7, 13, lambda x, z0=z0, z1=z1: first(x, z0, z1))
        for h in range(2):
            p = 2 * h + c
            loop(4 + 4 * h, 8 + 4 * h, lambda row, c=c: second(row, c))
            a = anom_ref[p].reshape(512, 256)
            g = lax.dot_general(a, a, TN, preferred_element_type=F32) * (1.0 / 512.0)
            last = g[128:, 128:]
            gpk[p, 0:128] = g[:128, 128:]
            gpk[p, 128:256] = jnp.where(row >= col, g[:128, :128], last)
            diag = jnp.sum(jnp.where(row == col, last, 0.0), axis=0, keepdims=True)
            gpk[p, 256:264] = jnp.broadcast_to(diag, (8, 128))
            vertical = (gab, below) if h else (gbe, above)
            sideways = (gle, right) if c else (gri, left)
            pair = [
                remote(
                    gpk.at[p], vertical[0].at[c], gram_send.at[2 * p], gram_recv.at[2 * p],
                    vertical[1], slot,
                ),
                remote(
                    gpk.at[p], sideways[0].at[h], gram_send.at[2 * p + 1],
                    gram_recv.at[2 * p + 1], ring, sideways[1],
                ),
            ]
            for copy in pair:
                copy.start()
            copies += pair

    def sum_wait(j):
        frm = lax.rem(slot + j, 8)
        remote(crb.at[slot], crb.at[frm], sum_send.at[j], sum_recv.at[frm], ring, frm).wait_recv()

    loop(1, 8, sum_wait)
    counts = crb[0]
    for k in range(1, 8):
        counts = counts + crb[k]
    lane = lax.broadcasted_iota(jnp.int32, (8, 128), 1)
    for h in range(2):
        for c in range(2):
            chosen = jnp.where(lane == h * 16 + 2 * slot + c, counts, 0.0)
            count = jnp.sum(chosen, axis=1, keepdims=True)
            wt_ref[2 * h + c] = jnp.broadcast_to(count / (count + 16.0), (8, 128))
    loop(1, rings, lambda j: count_copy(j).wait_send())
    loop(1, 8, lambda j: sum_copy(j).wait_send())
    for q in (0, 2, 3, 4, 5):
        loop(1, 8, lambda j, q=q: block_copy(q, lax.rem(slot + j, 8)).wait_send())
    for copy in copies:
        copy.wait()
    for c in range(2):
        for h in range(2):
            p = 2 * h + c
            up = gpk[c] if h else gab[c]
            down = gbe[c] if h else gpk[2 + c]
            lft = gpk[2 * h] if c else gle[h]
            rgt = gri[h] if c else gpk[2 * h + 1]
            avg_ref[p] = (2.0 * gpk[p] + up + down + lft + rgt) * (1.0 / 6.0)


def split(x):
    hi = x.astype(BF16)
    return hi, (x - hi.astype(F32)).astype(BF16)


def product(a, b):
    (ah, al), (bh, bl) = a, b
    return (
        jnp.dot(ah, bh, preferred_element_type=F32)
        + jnp.dot(ah, bl, preferred_element_type=F32)
        + jnp.dot(al, bh, preferred_element_type=F32)
    )


def analysis_kernel(avg_ref, wt_ref, yh, yl, zh, zl, last_ref, fh, fl):
    row = lax.broadcasted_iota(jnp.int32, (256, 256), 0)
    col = lax.broadcasted_iota(jnp.int32, (256, 256), 1)
    diagonal = row == col
    identity = jnp.where(diagonal, 1.0, 0.0)
    low = row[:128, :128] >= col[:128, :128]
    on = row[:128, :128] == col[:128, :128]

    def coefs(low_end, plain):
        alpha2 = jnp.where(plain, 1.0, 3.0 / (1.0 + low_end + low_end * low_end))
        alpha = jnp.sqrt(alpha2)
        reach = alpha * low_end
        after = 0.5 * reach * (3.0 - reach * reach)
        return 1.5 * alpha, 0.5 * alpha * alpha2, jnp.minimum(after, 1.0)

    ends, plains, scales = [], [], []
    for p in range(4):
        packed = avg_ref[p]
        upper_right = packed[0:128]
        both = packed[128:256]
        turned = both.T
        first = jnp.where(low, both, turned)
        last = jnp.where(on, jnp.broadcast_to(packed[256:257], (128, 128)), jnp.where(low, turned, both))
        averaged = jnp.concatenate(
            [
                jnp.concatenate([first, upper_right], axis=1),
                jnp.concatenate([upper_right.T, last], axis=1),
            ],
            axis=0,
        )
        system = identity + wt_ref[p, 0:1, 0:1] * averaged
        squares = jnp.sum(jnp.sum(system * system, axis=1, keepdims=True), axis=0, keepdims=True)
        norm = jnp.sqrt(squares)
        rows = jnp.max(
            jnp.sum(jnp.abs(system), axis=0, keepdims=True), axis=1, keepdims=True
        )
        plain = norm > PLAIN_NORM
        scale = jnp.where(plain, norm, jnp.minimum(norm, rows * 1.000001))
        start = system / scale
        low_end = jnp.where(plain, 0.0, jnp.sqrt(1.0 / scale) * 0.9999)
        a, b, after = coefs(low_end, plain)
        factor = a * identity - b * start
        y = product(split(start), split(factor))
        yh[p], yl[p] = split(y)
        zh[p], zl[p] = split(factor)
        ends.append(after)
        plains.append(plain)
        scales.append(scale)

    def some_left(ends, plains, k):
        left = jnp.zeros((1, 1), F32)
        for end, plain in zip(ends, plains):
            _, _, after = coefs(end, plain)
            todo = jnp.where(plain, jnp.where(k + 1 < NS_ITERS, 1.0, 0.0), jnp.where(1.0 - after > CONVERGED, 1.0, 0.0))
            left = jnp.maximum(left, todo)
        return jnp.max(left) > 0.5

    def body(carry):
        k, _, *ends = carry
        following = []
        for p in range(4):
            a, b, after = coefs(ends[p], plains[p])
            t = product((zh[p], zl[p]), (yh[p], yl[p]))
            fh[p], fl[p] = split(a * identity - b * t)
            following.append(after)
        for p in range(4):
            factor = (fh[p], fl[p])
            ny = product((yh[p], yl[p]), factor)
            nz = product(factor, (zh[p], zl[p]))
            yh[p], yl[p] = split(ny)
            zh[p], zl[p] = split(nz)
        return (k + 1, some_left(following, plains, k + 1), *following)

    last_k, _, *ends = lax.while_loop(
        lambda carry: carry[1], body, (1, some_left(ends, plains, 1), *ends)
    )
    for p in range(4):
        a, b, after = coefs(ends[p], plains[p])
        middle = jnp.where(plains[p], 1.0, 0.5 + 0.5 * after)
        for k, value in enumerate((a, b, 1.0 / (middle * jnp.sqrt(scales[p])))):
            last_ref[3 * p + k] = jnp.broadcast_to(value, (8, 128))


def return_kernel(
    rings,
    anom_ref,
    cen_ref,
    yh,
    yl,
    zh,
    zl,
    last_ref,
    coef_ref,
    wt_ref,
    out_ref,
    fh,
    fl,
    g,
    edge_out,
    edge_in,
    snd,
    rcv,
    pick,
    edge_send,
    edge_recv,
    main_send,
    main_recv,
    own_sem,
):
    ring, half, mem, slot = place()
    above = lax.rem(ring + rings - 1, rings)
    below = lax.rem(ring + 1, rings)
    left = lax.rem(slot + 7, 8)
    right = lax.rem(slot + 1, 8)
    barrier = pltpu.get_barrier_semaphore()
    loop(1, 8, lambda j: signal(barrier, ring, lax.rem(slot + j, 8)))
    signal(barrier, above, slot)
    signal(barrier, below, slot)

    diagonal = lax.broadcasted_iota(jnp.int32, (256, 256), 0) == lax.broadcasted_iota(
        jnp.int32, (256, 256), 1
    )
    for p in range(4):
        t = product((zh[p], zl[p]), (yh[p], yl[p]))
        a, b = last_ref[3 * p, 0:1, 0:1], last_ref[3 * p + 1, 0:1, 0:1]
        fh[p], fl[p] = split(jnp.where(diagonal, a, 0.0) - b * t)
    for p in range(4):
        inverse = product((fh[p], fl[p]), (zh[p], zl[p]))
        weights = (inverse * last_ref[3 * p + 2, 0:1, 0:1]).astype(BF16)
        update = jnp.dot(anom_ref[p].reshape(512, 256), weights, preferred_element_type=F32)
        centre = cen_ref[p].reshape(512, 128)
        h, c = p // 2, p % 2
        for mh in range(2):
            value = rounded(centre + update[:, mh * 128 : mh * 128 + 128])
            g[mh, 8 * h + 1 : 8 * h + 9, 8 * c + 1 : 8 * c + 9] = value.reshape(8, 8, 8, 128)
    for mh in range(2):
        lanes = slice(mh * 128, mh * 128 + 128)
        edge_out[0, :, lanes] = g[mh, 1, 1:17].reshape(128, 128).astype(BF16)
        edge_out[1, :, lanes] = g[mh, 16, 1:17].reshape(128, 128).astype(BF16)
        edge_out[2, :, lanes] = g[mh, 1:17, 1].reshape(128, 128).astype(BF16)
        edge_out[3, :, lanes] = g[mh, 1:17, 16].reshape(128, 128).astype(BF16)
    pl.semaphore_wait(barrier, 9)
    edges = [
        remote(edge_out.at[k], edge_in.at[k], edge_send.at[k], edge_recv.at[k], to_ring, to_slot)
        for k, (to_ring, to_slot) in enumerate(
            [(above, slot), (below, slot), (ring, left), (ring, right)]
        )
    ]
    for copy in edges:
        copy.start()
    sx = wt_ref[4][None]
    sy = wt_ref[5][None]

    def step_pair(h, pair, y0, y1):
        x = 8 * h + 2 * pair + 1
        rows = slice(8 * y0, 8 * y1)
        low = lax.broadcasted_iota(jnp.int32, (8 * (y1 - y0), 128), 1) < 64
        here, behind, ahead = slice(y0 + 1, y1 + 1), slice(y0, y1), slice(y0 + 2, y1 + 2)
        for mh in range(2):
            even, odd = [
                stencil(
                    g[mh, x + k, here], g[mh, x + k - 1, here], g[mh, x + k + 1, here],
                    g[mh, x + k, behind], g[mh, x + k, ahead], coef_ref[x + k - 1, y0:y1], sx, sy,
                ).reshape(8 * (y1 - y0), 128)
                for k in range(2)
            ]
            to = 4 * h + 2 * mh
            snd[to, pair, rows] = jnp.where(low, even, pltpu.roll(odd, 64, 1)).astype(BF16)
            snd[to + 1, pair, rows] = jnp.where(low, pltpu.roll(even, 64, 1), odd).astype(BF16)

    def parts(half_of):
        inner = pl.ds(1 - half_of, 3)
        return [
            (inner, slice(16, 112)), (inner, slice(0, 16)), (inner, slice(112, 128)),
            (3 * half_of, slice(0, 128)),
        ]

    def main_copy(part, to):
        pairs, rows = parts(to // 4)[part]
        return remote(
            snd.at[to, pairs, rows], rcv.at[slot, pairs, rows], main_send.at[part, to],
            main_recv.at[part, slot], ring, to,
        )

    def send(part):
        loop(1, 8, lambda j: main_copy(part, lax.rem(slot + j, 8)).start())

    for h in range(2):
        loop(1 - h, 4 - h, lambda pair, h=h: step_pair(h, pair, 2, 14))
        skip = half if h else 1 - half
        loop(skip, 4, lambda j, h=h: main_copy(0, 4 * h + lax.rem(mem + j, 4)).start())
    for copy in edges:
        copy.wait()
    for mh in range(2):
        lanes = slice(mh * 128, mh * 128 + 128)
        g[mh, 17, 1:17] = edge_in[0, :, lanes].astype(F32).reshape(16, 8, 128)
        g[mh, 0, 1:17] = edge_in[1, :, lanes].astype(F32).reshape(16, 8, 128)
        g[mh, 1:17, 17] = edge_in[2, :, lanes].astype(F32).reshape(16, 8, 128)
        g[mh, 1:17, 0] = edge_in[3, :, lanes].astype(F32).reshape(16, 8, 128)
    for part, y0 in ((1, 0), (2, 14)):
        for h in range(2):
            loop(1 - h, 4 - h, lambda pair, h=h, y0=y0: step_pair(h, pair, y0, y0 + 2))
        send(part)
    for h in range(2):
        step_pair(h, 3 * h, 0, 16)
    send(3)
    own = pltpu.make_async_copy(snd.at[slot], rcv.at[slot], own_sem)
    own.start()

    def pick_rows(i):
        row = lax.broadcasted_iota(jnp.int32, (128, 128), 0) + 128 * i
        lane = lax.broadcasted_iota(jnp.int32, (128, 128), 1)
        level = jnp.where(row // 8 == lane, lax.rem(row, 8), 8)
        rows = pl.ds(pl.multiple_of(128 * i, 128), 128)
        for f in range(8):
            pick[rows, f * 128 : f * 128 + 128] = jnp.where(level == f, 1.0, 0.0).astype(BF16)

    loop(0, 8, pick_rows)
    own.wait()

    def wait_part(part):
        def wait(j):
            frm = lax.rem(slot + j, 8)
            pairs, rows = parts(half)[part]
            remote(
                snd.at[frm, pairs, rows], rcv.at[frm, pairs, rows], main_send.at[part, frm],
                main_recv.at[part, frm], ring, frm,
            ).wait_recv()

        loop(1, 8, wait)

    def result_pair(pair):
        block = rcv[:, pair].reshape(1024, 128)
        result = lax.dot_general(block, pick[...], TN, preferred_element_type=F32).astype(BF16)
        out_ref[2 * pair] = result[:64]
        out_ref[2 * pair + 1] = result[64:]

    for part in range(3):
        wait_part(part)
    loop(1 - half, 4 - half, result_pair)
    wait_part(3)
    result_pair(3 * half)
    for part in range(4):
        loop(1, 8, lambda j, part=part: main_copy(part, lax.rem(slot + j, 8)).wait_send())


def vmem(count):
    return [pl.BlockSpec(memory_space=pltpu.VMEM)] * count


def local(member_collection, spreading_ratio, transport_ratio_row, transport_ratio_column, obs_patch):
    rings = lax.axis_size("tile") // 2
    DMA = pltpu.SemaphoreType.DMA
    obs = obs_patch.reshape(1, 256)

    def shape(dims, dtype=F32):
        return jax.ShapeDtypeStruct(dims, dtype)

    anom, cen, avg, wt, coef = pl.pallas_call(
        lambda *refs: forecast_kernel(rings, *refs),
        out_shape=[
            shape((4, 8, 64, 256), BF16),
            shape((4, 8, 64, 128)),
            shape((4, 264, 128)),
            shape((6, 8, 128)),
            shape((16, 16, 8, 128)),
        ],
        in_specs=[pl.BlockSpec(memory_space=pltpu.HBM)] * 3
        + [pl.BlockSpec(memory_space=pltpu.SMEM)] * 2,
        out_specs=vmem(5),
        scratch_shapes=[
            pltpu.VMEM((64, 8, 8, 128), BF16),
            pltpu.VMEM((8, 8, 128), F32),
            pltpu.VMEM((1, 256), jnp.int32),
            pltpu.VMEM((512, 1024), BF16),
            pltpu.VMEM((128, 1024), BF16),
            pltpu.VMEM((1024, 1024), BF16),
            pltpu.VMEM((4, 1056, 128), BF16),
            pltpu.VMEM((10, 4, 160, 128), BF16),
            pltpu.VMEM((2, 20, 20, 8, 128), F32),
            pltpu.VMEM((2, 18, 18, 8, 128), F32),
            pltpu.VMEM((20, 20, 8, 128), F32),
            pltpu.VMEM((32, 8, 128), F32),
            pltpu.VMEM((rings, 8, 128), F32),
            pltpu.VMEM((rings, 8, 128), F32),
            pltpu.VMEM((8, 8, 128), F32),
            pltpu.VMEM((4, 264, 128), F32),
            pltpu.VMEM((2, 264, 128), F32),
            pltpu.VMEM((2, 264, 128), F32),
            pltpu.VMEM((2, 264, 128), F32),
            pltpu.VMEM((2, 264, 128), F32),
            DMA((3,)),
            DMA((6, 8)),
            DMA((6, 8)),
            DMA((2,)),
            DMA((2,)),
            DMA((3,)),
            DMA((3,)),
            DMA((rings,)),
            DMA((rings,)),
            DMA((8,)),
            DMA((8,)),
            DMA((8,)),
            DMA((8,)),
        ],
        compiler_params=pltpu.CompilerParams(
            collective_id=0, has_side_effects=True, vmem_limit_bytes=VMEM_LIMIT
        ),
    )(member_collection, spreading_ratio, obs, transport_ratio_row, transport_ratio_column)

    square = shape((4, 256, 256), BF16)
    yh, yl, zh, zl, last = pl.pallas_call(
        analysis_kernel,
        out_shape=[square, square, square, square, shape((12, 8, 128))],
        in_specs=vmem(2),
        out_specs=vmem(5),
        scratch_shapes=[pltpu.VMEM((4, 256, 256), BF16)] * 2,
        compiler_params=pltpu.CompilerParams(vmem_limit_bytes=16 * 1024 * 1024),
    )(avg, wt)

    out = pl.pallas_call(
        lambda *refs: return_kernel(rings, *refs),
        out_shape=shape((8, 64, 1024), BF16),
        in_specs=vmem(9),
        out_specs=pl.BlockSpec(memory_space=pltpu.VMEM),
        scratch_shapes=[
            pltpu.VMEM((4, 256, 256), BF16),
            pltpu.VMEM((4, 256, 256), BF16),
            pltpu.VMEM((2, 18, 18, 8, 128), F32),
            pltpu.VMEM((4, 128, 256), BF16),
            pltpu.VMEM((4, 128, 256), BF16),
            pltpu.VMEM((8, 4, 128, 128), BF16),
            pltpu.VMEM((8, 4, 128, 128), BF16),
            pltpu.VMEM((1024, 1024), BF16),
            DMA((4,)),
            DMA((4,)),
            DMA((4, 8)),
            DMA((4, 8)),
            DMA,
        ],
        compiler_params=pltpu.CompilerParams(
            collective_id=1, has_side_effects=True, vmem_limit_bytes=24 * 1024 * 1024
        ),
    )(anom, cen, yh, yl, zh, zl, last, coef, wt)
    return jnp.transpose(out.reshape(8, 64, 8, 128), (1, 2, 0, 3))


def solution(mesh):
    placed = (P("mem", None, "tile", None), P(None, "tile", None), P(), P(), P(("mem", "tile")))
    return jax.shard_map(
        local, mesh=mesh, in_specs=placed, out_specs=P("mem", None, "tile", None), check_vma=False
    )
```
